32 devices in a mesh: dir: 2 (over core), batch: 8 (over z, y), unit: 2 (over x).
Axes of the slice: x: 2, y: 2, z: 4, core: 2. Of those that a mesh axis runs over, the one named last changes fastest.
Arguments:
- inputs: bfloat16 [256, 16, 512], P('batch'), may hold values from -6 to 6
- win_count: int32 [256], P('batch'), may hold values from 1 to 2, as said below
- last_live: int32 [256], P('batch'), may hold values from 1 to 8, as said below
- hidden_init: float32 [2, 256, 512], P('dir', 'batch'), may hold values from -3 to 3
- cell_init: float32 [2, 256, 4096], P('dir', 'batch', 'unit'), may hold values from -3 to 3
- w_input: bfloat16 [2, 512, 4, 4096], P('dir', None, None, 'unit'), may hold values from -0.25 to 0.25
- w_hidden: bfloat16 [2, 512, 4, 4096], P('dir', None, None, 'unit'), may hold values from -0.25 to 0.25
- gate_bias: float32 [2, 4, 4096], P('dir', None, 'unit'), may hold values from -3 to 3
- w_proj: bfloat16 [2, 4096, 512], P('dir', 'unit'), may hold values from -0.375 to 0.375
- out_grad: bfloat16 [2, 256, 16, 512], P('dir', 'batch'), may hold values from -6 to 6
Outputs:
- layer_out: bfloat16 [2, 256, 16, 512], P('dir', 'batch')
- input_grad: float32 [256, 16, 512], P('batch')
- w_input_grad: float32 [2, 512, 4, 4096], P('dir', None, None, 'unit')
- w_hidden_grad: float32 [2, 512, 4, 4096], P('dir', None, None, 'unit')
- bias_grad: float32 [2, 4, 4096], P('dir', None, 'unit')
- w_proj_grad: float32 [2, 4096, 512], P('dir', 'unit')
- hidden_final: float32 [2, 256, 512], P('dir', 'batch')
- cell_final: float32 [2, 256, 4096], P('dir', 'batch', 'unit')
The draws below stay inside these ranges and needn't reach their ends.
Inputs may be any that keep to these rules, and one draw needn't show every extreme that they name: `win_count`: stream 0 has 2 live windows and stream 1 has one. `last_live`: stream 0's last live window is full and stream 1's has one live step.
All inputs are finite; a program needn't handle non-finite values.
Results may differ from the reference program's by a relative error of at most 0.035.
Values may be sent and summed in bfloat16 or wider, within the bound.
A program may use at most 384 MiB of HBM per device.

```python
import jax
import jax.numpy as jnp
from jax import lax

D = 512
CELL = 4096
WIN = 8
WINS = 2
STEPS = 16
STREAMS = 256


def draw_win_count(key, part):
    values = jax.random.randint(key, (STREAMS,), 1, WINS + 1, dtype=jnp.int32)
    places = jnp.arange(STREAMS, dtype=jnp.int32)
    values = jnp.where(places == 0, WINS, values)
    return jnp.where(places == 1, 1, values).astype(jnp.int32)


def draw_last_live(key, part):
    values = jax.random.randint(key, (STREAMS,), 1, WIN + 1, dtype=jnp.int32)
    places = jnp.arange(STREAMS, dtype=jnp.int32)
    values = jnp.where(places == 0, WIN, values)
    return jnp.where(places == 1, 1, values).astype(jnp.int32)


def block_scale(own_key, extent, pieces, low, high):
    gain, own = 1.0, jax.random.fold_in(own_key, 6)
    for position, blocks in pieces:
        draws = jnp.exp(jax.random.uniform(jax.random.fold_in(own, position), (blocks,), jnp.float32, low / len(pieces), high / len(pieces)))
        gain = gain * jnp.repeat(draws, extent[position] // blocks).reshape([-1 if axis == position else 1 for axis in range(len(extent))])
    return gain


def noise(rng, shape, width, most, split=(), kind=jnp.bfloat16):
    values = width * jax.random.normal(rng, shape, jnp.float32)
    if split:
        values = values * block_scale(rng, shape, split, -0.22, 0.18)
    return jnp.clip(values, -most, most).astype(kind)


def setup_inputs(seed: int = 0) -> dict:
    splits = jax.random.split(jax.random.key(seed), 11)
    inputs = noise(splits[0], (STREAMS, STEPS, D), 1.0, 6.0, ((0, 8),))
    win_count = draw_win_count(jax.random.fold_in(splits[10], 71), 0)
    last_live = draw_last_live(jax.random.fold_in(splits[10], 71), 0)
    hidden_init = noise(splits[3], (2, STREAMS, D), 1.0, 3.0, ((0, 2), (1, 8)), jnp.float32)
    cell_init = noise(splits[4], (2, STREAMS, CELL), 1.0, 3.0, ((0, 2), (1, 8), (2, 2)), jnp.float32)
    w_input = noise(splits[5], (2, D, 4, CELL), D ** -0.5, 0.25, ((0, 2), (3, 2)))
    w_hidden = noise(splits[6], (2, D, 4, CELL), D ** -0.5, 0.25, ((0, 2), (3, 2)))
    gate_bias = noise(splits[7], (2, 4, CELL), 0.5, 3.0, ((0, 2), (2, 2)), jnp.float32)
    w_proj = noise(splits[8], (2, CELL, D), (CELL // 16) ** -0.5, 0.375, ((0, 2), (1, 2)))
    out_grad = noise(splits[9], (2, STREAMS, STEPS, D), 1.0, 6.0, ((0, 2), (1, 8)))
    return dict(inputs=inputs, win_count=win_count, last_live=last_live, hidden_init=hidden_init, cell_init=cell_init, w_input=w_input, w_hidden=w_hidden, gate_bias=gate_bias, w_proj=w_proj, out_grad=out_grad)


@jax.custom_vjp
def low(v):
    return lax.optimization_barrier(v.astype(jnp.bfloat16)).astype(jnp.float32)

@jax.custom_vjp
def low_back(v):
    return v

def low_keep(v):
    return (low(v), None)

def low_pass(kept, grad):
    return (grad,)

def back_keep(v):
    return (v, None)

def back_low(kept, grad):
    return (low(grad),)
low.defvjp(low_keep, low_pass)
low_back.defvjp(back_keep, back_low)
HIGHEST_PRECISION = lax.Precision.HIGHEST

def direction_pass(inputs_f32, live_mask, hidden_start, cell_start, weight_in, weight_hidden, bias_one, weight_proj):
    inputs_time = jnp.swapaxes(inputs_f32, 0, 1)
    mask_time = jnp.swapaxes(live_mask, 0, 1)[:, :, None]

    @jax.checkpoint
    def advance(state_in, step_data):
        hidden_low, cell_prev = state_in
        input_now, mask_now = step_data
        gates_pre = jnp.einsum('sd,dgc->sgc', input_now, weight_in, precision=HIGHEST_PRECISION)
        gates_pre = gates_pre + jnp.einsum('sd,dgc->sgc', hidden_low, weight_hidden, precision=HIGHEST_PRECISION)
        gates_pre = low_back(gates_pre + bias_one)
        in_gate = jax.nn.sigmoid(gates_pre[:, 0])
        forget_gate = jax.nn.sigmoid(gates_pre[:, 1])
        cand_gate = jnp.tanh(gates_pre[:, 2])
        out_gate = jax.nn.sigmoid(gates_pre[:, 3])
        cell_sum = forget_gate * cell_prev + in_gate * cand_gate
        cell_new = 3.0 * jnp.tanh(cell_sum / 3.0)
        cell_out = low(low_back(out_gate * jnp.tanh(cell_new)))
        proj_pre = low_back(jnp.dot(cell_out, weight_proj, precision=HIGHEST_PRECISION))
        hidden_new = low(3.0 * jnp.tanh(proj_pre / 3.0))
        hidden_next = mask_now * hidden_new + (1.0 - mask_now) * hidden_low
        cell_next = mask_now * cell_new + (1.0 - mask_now) * cell_prev
        return ((hidden_next, cell_next), input_now + mask_now * hidden_new)
    (hidden_last, cell_last), output_time = lax.scan(advance, (low(hidden_start), cell_start), (inputs_time, mask_time))
    return (jnp.swapaxes(output_time, 0, 1), hidden_last, cell_last)

def reference(inputs, win_count, last_live, hidden_init, cell_init, w_input, w_hidden, gate_bias, w_proj, out_grad):
    seq_length = (win_count - 1) * WIN + last_live
    live_mask = (jnp.arange(STEPS, dtype=jnp.int32)[None, :] < seq_length[:, None]).astype(jnp.float32)

    def forward(inputs_f32, w_in_all, w_hid_all, bias_all, w_proj_all):
        outputs = []
        hidden_ends = []
        cell_ends = []
        for side in range(2):
            if side == 0:
                seq_in = inputs_f32
                seq_mask = live_mask
            else:
                seq_in = inputs_f32[:, ::-1]
                seq_mask = live_mask[:, ::-1]
            result, hidden_last, cell_last = direction_pass(seq_in, seq_mask, hidden_init[side], cell_init[side], w_in_all[side], w_hid_all[side], bias_all[side], w_proj_all[side])
            if side == 1:
                result = result[:, ::-1]
            outputs.append(result)
            hidden_ends.append(hidden_last)
            cell_ends.append(cell_last)
        return (jnp.stack(outputs), (jnp.stack(hidden_ends), jnp.stack(cell_ends)))
    layer, pullback, finals = jax.vjp(forward, inputs.astype(jnp.float32), w_input.astype(jnp.float32), w_hidden.astype(jnp.float32), gate_bias, w_proj.astype(jnp.float32), has_aux=True)
    input_grad, w_input_grad, w_hidden_grad, bias_grad, w_proj_grad = pullback(out_grad.astype(jnp.float32))
    return (layer.astype(jnp.bfloat16), input_grad, w_input_grad, w_hidden_grad, bias_grad, w_proj_grad, finals[0], finals[1])
```

```python
import functools

import jax
import jax.numpy as jnp
from jax import lax
from jax.experimental import pallas as pl
from jax.experimental.pallas import tpu as pltpu
from jax.sharding import PartitionSpec as P

WIN = 8
BLK = 256
RING = 4
MESH = pl.DeviceIdType.MESH
BF = jnp.bfloat16
F32 = jnp.float32
NT = (((1,), (1,)), ((), ()))
VMEM_LIMIT = 60 * 1024 * 1024
THIRD = 1.0 / 3.0


def sigmoid(v):
    return 0.5 * jnp.tanh(0.5 * v) + 0.5


def mm(a, b):
    return jnp.dot(a, b, preferred_element_type=F32)


def mm_nt(a, b):
    return lax.dot_general(a, b, NT, preferred_element_type=F32)


def identity():
    rows = lax.broadcasted_iota(jnp.int32, (BLK, BLK), 0)
    cols = lax.broadcasted_iota(jnp.int32, (BLK, BLK), 1)
    return jnp.where(rows == cols, 1.0, 0.0).astype(BF)


def gate_order():
    rows = lax.broadcasted_iota(jnp.int32, (BLK, BLK), 0)
    cols = lax.broadcasted_iota(jnp.int32, (BLK, BLK), 1)
    want = (rows & (BLK // 4 - 1)) * 4 + (rows >> 6)
    return jnp.where(want == cols, 1.0, 0.0).astype(BF)


def recurrence_kernel(
    x_ref,
    y_ref,
    len_ref,
    h0_ref,
    c0_ref,
    bias_ref,
    wx_hbm,
    wh_hbm,
    wp_hbm,
    lay_ref,
    hfin_ref,
    cfin_ref,
    dx_ref,
    dzg,
    xhg,
    mg,
    drg,
    wx,
    wh,
    wht,
    wp,
    wpt,
    raw,
    z,
    c,
    th,
    h,
    m,
    dr,
    dz,
    dc,
    dh,
    snd,
    rcv,
    load_sem,
    ex_send,
    ex_recv,
    y_send,
    y_recv,
    own_sem,
    x_sem,
):
    steps, streams, width = x_ref.shape
    units = wp.shape[0]
    tiles = units // BLK
    gate4 = 4 * BLK
    half_cols = 2 * units
    half_units = units // 2
    flip = lax.axis_index("dir")
    batch = lax.axis_index("batch")
    unit = lax.axis_index("unit")
    mine = lax.rem(batch, 2)
    other = 1 - mine
    y_dev = {"batch": batch + 1 - 2 * mine}
    x_dev = {"unit": 1 - unit}

    def place(t):
        return t + flip * (steps - 1 - 2 * t)

    barrier = pltpu.get_barrier_semaphore()
    pl.semaphore_signal(barrier, 1, device_id=x_dev, device_id_type=MESH)
    pl.semaphore_signal(barrier, 1, device_id=y_dev, device_id_type=MESH)

    blocks = width * 4 // BLK
    proj_copy = pltpu.make_async_copy(wp_hbm, wp, load_sem.at[2])
    proj_copy.start()

    def load(w_hbm, b, slot):
        return pltpu.make_async_copy(
            w_hbm.reshape(width * 4, units).at[pl.ds(pl.multiple_of(b * BLK, BLK), BLK)],
            raw.at[slot],
            load_sem.at[slot],
        )

    order = gate_order()

    def spread(w_hbm, w):
        def body(b, carry):
            slot = lax.rem(b, 2)

            @pl.when(b + 1 < blocks)
            def _():
                load(w_hbm, b + 1, 1 - slot).start()

            load(w_hbm, b, slot).wait()
            for j in range(tiles):
                got = mm(order, raw[slot, :, j * BLK : (j + 1) * BLK]).astype(BF)
                for g in range(4):
                    col = j * gate4 + g * BLK
                    w[pl.ds(pl.multiple_of(b * 64, 64), 64), col : col + BLK] = got[
                        g * 64 : (g + 1) * 64
                    ]
            return carry

        load(w_hbm, 0, 0).start()
        lax.fori_loop(0, blocks, body, 0)

    spread(wx_hbm, wx)
    spread(wh_hbm, wh)

    pl.semaphore_wait(barrier, 2)
    x_remote = pltpu.make_async_remote_copy(
        x_ref,
        xhg.at[mine, :, :, pl.ds(0, width)],
        x_sem.at[0],
        x_sem.at[1],
        device_id=y_dev,
        device_id_type=MESH,
    )
    x_local = pltpu.make_async_copy(x_ref, xhg.at[mine, :, :, pl.ds(0, width)], x_sem.at[2])
    x_remote.start()
    x_local.start()

    def exchange(k):
        slot = lax.rem(k, 2)
        return pltpu.make_async_remote_copy(
            snd.at[slot],
            rcv.at[slot],
            ex_send.at[slot],
            ex_recv.at[slot],
            device_id=x_dev,
            device_id_type=MESH,
        )

    def pair(kind, t, away, keep, target):
        return (
            pltpu.make_async_remote_copy(
                away,
                target,
                y_send.at[kind, t],
                y_recv.at[kind, t],
                device_id=y_dev,
                device_id_type=MESH,
            ),
            pltpu.make_async_copy(keep, target, own_sem.at[kind, t]),
        )

    def h_pair(t):
        return pair(0, t, h.at[t], h.at[t], xhg.at[mine, place(t), :, pl.ds(width, width)])

    def m_pair(t):
        slot = lax.rem(t, RING)
        away = m.at[slot, :, pl.ds(pl.multiple_of(other * half_units, half_units), half_units)]
        keep = m.at[slot, :, pl.ds(pl.multiple_of(mine * half_units, half_units), half_units)]
        return pair(1, t, away, keep, mg.at[mine, place(t)])

    def dr_pair(t):
        return pair(2, t, dr.at[t], dr.at[t], drg.at[mine, place(t)])

    def dz_pair(t):
        slot = lax.rem(t, RING)
        away = dz.at[slot, :, pl.ds(pl.multiple_of(other * half_cols, half_cols), half_cols)]
        keep = dz.at[slot, :, pl.ds(pl.multiple_of(mine * half_cols, half_cols), half_cols)]
        return pair(3, t, away, keep, dzg.at[mine, place(t)])

    def begin(copies):
        for one in copies:
            one.start()

    def sent(copies):
        copies[0].wait_send()
        copies[1].wait()

    def live_of(t, cols):
        live = jnp.where(len_ref[...] > place(t), 1.0, 0.0)
        return jnp.concatenate([live] * (cols // 128), 1)

    def input_part(t):
        now = x_ref[place(t)]
        for j in range(tiles):
            part = mm(now, wx[:, j * gate4 : (j + 1) * gate4])
            for g in range(4):
                z[t, :, j * gate4 + g * BLK : j * gate4 + (g + 1) * BLK] = (
                    part[:, g * BLK : (g + 1) * BLK] + bias_ref[g : g + 1, j * BLK : (j + 1) * BLK]
                )

    eye = identity()
    h[0] = h0_ref[...].astype(BF)
    c[0] = c0_ref[...]
    input_part(0)
    proj_copy.wait()
    turn_cols = 4 * units // steps
    turn_units = units // steps

    def forward(t, carry):
        slot = lax.rem(t, RING)

        @pl.when(t >= RING)
        def _():
            sent(m_pair(t - RING))

        live = live_of(t, BLK) > 0.5
        hidden = h[t]
        for j in range(tiles):
            cols = slice(j * BLK, (j + 1) * BLK)
            base = j * gate4
            pre = z[t, :, base : base + gate4] + mm(hidden, wh[:, base : base + gate4])
            in_gate = sigmoid(pre[:, :BLK])
            forget = sigmoid(pre[:, BLK : 2 * BLK])
            cand = jnp.tanh(pre[:, 2 * BLK : 3 * BLK])
            out_gate = sigmoid(pre[:, 3 * BLK :])
            prev = c[t, :, cols]
            new = 3.0 * jnp.tanh((forget * prev + in_gate * cand) * THIRD)
            m[slot, :, cols] = (out_gate * jnp.tanh(new)).astype(BF)
            z[t, :, base : base + BLK] = in_gate
            z[t, :, base + BLK : base + 2 * BLK] = forget
            z[t, :, base + 2 * BLK : base + 3 * BLK] = cand
            z[t, :, base + 3 * BLK : base + gate4] = out_gate
            c[t + 1, :, cols] = jnp.where(live, new, prev)
        two = lax.rem(t, 2)
        snd[two] = mm(m[slot], wp[...]).astype(BF)
        copy = exchange(t)
        copy.start()
        begin(h_pair(t))
        begin(m_pair(t))

        @pl.when(t + 1 < steps)
        def _():
            input_part(t + 1)

        at = pl.multiple_of(t * turn_cols, turn_cols)
        for kb in range(width // BLK):
            for cb in range(turn_cols // BLK):
                wht[pl.ds(at + cb * BLK, BLK), kb * BLK : (kb + 1) * BLK] = mm_nt(
                    eye, wh[kb * BLK : (kb + 1) * BLK, pl.ds(at + cb * BLK, BLK)]
                ).astype(BF)
        at = pl.multiple_of(t * turn_units, turn_units)
        for kb in range(width // BLK):
            wpt[kb * BLK : (kb + 1) * BLK, pl.ds(at, turn_units)] = mm_nt(
                eye, wp[pl.ds(at, turn_units), kb * BLK : (kb + 1) * BLK]
            ).astype(BF)
        copy.wait()
        total = snd[two].astype(F32) + rcv[two].astype(F32)
        squash = jnp.tanh(total * THIRD)
        th[t] = squash
        new_hidden = (3.0 * squash).astype(BF)
        live_h = live_of(t, width)
        lay_ref[place(t)] = (
            x_ref[place(t)].astype(F32) + live_h * new_hidden.astype(F32)
        ).astype(BF)
        h[t + 1] = jnp.where(live_h > 0.5, new_hidden.astype(F32), hidden.astype(F32)).astype(BF)
        return carry

    lax.fori_loop(0, steps, forward, 0)
    hfin_ref[...] = h[steps].astype(F32)
    cfin_ref[...] = c[steps]

    dc[...] = jnp.zeros_like(dc)
    dh[...] = jnp.zeros_like(dh)

    def backward(k, carry):
        t = steps - 1 - k
        slot = lax.rem(t, RING)

        @pl.when(k >= RING)
        def _():
            sent(dz_pair(t + RING))

        grad_hidden = dh[...]
        live_h = live_of(t, width)
        squash = th[t]
        y_now = y_ref[place(t)].astype(F32)
        low = (live_h * (y_now + grad_hidden) * (1.0 - squash * squash)).astype(BF)
        dr[t] = low
        live = live_of(t, BLK)
        part = jnp.zeros((streams, width), F32)
        for j in range(tiles):
            cols = slice(j * BLK, (j + 1) * BLK)
            base = j * gate4
            grad_m = mm(low, wpt[:, cols]).astype(BF).astype(F32)
            in_gate = z[t, :, base : base + BLK]
            forget = z[t, :, base + BLK : base + 2 * BLK]
            cand = z[t, :, base + 2 * BLK : base + 3 * BLK]
            out_gate = z[t, :, base + 3 * BLK : base + gate4]
            prev = c[t, :, cols]
            new = c[t + 1, :, cols]
            grad_c = dc[:, cols]
            tanh_new = jnp.tanh(new)
            grad_n = live * grad_c + grad_m * out_gate * (1.0 - tanh_new * tanh_new)
            third = new * THIRD
            grad_u = grad_n * (1.0 - third * third)
            dz[slot, :, base : base + BLK] = (grad_u * cand * in_gate * (1.0 - in_gate)).astype(BF)
            dz[slot, :, base + BLK : base + 2 * BLK] = (
                grad_u * prev * forget * (1.0 - forget)
            ).astype(BF)
            dz[slot, :, base + 2 * BLK : base + 3 * BLK] = (
                grad_u * in_gate * (1.0 - cand * cand)
            ).astype(BF)
            dz[slot, :, base + 3 * BLK : base + gate4] = (
                grad_m * tanh_new * out_gate * (1.0 - out_gate)
            ).astype(BF)
            dc[:, cols] = (1.0 - live) * grad_c + grad_u * forget
            part = part + mm(dz[slot, :, base : base + gate4], wht[base : base + gate4, :])
        two = lax.rem(k, 2)
        snd[two] = part.astype(BF)
        copy = exchange(k)
        copy.start()
        begin(dz_pair(t))
        begin(dr_pair(t))
        grad_x = y_now * jnp.where(unit == 0, 1.0, 0.0)
        for j in range(tiles):
            base = j * gate4
            grad_x = grad_x + mm_nt(dz[slot, :, base : base + gate4], wx[:, base : base + gate4])
        dx_ref[place(t)] = grad_x.astype(BF)
        copy.wait()
        dh[...] = (1.0 - live_h) * grad_hidden + (snd[two].astype(F32) + rcv[two].astype(F32))
        return carry

    lax.fori_loop(0, steps, backward, 0)

    def last_m(i, carry):
        sent(m_pair(steps - RING + i))
        sent(dz_pair(i))
        return carry

    lax.fori_loop(0, RING, last_m, 0)

    def finish(t, carry):
        sent(h_pair(t))
        sent(dr_pair(t))
        h_pair(t)[0].wait_recv()
        m_pair(t)[0].wait_recv()
        dr_pair(t)[0].wait_recv()
        dz_pair(t)[0].wait_recv()
        return carry

    lax.fori_loop(0, steps, finish, 0)
    x_remote.wait()
    x_local.wait()


def recurrence(x_time, y_time, lens, hidden0, cell0, bias, w_in, w_hid, proj):
    steps, streams, width = x_time.shape
    units = proj.shape[0]
    vmem = pl.BlockSpec(memory_space=pltpu.VMEM)
    hbm = pl.BlockSpec(memory_space=pl.ANY)
    shape = jax.ShapeDtypeStruct
    return pl.pallas_call(
        recurrence_kernel,
        out_shape=(
            shape((steps, streams, width), BF),
            shape((streams, width), F32),
            shape((streams, units), F32),
            shape((steps, streams, width), BF),
            shape((2, steps, streams, 2 * units), BF),
            shape((2, steps, streams, 2 * width), BF),
            shape((2, steps, streams, units // 2), BF),
            shape((2, steps, streams, width), BF),
        ),
        in_specs=[vmem] * 6 + [hbm] * 3,
        out_specs=(vmem, vmem, vmem, vmem, hbm, hbm, hbm, hbm),
        scratch_shapes=[
            pltpu.VMEM((width, 4 * units), BF),
            pltpu.VMEM((width, 4 * units), BF),
            pltpu.VMEM((4 * units, width), BF),
            pltpu.VMEM((units, width), BF),
            pltpu.VMEM((width, units), BF),
            pltpu.VMEM((2, BLK, units), BF),
            pltpu.VMEM((steps, streams, 4 * units), F32),
            pltpu.VMEM((steps + 1, streams, units), F32),
            pltpu.VMEM((steps, streams, width), F32),
            pltpu.VMEM((steps + 1, streams, width), BF),
            pltpu.VMEM((RING, streams, units), BF),
            pltpu.VMEM((steps, streams, width), BF),
            pltpu.VMEM((RING, streams, 4 * units), BF),
            pltpu.VMEM((streams, units), F32),
            pltpu.VMEM((streams, width), F32),
            pltpu.VMEM((2, streams, width), BF),
            pltpu.VMEM((2, streams, width), BF),
            pltpu.SemaphoreType.DMA((3,)),
            pltpu.SemaphoreType.DMA((2,)),
            pltpu.SemaphoreType.DMA((2,)),
            pltpu.SemaphoreType.DMA((4, steps)),
            pltpu.SemaphoreType.DMA((4, steps)),
            pltpu.SemaphoreType.DMA((4, steps)),
            pltpu.SemaphoreType.DMA((3,)),
        ],
        compiler_params=pltpu.CompilerParams(
            collective_id=0, has_side_effects=True, vmem_limit_bytes=VMEM_LIMIT
        ),
        name="recurrence",
    )(x_time, y_time, lens, hidden0, cell0, bias, w_in, w_hid, proj)


def gradient_kernel(
    lanes,
    dz_hbm,
    xh_hbm,
    m_hbm,
    dr_hbm,
    dx_ref,
    res,
    bres,
    ig_ref,
    dz,
    xh,
    xht,
    m,
    mt,
    dr,
    acc,
    own,
    from_left,
    from_right,
    bown,
    bleft,
    bright,
    rx,
    red,
    load_sem,
    l_recv,
    r_recv,
    y_recv,
    l_send,
    r_send,
    y_send,
    o_sem,
    g_send,
    g_recv,
):
    rows, cols = dz.shape
    depth = xh.shape[1]
    row_blocks = depth // BLK
    col_blocks = cols // BLK
    n_cat = row_blocks * col_blocks
    proj_cols = dr.shape[1] // BLK
    n_all = n_cat + (m.shape[1] // BLK) * proj_cols
    flip = lax.axis_index("dir")
    batch = lax.axis_index("batch")
    unit = lax.axis_index("unit")
    mine = lax.rem(batch, 2)
    lane = lax.div(batch, 2)
    mid = lanes // 2
    y_dev = {"batch": batch + 1 - 2 * mine}
    l_dev = {"batch": batch - 2}
    r_dev = {"batch": batch + 2}
    has_left = lane > 0
    has_right = lane < lanes - 1
    before = lane < mid
    after = lane > mid
    middle = lane == mid

    def group(o):
        return {
            "dir": flip + (o % 2) * (1 - 2 * flip),
            "unit": unit + (o // 2) * (1 - 2 * unit),
        }

    loads = [
        pltpu.make_async_copy(xh_hbm, xh, load_sem.at[0]),
        pltpu.make_async_copy(dz_hbm, dz, load_sem.at[1]),
        pltpu.make_async_copy(m_hbm, m, load_sem.at[2]),
        pltpu.make_async_copy(dr_hbm, dr, load_sem.at[3]),
    ]
    for one in loads:
        one.start()
    barrier = pltpu.get_barrier_semaphore()
    pl.semaphore_signal(barrier, 1, device_id=y_dev, device_id_type=MESH)
    for o in (1, 2, 3):
        pl.semaphore_signal(barrier, 1, device_id=group(o), device_id_type=MESH)

    @pl.when(has_left)
    def _():
        pl.semaphore_signal(barrier, 1, device_id=l_dev, device_id_type=MESH)

    @pl.when(has_right)
    def _():
        pl.semaphore_signal(barrier, 1, device_id=r_dev, device_id_type=MESH)

    eye = identity()

    def turn(src, dst):
        for a in range(src.shape[1] // BLK):
            for b in range(src.shape[0] // BLK):
                dst[a * BLK : (a + 1) * BLK, b * BLK : (b + 1) * BLK] = mm_nt(
                    eye, src[b * BLK : (b + 1) * BLK, a * BLK : (a + 1) * BLK]
                ).astype(BF)

    loads[0].wait()
    turn(xh, xht)
    loads[2].wait()
    turn(m, mt)
    loads[1].wait()
    loads[3].wait()

    peers = 4 + jnp.where(has_left, 1, 0) + jnp.where(has_right, 1, 0)
    pl.semaphore_wait(barrier, peers)

    quarter = dx_ref.shape[0] // 4
    me = flip + 2 * unit

    def member(o):
        p = group(o)
        return p["dir"] + 2 * p["unit"]

    def share(o):
        return pltpu.make_async_remote_copy(
            dx_ref.at[pl.ds(member(o) * quarter, quarter)],
            rx.at[o - 1],
            g_send.at[0, o - 1],
            g_recv.at[0, o - 1],
            device_id=group(o),
            device_id_type=MESH,
        )

    def spread(o):
        return pltpu.make_async_remote_copy(
            red,
            ig_ref.at[pl.ds(me * quarter, quarter)],
            g_send.at[1, o - 1],
            g_recv.at[1, o - 1],
            device_id=group(o),
            device_id_type=MESH,
        )

    for o in (1, 2, 3):
        share(o).start()

    def remote(src, dst, send, recv, k, device):
        return pltpu.make_async_remote_copy(
            src, dst, send.at[k], recv.at[k], device_id=device, device_id_type=MESH
        )

    def reduce(k, value, own_k, left_k, right_k, res_k):
        go_right = remote(own_k, left_k, r_send, l_recv, k, r_dev)
        go_left = remote(own_k, right_k, l_send, r_recv, k, l_dev)
        left_in = remote(own_k, left_k, r_send, l_recv, k, l_dev)
        right_in = remote(own_k, right_k, l_send, r_recv, k, r_dev)

        @pl.when(before)
        def _():
            @pl.when(has_left)
            def _():
                left_in.wait_recv()
                own_k[...] = (value() + left_k[...].astype(F32)).astype(BF)

            @pl.when(jnp.logical_not(has_left))
            def _():
                own_k[...] = value().astype(BF)

            go_right.start()

        @pl.when(after)
        def _():
            @pl.when(has_right)
            def _():
                right_in.wait_recv()
                own_k[...] = (value() + right_k[...].astype(F32)).astype(BF)

            @pl.when(jnp.logical_not(has_right))
            def _():
                own_k[...] = value().astype(BF)

            go_left.start()

        @pl.when(middle)
        def _():
            total = value()
            if mid > 0:
                left_in.wait_recv()
                total = total + left_k[...].astype(F32)
            if mid < lanes - 1:
                right_in.wait_recv()
                total = total + right_k[...].astype(F32)
            own_k[...] = total.astype(BF)
            if mid > 0:
                remote(own_k, res_k, l_send, r_recv, k, l_dev).start()
            if mid < lanes - 1:
                remote(own_k, res_k, r_send, l_recv, k, r_dev).start()
            remote(own_k, res_k, y_send, y_recv, k, y_dev).start()
            pltpu.make_async_copy(own_k, res_k, o_sem.at[k]).start()

    def publish(k, res_k):
        @pl.when(before)
        def _():
            remote(res_k, res_k, l_send, r_recv, k, l_dev).wait_recv()

            @pl.when(has_left)
            def _():
                remote(res_k, res_k, l_send, r_recv, k, l_dev).start()

            remote(res_k, res_k, y_send, y_recv, k, y_dev).start()

        @pl.when(after)
        def _():
            remote(res_k, res_k, r_send, l_recv, k, r_dev).wait_recv()

            @pl.when(has_right)
            def _():
                remote(res_k, res_k, r_send, l_recv, k, r_dev).start()

            remote(res_k, res_k, y_send, y_recv, k, y_dev).start()

    def finish(k, own_k, res_k):
        remote(res_k, res_k, y_send, y_recv, k, y_dev).wait()
        to_left = remote(own_k, res_k, l_send, r_recv, k, l_dev)
        to_right = remote(own_k, res_k, r_send, l_recv, k, r_dev)

        @pl.when(has_left)
        def _():
            to_left.wait_send()

        @pl.when(has_right)
        def _():
            to_right.wait_send()

        @pl.when(middle)
        def _():
            pltpu.make_async_copy(own_k, res_k, o_sem.at[k]).wait()

    ones = jnp.ones((16, rows), BF)
    total = jnp.zeros((16, BLK), F32)
    which = lax.broadcasted_iota(jnp.int32, (16, BLK), 0)
    for b in range(col_blocks):
        sums = mm(ones, dz[:, b * BLK : (b + 1) * BLK])
        total = total + jnp.where(which == b, sums, 0.0)
    acc[0:16, :] = total
    reduce(n_all, lambda: acc[0:16, :], bown, bleft, bright, bres.at[mine])

    lag = 5 * jnp.where(before, mid - lane, lane - mid) + 2

    def body(k, carry):
        @pl.when(k < n_all)
        def _():
            @pl.when(k < n_cat)
            def _():
                r = pl.multiple_of(lax.rem(k, row_blocks) * BLK, BLK)
                b = pl.multiple_of(lax.div(k, row_blocks) * BLK, BLK)
                acc[...] = mm(xht[pl.ds(r, BLK), :], dz[:, pl.ds(b, BLK)])

            @pl.when(k >= n_cat)
            def _():
                n = k - n_cat
                r = pl.multiple_of(lax.div(n, proj_cols) * BLK, BLK)
                b = pl.multiple_of(lax.rem(n, proj_cols) * BLK, BLK)
                acc[...] = mm(mt[pl.ds(r, BLK), :], dr[:, pl.ds(b, BLK)])

            reduce(
                k,
                lambda: acc[...],
                own.at[k],
                from_left.at[k],
                from_right.at[k],
                res.at[mine, k],
            )

        @pl.when(k == 10)
        def _():
            sums = dx_ref[pl.ds(me * quarter, quarter)].astype(F32)
            for o in (1, 2, 3):
                share(o).wait_recv()
                sums = sums + rx[o - 1].astype(F32)
            red[...] = sums.astype(BF)
            ig_ref[pl.ds(me * quarter, quarter)] = red[...]
            for o in (1, 2, 3):
                spread(o).start()

        n = k - lag

        @pl.when(jnp.logical_and(n >= 0, n < n_all))
        def _():
            publish(n, res.at[mine, n])

        return carry

    lax.fori_loop(0, n_all + 5 * max(mid, lanes - 1 - mid) + 2, body, 0)
    publish(n_all, bres.at[mine])

    def end(k, carry):
        finish(k, own.at[k], res.at[mine, k])
        return carry

    lax.fori_loop(0, n_all, end, 0)
    finish(n_all, bown, bres.at[mine])
    for o in (1, 2, 3):
        share(o).wait_send()
        spread(o).wait()


def gradients(lanes, dzg, xhg, mg, drg, dx):
    rows, cols = dzg.shape
    depth = xhg.shape[1]
    n_all = (depth // BLK) * (cols // BLK) + (mg.shape[1] // BLK) * (drg.shape[1] // BLK)
    steps, streams, width = dx.shape
    vmem = pl.BlockSpec(memory_space=pltpu.VMEM)
    hbm = pl.BlockSpec(memory_space=pl.ANY)
    shape = jax.ShapeDtypeStruct
    sems = pltpu.SemaphoreType.DMA((n_all + 1,))
    return pl.pallas_call(
        functools.partial(gradient_kernel, lanes),
        out_shape=(
            shape((2, n_all, BLK, BLK), BF),
            shape((2, 16, BLK), BF),
            shape((steps, streams, width), BF),
        ),
        in_specs=[hbm] * 4 + [vmem],
        out_specs=(hbm, hbm, vmem),
        scratch_shapes=[
            pltpu.VMEM((rows, cols), BF),
            pltpu.VMEM((rows, depth), BF),
            pltpu.VMEM((depth, rows), BF),
            pltpu.VMEM(mg.shape, BF),
            pltpu.VMEM((mg.shape[1], rows), BF),
            pltpu.VMEM(drg.shape, BF),
            pltpu.VMEM((BLK, BLK), F32),
            pltpu.VMEM((n_all, BLK, BLK), BF),
            pltpu.VMEM((n_all, BLK, BLK), BF),
            pltpu.VMEM((n_all, BLK, BLK), BF),
            pltpu.VMEM((16, BLK), BF),
            pltpu.VMEM((16, BLK), BF),
            pltpu.VMEM((16, BLK), BF),
            pltpu.VMEM((3, steps // 4, streams, width), BF),
            pltpu.VMEM((steps // 4, streams, width), BF),
            pltpu.SemaphoreType.DMA((4,)),
            sems,
            sems,
            sems,
            sems,
            sems,
            sems,
            sems,
            pltpu.SemaphoreType.DMA((2, 3)),
            pltpu.SemaphoreType.DMA((2, 3)),
        ],
        compiler_params=pltpu.CompilerParams(
            collective_id=1, has_side_effects=True, vmem_limit_bytes=VMEM_LIMIT
        ),
        name="gradients",
    )(dzg, xhg, mg, drg, dx)


def widen_kernel(n_cat, res, bres, wx_out, wh_out, b_out, wp_out, low, wide, bias, p_low, in_sem, out_sem, p_sem):
    units = wx_out.shape[2]
    row_blocks = low.shape[1]
    half = row_blocks // 2
    col_blocks = n_cat // row_blocks
    count = 2 * col_blocks
    n_proj = p_low.shape[1]
    proj_cols = wp_out.shape[1] // BLK

    def fetch(k, slot):
        return pltpu.make_async_copy(
            res.at[lax.div(k, col_blocks), pl.ds(lax.rem(k, col_blocks) * row_blocks, row_blocks)],
            low.at[slot],
            in_sem.at[slot],
        )

    def store(k, slot):
        owner = lax.div(k, col_blocks)
        b = lax.rem(k, col_blocks)
        gate = lax.rem(b, 4)
        u = pl.multiple_of(owner * (units // 2) + lax.div(b, 4) * BLK, BLK)
        return [
            pltpu.make_async_copy(
                wide.at[slot, i],
                out.at[:, gate, pl.ds(u, BLK)],
                out_sem.at[slot, i],
            )
            for i, out in enumerate((wx_out, wh_out))
        ]

    proj = [
        pltpu.make_async_copy(res.at[o, pl.ds(n_cat, n_proj)], p_low.at[o], p_sem.at[o])
        for o in range(2)
    ]
    for one in proj:
        one.start()
    fetch(0, 0).start()

    def body(k, carry):
        slot = lax.rem(k, 2)

        @pl.when(k + 1 < count)
        def _():
            fetch(k + 1, 1 - slot).start()

        @pl.when(k >= 2)
        def _():
            for one in store(k - 2, slot):
                one.wait()

        fetch(k, slot).wait()
        for r in range(row_blocks):
            wide[slot, r // half, (r % half) * BLK : (r % half + 1) * BLK, :] = low[slot, r].astype(F32)
        for one in store(k, slot):
            one.start()
        return carry

    lax.fori_loop(0, count, body, 0)
    for owner in range(2):
        proj[owner].wait()
        for n in range(n_proj):
            r = owner * (units // 2) + (n // proj_cols) * BLK
            col = (n % proj_cols) * BLK
            wp_out[r : r + BLK, col : col + BLK] = p_low[owner, n].astype(F32)
        for b in range(col_blocks):
            u = owner * (units // 2) + (b // 4) * BLK
            b_out[b % 4 : b % 4 + 1, u : u + BLK] = bres[owner, b : b + 1, :].astype(F32)
    for k in (count - 2, count - 1):
        for one in store(k, k % 2):
            one.wait()


def widen(res, bres, width, units):
    row_blocks = 2 * width // BLK
    n_cat = row_blocks * (2 * units // BLK)
    n_proj = res.shape[1] - n_cat
    vmem = pl.BlockSpec(memory_space=pltpu.VMEM)
    hbm = pl.BlockSpec(memory_space=pl.ANY)
    shape = jax.ShapeDtypeStruct
    return pl.pallas_call(
        functools.partial(widen_kernel, n_cat),
        out_shape=(
            shape((width, 4, units), F32),
            shape((width, 4, units), F32),
            shape((4, units), F32),
            shape((units, width), F32),
        ),
        in_specs=[hbm, vmem],
        out_specs=(hbm, hbm, vmem, vmem),
        scratch_shapes=[
            pltpu.VMEM((2, row_blocks, BLK, BLK), BF),
            pltpu.VMEM((2, 2, width, BLK), F32),
            pltpu.VMEM((8, BLK), F32),
            pltpu.VMEM((2, n_proj, BLK, BLK), BF),
            pltpu.SemaphoreType.DMA((2,)),
            pltpu.SemaphoreType.DMA((2, 2)),
            pltpu.SemaphoreType.DMA((2,)),
        ],
        compiler_params=pltpu.CompilerParams(vmem_limit_bytes=VMEM_LIMIT),
        name="widen",
    )(res, bres)


def on_device(
    inputs,
    win_count,
    last_live,
    hidden_init,
    cell_init,
    w_input,
    w_hidden,
    gate_bias,
    w_proj,
    out_grad,
):
    streams, steps, width = inputs.shape
    units = w_proj.shape[1]
    lanes = lax.axis_size("batch") // 2
    x_time = jnp.swapaxes(inputs, 0, 1)
    y_time = jnp.swapaxes(out_grad[0], 0, 1)
    lens = jnp.broadcast_to(((win_count - 1) * WIN + last_live)[:, None], (streams, 128))
    lay, hfin, cfin, dx, dzg, xhg, mg, drg = recurrence(
        x_time,
        y_time,
        lens,
        hidden_init[0],
        cell_init[0],
        gate_bias[0],
        w_input[0],
        w_hidden[0],
        w_proj[0],
    )
    rows = 2 * steps * streams
    res, bres, ig = gradients(
        lanes,
        dzg.reshape(rows, 2 * units),
        xhg.reshape(rows, 2 * width),
        mg.reshape(rows, units // 2),
        drg.reshape(rows, width),
        dx,
    )
    wx_grad, wh_grad, b_grad, wp_grad = widen(res, bres, width, units)
    return (
        jnp.swapaxes(lay, 0, 1)[None],
        jnp.swapaxes(ig, 0, 1).astype(F32),
        wx_grad[None],
        wh_grad[None],
        b_grad[None],
        wp_grad[None],
        hfin[None],
        cfin[None],
    )


def solution(mesh):
    placed = (
        P("batch", None, None),
        P("batch"),
        P("batch"),
        P("dir", "batch", None),
        P("dir", "batch", "unit"),
        P("dir", None, None, "unit"),
        P("dir", None, None, "unit"),
        P("dir", None, "unit"),
        P("dir", "unit", None),
        P("dir", "batch", None, None),
    )
    return jax.shard_map(
        on_device,
        mesh=mesh,
        in_specs=placed,
        out_specs=(
            P("dir", "batch", None, None),
            P("batch", None, None),
            P("dir", None, None, "unit"),
            P("dir", None, None, "unit"),
            P("dir", None, "unit"),
            P("dir", "unit", None),
            P("dir", "batch", None),
            P("dir", "batch", "unit"),
        ),
        check_vma=False,
    )
```

```python
import functools

import jax
import jax.numpy as jnp
from jax import lax
from jax.experimental import pallas as pl
from jax.experimental.pallas import tpu as pltpu
from jax.sharding import PartitionSpec as P

WIN = 8
BLK = 256
CUT = 128
RING = 4
LAG = 8
MESH = pl.DeviceIdType.MESH
BF = jnp.bfloat16
F32 = jnp.float32
NT = (((1,), (1,)), ((), ()))
VMEM_LIMIT = 60 * 1024 * 1024
THIRD = 1.0 / 3.0


def sigmoid(v):
    return 0.5 * jnp.tanh(0.5 * v) + 0.5


def mm(a, b):
    return jnp.dot(a, b, preferred_element_type=F32)


def mm_nt(a, b):
    return lax.dot_general(a, b, NT, preferred_element_type=F32)


def identity():
    rows = lax.broadcasted_iota(jnp.int32, (BLK, BLK), 0)
    cols = lax.broadcasted_iota(jnp.int32, (BLK, BLK), 1)
    return jnp.where(rows == cols, 1.0, 0.0).astype(BF)


def gate_order():
    rows = lax.broadcasted_iota(jnp.int32, (BLK, BLK), 0)
    cols = lax.broadcasted_iota(jnp.int32, (BLK, BLK), 1)
    want = (rows & (BLK // 4 - 1)) * 4 + (rows >> 6)
    return jnp.where(want == cols, 1.0, 0.0).astype(BF)


def recurrence_kernel(
    x_hbm,
    y_hbm,
    win_ref,
    last_ref,
    h0_ref,
    c0_ref,
    bias_ref,
    wx_hbm,
    wh_hbm,
    wp_hbm,
    lay_ref,
    hfin_ref,
    cfin_ref,
    dx_ref,
    dzg,
    xhg,
    mg,
    drg,
    w,
    wht,
    wp,
    wpt,
    raw,
    z,
    c,
    th,
    x_flat,
    y_flat,
    xh,
    y_now,
    m,
    dr,
    dz,
    dc,
    dh,
    lens,
    snd,
    rcv,
    raw_sem,
    load_sem,
    ex_send,
    ex_recv,
    y_send,
    y_recv,
    own_sem,
):
    steps, streams, width = lay_ref.shape
    units = wp.shape[0]
    tiles = units // BLK
    gate4 = 4 * BLK
    half_cols = 2 * units
    half_units = units // 2
    flip = lax.axis_index("dir")
    batch = lax.axis_index("batch")
    unit = lax.axis_index("unit")
    mine = lax.rem(batch, 2)
    other = 1 - mine
    y_dev = {"batch": batch + 1 - 2 * mine}
    x_dev = {"unit": 1 - unit}
    hid = slice(width, 2 * width)

    def place(t):
        return t + flip * (steps - 1 - 2 * t)

    slots = raw.shape[0]
    span = raw.shape[2]
    halves = units // span
    blocks = halves * width * 4 // BLK

    def fetch(n, w_hbm, slot):
        b = lax.div(n, halves)
        col = lax.rem(n, halves)
        return pltpu.make_async_copy(
            w_hbm.reshape(width * 4, units).at[
                pl.ds(pl.multiple_of(b * BLK, BLK), BLK), pl.ds(pl.multiple_of(col * span, span), span)
            ],
            raw.at[slot],
            raw_sem.at[slot],
        )

    def fetch_any(n):
        slot = lax.rem(n, slots)

        @pl.when(n < blocks)
        def _():
            fetch(n, wx_hbm, slot).start()

        @pl.when(jnp.logical_and(n >= blocks, n < 2 * blocks))
        def _():
            fetch(n - blocks, wh_hbm, slot).start()

    for n in range(slots - 1):
        fetch(n, wx_hbm, n).start()
    x_copy = pltpu.make_async_copy(x_hbm.reshape(streams * steps, width), x_flat, load_sem.at[0])
    y_copy = pltpu.make_async_copy(y_hbm.reshape(streams * steps, width), y_flat, load_sem.at[1])
    proj_copy = pltpu.make_async_copy(wp_hbm, wp, load_sem.at[2])
    x_copy.start()
    proj_copy.start()
    y_copy.start()
    barrier = pltpu.get_barrier_semaphore()
    pl.semaphore_signal(barrier, 1, device_id=x_dev, device_id_type=MESH)
    pl.semaphore_signal(barrier, 1, device_id=y_dev, device_id_type=MESH)

    order = gate_order()

    def spread(n, carry):
        slot = lax.rem(n, slots)
        fetch_any(n + slots - 1)
        fetch(0, wx_hbm, slot).wait()
        which = lax.div(n, blocks)
        left = n - which * blocks
        row = pl.multiple_of(lax.div(left, halves) * 64, 64)
        col = lax.rem(left, halves) * (4 * span)
        for j in range(span // BLK):
            got = mm(order, raw[slot, :, j * BLK : (j + 1) * BLK]).astype(BF)
            for g in range(4):
                w[
                    which,
                    pl.ds(row, 64),
                    pl.ds(pl.multiple_of(col + j * gate4 + g * BLK, BLK), BLK),
                ] = got[g * 64 : (g + 1) * 64]
        return carry

    lax.fori_loop(0, 2 * blocks, spread, 0)
    wx, wh = w.at[0], w.at[1]

    row_len = ((win_ref[...] - 1) * WIN + last_ref[...]).astype(F32)
    rows = lax.broadcasted_iota(jnp.int32, (streams, streams), 0)
    cols = lax.broadcasted_iota(jnp.int32, (streams, streams), 1)
    spot = jnp.where(rows == cols, jnp.broadcast_to(row_len, (streams, streams)), 0.0)
    lens[...] = jnp.broadcast_to(jnp.sum(spot, axis=1, keepdims=True), lens.shape)

    def live_of(t, count):
        live = jnp.where(lens[...] > place(t).astype(F32), 1.0, 0.0)
        return jnp.concatenate([live] * (count // 128), 1)

    def pick(flat, t):
        s = lax.broadcasted_iota(jnp.int32, (streams, streams * steps), 0)
        r = lax.broadcasted_iota(jnp.int32, (streams, streams * steps), 1)
        want = jnp.where(r == s * steps + place(t), 1.0, 0.0).astype(BF)
        return mm(want, flat[...]).astype(BF)

    def exchange(k):
        slot = lax.rem(k, 2)
        return pltpu.make_async_remote_copy(
            snd.at[slot],
            rcv.at[slot],
            ex_send.at[slot],
            ex_recv.at[slot],
            device_id=x_dev,
            device_id_type=MESH,
        )

    def pair(kind, t, away, keep, target):
        return (
            pltpu.make_async_remote_copy(
                away,
                target,
                y_send.at[kind, t],
                y_recv.at[kind, t],
                device_id=y_dev,
                device_id_type=MESH,
            ),
            pltpu.make_async_copy(keep, target, own_sem.at[kind, t]),
        )

    def xh_pair(t):
        return pair(0, t, xh.at[t], xh.at[t], xhg.at[mine, place(t)])

    def m_pair(t):
        slot = lax.rem(t, RING)
        away = m.at[slot, :, pl.ds(pl.multiple_of(other * half_units, half_units), half_units)]
        keep = m.at[slot, :, pl.ds(pl.multiple_of(mine * half_units, half_units), half_units)]
        return pair(1, t, away, keep, mg.at[mine, place(t)])

    def dr_pair(t):
        return pair(2, t, dr.at[t], dr.at[t], drg.at[mine, place(t)])

    def dz_pair(t):
        slot = lax.rem(t, RING)
        away = dz.at[slot, :, pl.ds(pl.multiple_of(other * half_cols, half_cols), half_cols)]
        keep = dz.at[slot, :, pl.ds(pl.multiple_of(mine * half_cols, half_cols), half_cols)]
        return pair(3, t, away, keep, dzg.at[mine, place(t)])

    def begin(copies):
        for one in copies:
            one.start()

    def sent(copies):
        copies[0].wait_send()
        copies[1].wait()

    def input_part(t):
        now = xh[t, :, :width]
        for j in range(tiles):
            part = mm(now, wx[:, j * gate4 : (j + 1) * gate4])
            for g in range(4):
                z[t, :, j * gate4 + g * BLK : j * gate4 + (g + 1) * BLK] = (
                    part[:, g * BLK : (g + 1) * BLK] + bias_ref[g : g + 1, j * BLK : (j + 1) * BLK]
                )

    eye = identity()
    x_copy.wait()
    xh[0, :, :width] = pick(x_flat, 0)
    xh[0, :, hid] = h0_ref[...].astype(BF)
    c[0] = c0_ref[...]
    input_part(0)
    proj_copy.wait()
    y_copy.wait()
    turn_cols = 4 * units // steps
    turn_units = units // steps
    pl.semaphore_wait(barrier, 2)

    def forward(t, carry):
        slot = lax.rem(t, RING)

        @pl.when(t >= RING)
        def _():
            sent(m_pair(t - RING))

        live = live_of(t, BLK) > 0.5
        hidden = xh[t, :, hid]
        for j in range(tiles):
            cols = slice(j * BLK, (j + 1) * BLK)
            base = j * gate4
            pre = z[t, :, base : base + gate4] + mm(hidden, wh[:, base : base + gate4])
            in_gate = sigmoid(pre[:, :BLK])
            forget = sigmoid(pre[:, BLK : 2 * BLK])
            cand = jnp.tanh(pre[:, 2 * BLK : 3 * BLK])
            out_gate = sigmoid(pre[:, 3 * BLK :])
            prev = c[t, :, cols]
            new = 3.0 * jnp.tanh((forget * prev + in_gate * cand) * THIRD)
            m[slot, :, cols] = (out_gate * jnp.tanh(new)).astype(BF)
            z[t, :, base : base + BLK] = in_gate
            z[t, :, base + BLK : base + 2 * BLK] = forget
            z[t, :, base + 2 * BLK : base + 3 * BLK] = cand
            z[t, :, base + 3 * BLK : base + gate4] = out_gate
            c[t + 1, :, cols] = jnp.where(live, new, prev)
        two = lax.rem(t, 2)
        snd[two] = mm(m[slot], wp[...]).astype(BF)
        copy = exchange(t)
        copy.start()
        begin(xh_pair(t))
        begin(m_pair(t))

        @pl.when(t + 1 < steps)
        def _():
            xh[t + 1, :, :width] = pick(x_flat, t + 1)
            input_part(t + 1)

        at = pl.multiple_of(t * turn_cols, turn_cols)
        for kb in range(width // BLK):
            for cb in range(turn_cols // BLK):
                wht[pl.ds(at + cb * BLK, BLK), kb * BLK : (kb + 1) * BLK] = mm_nt(
                    eye, wh[kb * BLK : (kb + 1) * BLK, pl.ds(at + cb * BLK, BLK)]
                ).astype(BF)
        at = pl.multiple_of(t * turn_units, turn_units)
        for kb in range(width // BLK):
            wpt[kb * BLK : (kb + 1) * BLK, pl.ds(at, turn_units)] = mm_nt(
                eye, wp[pl.ds(at, turn_units), kb * BLK : (kb + 1) * BLK]
            ).astype(BF)
        copy.wait()
        total = snd[two].astype(F32) + rcv[two].astype(F32)
        squash = jnp.tanh(total * THIRD)
        th[t] = squash
        new_hidden = (3.0 * squash).astype(BF).astype(F32)
        live_h = live_of(t, width)
        lay_ref[place(t)] = (xh[t, :, :width].astype(F32) + live_h * new_hidden).astype(BF)
        after = jnp.where(live_h > 0.5, new_hidden, hidden.astype(F32))

        @pl.when(t + 1 < steps)
        def _():
            xh[t + 1, :, hid] = after.astype(BF)

        @pl.when(t + 1 == steps)
        def _():
            hfin_ref[...] = after

        return carry

    lax.fori_loop(0, steps, forward, 0)
    cfin_ref[...] = c[steps]
    dc[...] = jnp.zeros_like(dc)
    dh[...] = jnp.zeros_like(dh)
    y_now[0] = pick(y_flat, steps - 1)

    def backward(k, carry):
        t = steps - 1 - k
        slot = lax.rem(t, RING)
        two = lax.rem(k, 2)

        @pl.when(k >= RING)
        def _():
            sent(dz_pair(t + RING))

        grad_hidden = dh[...]
        live_h = live_of(t, width)
        squash = th[t]
        y_low = y_now[two].astype(F32)
        low = (live_h * (y_low + grad_hidden) * (1.0 - squash * squash)).astype(BF)
        dr[t] = low
        live = live_of(t, BLK)
        part = jnp.zeros((streams, width), F32)
        for j in range(tiles):
            cols = slice(j * BLK, (j + 1) * BLK)
            base = j * gate4
            grad_m = mm(low, wpt[:, cols]).astype(BF).astype(F32)
            in_gate = z[t, :, base : base + BLK]
            forget = z[t, :, base + BLK : base + 2 * BLK]
            cand = z[t, :, base + 2 * BLK : base + 3 * BLK]
            out_gate = z[t, :, base + 3 * BLK : base + gate4]
            prev = c[t, :, cols]
            new = c[t + 1, :, cols]
            grad_c = dc[:, cols]
            tanh_new = jnp.tanh(new)
            grad_n = live * grad_c + grad_m * out_gate * (1.0 - tanh_new * tanh_new)
            third = new * THIRD
            grad_u = grad_n * (1.0 - third * third)
            dz[slot, :, base : base + BLK] = (grad_u * cand * in_gate * (1.0 - in_gate)).astype(BF)
            dz[slot, :, base + BLK : base + 2 * BLK] = (
                grad_u * prev * forget * (1.0 - forget)
            ).astype(BF)
            dz[slot, :, base + 2 * BLK : base + 3 * BLK] = (
                grad_u * in_gate * (1.0 - cand * cand)
            ).astype(BF)
            dz[slot, :, base + 3 * BLK : base + gate4] = (
                grad_m * tanh_new * out_gate * (1.0 - out_gate)
            ).astype(BF)
            dc[:, cols] = (1.0 - live) * grad_c + grad_u * forget
            part = part + mm(dz[slot, :, base : base + gate4], wht[base : base + gate4, :])
        snd[two] = part.astype(BF)
        copy = exchange(k)
        copy.start()
        begin(dz_pair(t))
        begin(dr_pair(t))

        @pl.when(k + 1 < steps)
        def _():
            y_now[1 - two] = pick(y_flat, t - 1)

        grad_x = y_low * jnp.where(unit == 0, 1.0, 0.0)
        for j in range(tiles):
            base = j * gate4
            grad_x = grad_x + mm_nt(dz[slot, :, base : base + gate4], wx[:, base : base + gate4])
        dx_ref[place(t)] = grad_x.astype(BF)
        copy.wait()
        dh[...] = (1.0 - live_h) * grad_hidden + (snd[two].astype(F32) + rcv[two].astype(F32))
        return carry

    lax.fori_loop(0, steps, backward, 0)

    def last(i, carry):
        sent(m_pair(steps - RING + i))
        sent(dz_pair(i))
        return carry

    lax.fori_loop(0, RING, last, 0)

    def finish(t, carry):
        sent(xh_pair(t))
        sent(dr_pair(t))
        xh_pair(t)[0].wait_recv()
        m_pair(t)[0].wait_recv()
        dr_pair(t)[0].wait_recv()
        dz_pair(t)[0].wait_recv()
        return carry

    lax.fori_loop(0, steps, finish, 0)


def recurrence(inputs, out_grad, win, last, hidden0, cell0, bias, w_in, w_hid, proj):
    streams, steps, width = inputs.shape
    units = proj.shape[0]
    vmem = pl.BlockSpec(memory_space=pltpu.VMEM)
    hbm = pl.BlockSpec(memory_space=pl.ANY)
    shape = jax.ShapeDtypeStruct
    return pl.pallas_call(
        recurrence_kernel,
        out_shape=(
            shape((steps, streams, width), BF),
            shape((streams, width), F32),
            shape((streams, units), F32),
            shape((steps, streams, width), BF),
            shape((2, steps, streams, 2 * units), BF),
            shape((2, steps, streams, 2 * width), BF),
            shape((2, steps, streams, units // 2), BF),
            shape((2, steps, streams, width), BF),
        ),
        in_specs=[hbm] * 2 + [vmem] * 5 + [hbm] * 3,
        out_specs=(vmem, vmem, vmem, vmem, hbm, hbm, hbm, hbm),
        scratch_shapes=[
            pltpu.VMEM((2, width, 4 * units), BF),
            pltpu.VMEM((4 * units, width), BF),
            pltpu.VMEM((units, width), BF),
            pltpu.VMEM((width, units), BF),
            pltpu.VMEM((4, BLK, units // 2), BF),
            pltpu.VMEM((steps, streams, 4 * units), F32),
            pltpu.VMEM((steps + 1, streams, units), F32),
            pltpu.VMEM((steps, streams, width), F32),
            pltpu.VMEM((streams * steps, width), BF),
            pltpu.VMEM((streams * steps, width), BF),
            pltpu.VMEM((steps, streams, 2 * width), BF),
            pltpu.VMEM((2, streams, width), BF),
            pltpu.VMEM((RING, streams, units), BF),
            pltpu.VMEM((steps, streams, width), BF),
            pltpu.VMEM((RING, streams, 4 * units), BF),
            pltpu.VMEM((streams, units), F32),
            pltpu.VMEM((streams, width), F32),
            pltpu.VMEM((streams, 128), F32),
            pltpu.VMEM((2, streams, width), BF),
            pltpu.VMEM((2, streams, width), BF),
            pltpu.SemaphoreType.DMA((4,)),
            pltpu.SemaphoreType.DMA((3,)),
            pltpu.SemaphoreType.DMA((2,)),
            pltpu.SemaphoreType.DMA((2,)),
            pltpu.SemaphoreType.DMA((4, steps)),
            pltpu.SemaphoreType.DMA((4, steps)),
            pltpu.SemaphoreType.DMA((4, steps)),
        ],
        compiler_params=pltpu.CompilerParams(
            collective_id=0, has_side_effects=True, vmem_limit_bytes=VMEM_LIMIT
        ),
        name="recurrence",
    )(inputs, out_grad, win, last, hidden0, cell0, bias, w_in, w_hid, proj)


def gradient_kernel(
    lanes,
    dz_hbm,
    xh_hbm,
    m_hbm,
    dr_hbm,
    dx_ref,
    res,
    bres,
    ig_ref,
    dz,
    xh,
    xht,
    m,
    mt,
    dr,
    acc,
    bsum,
    own,
    from_left,
    from_right,
    bown,
    bleft,
    bright,
    rx,
    red,
    load_sem,
    dz_sem,
    l_recv,
    r_recv,
    y_recv,
    l_send,
    r_send,
    y_send,
    o_sem,
    g_send,
    g_recv,
):
    rows, cols = dz.shape
    depth = xh.shape[1]
    row_blocks = depth // CUT
    col_blocks = cols // BLK
    n_cat = row_blocks * col_blocks
    proj_cols = dr.shape[1] // BLK
    n_all = n_cat + (m.shape[1] // CUT) * proj_cols
    flip = lax.axis_index("dir")
    batch = lax.axis_index("batch")
    unit = lax.axis_index("unit")
    mine = lax.rem(batch, 2)
    lane = lax.div(batch, 2)
    mid = lanes // 2
    y_dev = {"batch": batch + 1 - 2 * mine}
    l_dev = {"batch": batch - 2}
    r_dev = {"batch": batch + 2}
    has_left = lane > 0
    has_right = lane < lanes - 1
    before = lane < mid
    after = lane > mid
    middle = lane == mid

    def group(o):
        return {
            "dir": flip + (o % 2) * (1 - 2 * flip),
            "unit": unit + (o // 2) * (1 - 2 * unit),
        }

    barrier = pltpu.get_barrier_semaphore()
    pl.semaphore_signal(barrier, 1, device_id=y_dev, device_id_type=MESH)
    for o in (1, 2, 3):
        pl.semaphore_signal(barrier, 1, device_id=group(o), device_id_type=MESH)

    @pl.when(has_left)
    def _():
        pl.semaphore_signal(barrier, 1, device_id=l_dev, device_id_type=MESH)

    @pl.when(has_right)
    def _():
        pl.semaphore_signal(barrier, 1, device_id=r_dev, device_id_type=MESH)

    xh_load = pltpu.make_async_copy(xh_hbm, xh, load_sem.at[0])
    m_load = pltpu.make_async_copy(m_hbm, m, load_sem.at[1])
    dr_load = pltpu.make_async_copy(dr_hbm, dr, load_sem.at[2])

    def dz_load(b):
        at = pl.ds(pl.multiple_of(b * BLK, BLK), BLK)
        return pltpu.make_async_copy(dz_hbm.at[:, at], dz.at[:, at], dz_sem.at[b])

    xh_load.start()

    def load_all(b, carry):
        dz_load(b).start()
        return carry

    lax.fori_loop(0, col_blocks, load_all, 0)
    m_load.start()
    dr_load.start()

    eye = identity()

    def turn(src, dst, a):
        at = pl.ds(pl.multiple_of(a * BLK, BLK), BLK)
        for b in range(rows // BLK):
            dst[at, b * BLK : (b + 1) * BLK] = mm_nt(
                eye, src[b * BLK : (b + 1) * BLK, at]
            ).astype(BF)

    quarter = dx_ref.shape[0] // 4
    me = flip + 2 * unit

    def member(o):
        p = group(o)
        return p["dir"] + 2 * p["unit"]

    def share(o):
        return pltpu.make_async_remote_copy(
            dx_ref.at[pl.ds(member(o) * quarter, quarter)],
            rx.at[o - 1],
            g_send.at[0, o - 1],
            g_recv.at[0, o - 1],
            device_id=group(o),
            device_id_type=MESH,
        )

    def hand_out(o):
        return pltpu.make_async_remote_copy(
            red,
            ig_ref.at[pl.ds(me * quarter, quarter)],
            g_send.at[1, o - 1],
            g_recv.at[1, o - 1],
            device_id=group(o),
            device_id_type=MESH,
        )

    bsum[...] = jnp.zeros_like(bsum)
    xh_load.wait()
    turn(xh, xht, 0)
    peers = 4 + jnp.where(has_left, 1, 0) + jnp.where(has_right, 1, 0)
    pl.semaphore_wait(barrier, peers)

    def remote(src, dst, send, recv, k, device):
        return pltpu.make_async_remote_copy(
            src, dst, send.at[k], recv.at[k], device_id=device, device_id_type=MESH
        )

    class Chunk:
        def __init__(self, k, own_k, left_k, right_k, res_k):
            self.k, self.own, self.left, self.right, self.res = k, own_k, left_k, right_k, res_k

        def to_left(self, src):
            return remote(src, self.right, l_send, r_recv, self.k, l_dev)

        def to_right(self, src):
            return remote(src, self.left, r_send, l_recv, self.k, r_dev)

        def left_in(self):
            return remote(self.own, self.left, r_send, l_recv, self.k, l_dev)

        def right_in(self):
            return remote(self.own, self.right, l_send, r_recv, self.k, r_dev)

        def to_y(self, src):
            return remote(src, self.res, y_send, y_recv, self.k, y_dev)

        def keep(self, src):
            return pltpu.make_async_copy(src, self.res, o_sem.at[self.k])

        def reduce(self, value):
            @pl.when(before)
            def _():
                @pl.when(has_left)
                def _():
                    self.left_in().wait_recv()
                    self.own[...] = (value() + self.left[...].astype(F32)).astype(BF)

                @pl.when(jnp.logical_not(has_left))
                def _():
                    self.own[...] = value().astype(BF)

                self.to_right(self.own).start()

            @pl.when(after)
            def _():
                @pl.when(has_right)
                def _():
                    self.right_in().wait_recv()
                    self.own[...] = (value() + self.right[...].astype(F32)).astype(BF)

                @pl.when(jnp.logical_not(has_right))
                def _():
                    self.own[...] = value().astype(BF)

                self.to_left(self.own).start()

            @pl.when(middle)
            def _():
                total = value()
                if mid > 0:
                    self.left_in().wait_recv()
                    total = total + self.left[...].astype(F32)
                if mid < lanes - 1:
                    self.right_in().wait_recv()
                    total = total + self.right[...].astype(F32)
                self.own[...] = total.astype(BF)
                if mid > 0:
                    self.to_left(self.own).start()
                if mid < lanes - 1:
                    self.to_right(self.own).start()
                self.to_y(self.own).start()
                self.keep(self.own).start()

        def publish(self):
            @pl.when(before)
            def _():
                self.right_in().wait_recv()

                @pl.when(has_left)
                def _():
                    self.to_left(self.right).start()

                self.to_y(self.right).start()
                self.keep(self.right).start()

            @pl.when(after)
            def _():
                self.left_in().wait_recv()

                @pl.when(has_right)
                def _():
                    self.to_right(self.left).start()

                self.to_y(self.left).start()
                self.keep(self.left).start()

        def finish(self):
            self.to_y(self.own).wait()

            @pl.when(has_left)
            def _():
                self.to_left(self.own).wait_send()

            @pl.when(has_right)
            def _():
                self.to_right(self.own).wait_send()

            self.keep(self.own).wait()

    def chunk(k):
        return Chunk(k, own.at[k], from_left.at[k], from_right.at[k], res.at[mine, k])

    bias = Chunk(n_all, bown, bleft, bright, bres.at[mine])
    ones = jnp.ones((16, rows), BF)
    which = lax.broadcasted_iota(jnp.int32, (16, BLK), 0)
    lag = LAG * jnp.where(before, mid - lane, lane - mid) + 3
    turns = depth // BLK

    def body(k, carry):
        @pl.when(jnp.logical_and(k > 0, k < turns))
        def _():
            turn(xh, xht, k)

        @pl.when(k == row_blocks)
        def _():
            m_load.wait()
            dr_load.wait()
            for o in (1, 2, 3):
                share(o).start()

        @pl.when(jnp.logical_and(k >= row_blocks, k < row_blocks + m.shape[1] // BLK))
        def _():
            turn(m, mt, k - row_blocks)

        @pl.when(k < n_all)
        def _():
            @pl.when(k < n_cat)
            def _():
                b = lax.div(k, row_blocks)
                r = pl.multiple_of(lax.rem(k, row_blocks) * CUT, CUT)
                at = pl.ds(pl.multiple_of(b * BLK, BLK), BLK)

                @pl.when(r == 0)
                def _():
                    dz_load(b).wait()
                    bsum[...] += jnp.where(which == b, mm(ones, dz[:, at]), 0.0)

                acc[...] = mm(xht[pl.ds(r, CUT), :], dz[:, at])

            @pl.when(k >= n_cat)
            def _():
                n = k - n_cat
                r = pl.multiple_of(lax.div(n, proj_cols) * CUT, CUT)
                b = pl.multiple_of(lax.rem(n, proj_cols) * BLK, BLK)
                acc[...] = mm(mt[pl.ds(r, CUT), :], dr[:, pl.ds(b, BLK)])

            chunk(k).reduce(lambda: acc[...])

            @pl.when(k == n_cat)
            def _():
                bias.reduce(lambda: bsum[...])

        @pl.when(k == 4 * row_blocks)
        def _():
            sums = dx_ref[pl.ds(me * quarter, quarter)].astype(F32)
            for o in (1, 2, 3):
                share(o).wait_recv()
                sums = sums + rx[o - 1].astype(F32)
            red[...] = sums.astype(BF)
            ig_ref[pl.ds(me * quarter, quarter)] = red[...]
            for o in (1, 2, 3):
                hand_out(o).start()

        n = k - lag

        @pl.when(jnp.logical_and(n >= 0, n < n_all))
        def _():
            chunk(n).publish()

            @pl.when(n == n_cat)
            def _():
                bias.publish()

        return carry

    lax.fori_loop(0, n_all + LAG * max(mid, lanes - 1 - mid) + 3, body, 0)

    def end(k, carry):
        chunk(k).finish()
        return carry

    lax.fori_loop(0, n_all, end, 0)
    bias.finish()
    for o in (1, 2, 3):
        share(o).wait_send()
        hand_out(o).wait()


def gradients(lanes, dzg, xhg, mg, drg, dx):
    rows, cols = dzg.shape
    depth = xhg.shape[1]
    n_all = (depth // CUT) * (cols // BLK) + (mg.shape[1] // CUT) * (drg.shape[1] // BLK)
    steps, streams, width = dx.shape
    vmem = pl.BlockSpec(memory_space=pltpu.VMEM)
    hbm = pl.BlockSpec(memory_space=pl.ANY)
    shape = jax.ShapeDtypeStruct
    sems = pltpu.SemaphoreType.DMA((n_all + 1,))
    return pl.pallas_call(
        functools.partial(gradient_kernel, lanes),
        out_shape=(
            shape((2, n_all, CUT, BLK), BF),
            shape((2, 16, BLK), BF),
            shape((steps, streams, width), BF),
        ),
        in_specs=[hbm] * 4 + [vmem],
        out_specs=(hbm, hbm, vmem),
        scratch_shapes=[
            pltpu.VMEM((rows, cols), BF),
            pltpu.VMEM((rows, depth), BF),
            pltpu.VMEM((depth, rows), BF),
            pltpu.VMEM(mg.shape, BF),
            pltpu.VMEM((mg.shape[1], rows), BF),
            pltpu.VMEM(drg.shape, BF),
            pltpu.VMEM((CUT, BLK), F32),
            pltpu.VMEM((16, BLK), F32),
            pltpu.VMEM((n_all, CUT, BLK), BF),
            pltpu.VMEM((n_all, CUT, BLK), BF),
            pltpu.VMEM((n_all, CUT, BLK), BF),
            pltpu.VMEM((16, BLK), BF),
            pltpu.VMEM((16, BLK), BF),
            pltpu.VMEM((16, BLK), BF),
            pltpu.VMEM((3, steps // 4, streams, width), BF),
            pltpu.VMEM((steps // 4, streams, width), BF),
            pltpu.SemaphoreType.DMA((3,)),
            pltpu.SemaphoreType.DMA((cols // BLK,)),
            sems,
            sems,
            sems,
            sems,
            sems,
            sems,
            sems,
            pltpu.SemaphoreType.DMA((2, 3)),
            pltpu.SemaphoreType.DMA((2, 3)),
        ],
        compiler_params=pltpu.CompilerParams(
            collective_id=1, has_side_effects=True, vmem_limit_bytes=VMEM_LIMIT
        ),
        name="gradients",
    )(dzg, xhg, mg, drg, dx)


def widen_kernel(
    n_cat,
    res,
    bres,
    lay_in,
    ig_in,
    hfin_in,
    cfin_in,
    lay_out,
    ig_out,
    wx_out,
    wh_out,
    b_out,
    wp_out,
    hfin_out,
    cfin_out,
    low,
    wide,
    lay_buf,
    ig_buf,
    p_low,
    in_sem,
    out_sem,
    p_sem,
    s_sem,
    ig_sem,
):
    width, _, units = wx_out.shape
    steps, streams, _ = lay_in.shape
    slots = low.shape[0]
    row_blocks = low.shape[1]
    half = row_blocks // 2
    col_blocks = n_cat // row_blocks
    count = 2 * col_blocks
    n_proj = p_low.shape[1]
    proj_cols = width // BLK

    def fetch(k):
        slot = lax.rem(k, slots)
        return pltpu.make_async_copy(
            res.at[lax.div(k, col_blocks), pl.ds(lax.rem(k, col_blocks) * row_blocks, row_blocks)],
            low.at[slot],
            in_sem.at[slot],
        )

    def store(k):
        slot = lax.rem(k, slots)
        owner = lax.div(k, col_blocks)
        b = lax.rem(k, col_blocks)
        gate = lax.rem(b, 4)
        u = pl.multiple_of(owner * (units // 2) + lax.div(b, 4) * BLK, BLK)
        return [
            pltpu.make_async_copy(
                wide.at[slot, i],
                out.at[:, gate, pl.ds(u, BLK)],
                out_sem.at[slot, i],
            )
            for i, out in enumerate((wx_out, wh_out))
        ]

    for k in range(slots - 1):
        fetch(k).start()
    proj = [
        pltpu.make_async_copy(res.at[o, pl.ds(n_cat, n_proj)], p_low.at[o], p_sem.at[o])
        for o in range(2)
    ]
    states = [
        pltpu.make_async_copy(hfin_in, hfin_out, s_sem.at[0]),
        pltpu.make_async_copy(cfin_in, cfin_out, s_sem.at[1]),
    ]
    for one in proj + states:
        one.start()

    def body(k, carry):
        slot = lax.rem(k, slots)

        @pl.when(k >= slots)
        def _():
            for one in store(k - slots):
                one.wait()

        fetch(k).wait()
        for r in range(row_blocks):
            wide[slot, r // half, (r % half) * CUT : (r % half + 1) * CUT, :] = low[slot, r].astype(F32)
        for one in store(k):
            one.start()

        @pl.when(k + slots - 1 < count)
        def _():
            fetch(k + slots - 1).start()

        return carry

    lax.fori_loop(0, slots, body, 0)

    t = lax.broadcasted_iota(jnp.int32, (steps, streams * steps), 0)
    r = lax.broadcasted_iota(jnp.int32, (steps, streams * steps), 1)
    flat = lay_in[...].reshape(streams * steps, width)
    bunch = BLK // steps
    for b in range(streams // bunch):
        want = jnp.concatenate(
            [jnp.where(r == t * streams + b * bunch + s, 1.0, 0.0) for s in range(bunch)], 0
        ).astype(BF)
        lay_buf[b * BLK : (b + 1) * BLK, :] = mm(want, flat).astype(BF)
    lay_copy = pltpu.make_async_copy(lay_buf, lay_out.reshape(streams * steps, width), s_sem.at[2])
    lay_copy.start()
    ig_copies = []
    for step in range(steps):
        ig_buf[step] = ig_in[step].astype(F32)
        ig_copies.append(
            pltpu.make_async_copy(ig_buf.at[step], ig_out.at[:, step, :], ig_sem.at[step])
        )
        ig_copies[-1].start()
    for owner in range(2):
        proj[owner].wait()
        for n in range(n_proj):
            row = owner * (units // 2) + (n // proj_cols) * CUT
            col = (n % proj_cols) * BLK
            wp_out[row : row + CUT, col : col + BLK] = p_low[owner, n].astype(F32)
        for b in range(col_blocks):
            u = owner * (units // 2) + (b // 4) * BLK
            b_out[b % 4 : b % 4 + 1, u : u + BLK] = bres[owner, b : b + 1, :].astype(F32)

    lax.fori_loop(slots, count, body, 0)
    for k in range(count - slots, count):
        for one in store(k):
            one.wait()
    for one in [*states, lay_copy, *ig_copies]:
        one.wait()


def widen(res, bres, lay, ig, hfin, cfin):
    steps, streams, width = lay.shape
    units = cfin.shape[1]
    row_blocks = 2 * width // CUT
    n_cat = row_blocks * (2 * units // BLK)
    n_proj = res.shape[1] - n_cat
    slots = 4
    vmem = pl.BlockSpec(memory_space=pltpu.VMEM)
    hbm = pl.BlockSpec(memory_space=pl.ANY)
    shape = jax.ShapeDtypeStruct
    return pl.pallas_call(
        functools.partial(widen_kernel, n_cat),
        out_shape=(
            shape((streams, steps, width), BF),
            shape((streams, steps, width), F32),
            shape((width, 4, units), F32),
            shape((width, 4, units), F32),
            shape((4, units), F32),
            shape((units, width), F32),
            shape((streams, width), F32),
            shape((streams, units), F32),
        ),
        in_specs=[hbm, vmem, vmem, vmem, hbm, hbm],
        out_specs=(hbm, hbm, hbm, hbm, vmem, vmem, hbm, hbm),
        scratch_shapes=[
            pltpu.VMEM((slots, row_blocks, CUT, BLK), BF),
            pltpu.VMEM((slots, 2, width, BLK), F32),
            pltpu.VMEM((streams * steps, width), BF),
            pltpu.VMEM((steps, streams, width), F32),
            pltpu.VMEM((2, n_proj, CUT, BLK), BF),
            pltpu.SemaphoreType.DMA((slots,)),
            pltpu.SemaphoreType.DMA((slots, 2)),
            pltpu.SemaphoreType.DMA((2,)),
            pltpu.SemaphoreType.DMA((3,)),
            pltpu.SemaphoreType.DMA((steps,)),
        ],
        compiler_params=pltpu.CompilerParams(vmem_limit_bytes=VMEM_LIMIT),
        name="widen",
    )(res, bres, lay, ig, hfin, cfin)


def on_device(
    inputs,
    win_count,
    last_live,
    hidden_init,
    cell_init,
    w_input,
    w_hidden,
    gate_bias,
    w_proj,
    out_grad,
):
    streams, steps, width = inputs.shape
    units = w_proj.shape[1]
    lanes = lax.axis_size("batch") // 2
    lay, hfin, cfin, dx, dzg, xhg, mg, drg = recurrence(
        inputs,
        out_grad[0],
        win_count.reshape(1, streams),
        last_live.reshape(1, streams),
        hidden_init[0],
        cell_init[0],
        gate_bias[0],
        w_input[0],
        w_hidden[0],
        w_proj[0],
    )
    rows = 2 * steps * streams
    res, bres, ig = gradients(
        lanes,
        dzg.reshape(rows, 2 * units),
        xhg.reshape(rows, 2 * width),
        mg.reshape(rows, units // 2),
        drg.reshape(rows, width),
        dx,
    )
    out = widen(res, bres, lay, ig, hfin, cfin)
    layer_out, input_grad, wx_grad, wh_grad, b_grad, wp_grad, hidden_final, cell_final = out
    return (
        layer_out[None],
        input_grad,
        wx_grad[None],
        wh_grad[None],
        b_grad[None],
        wp_grad[None],
        hidden_final[None],
        cell_final[None],
    )


def solution(mesh):
    placed = (
        P("batch", None, None),
        P("batch"),
        P("batch"),
        P("dir", "batch", None),
        P("dir", "batch", "unit"),
        P("dir", None, None, "unit"),
        P("dir", None, None, "unit"),
        P("dir", None, "unit"),
        P("dir", "unit", None),
        P("dir", "batch", None, None),
    )
    return jax.shard_map(
        on_device,
        mesh=mesh,
        in_specs=placed,
        out_specs=(
            P("dir", "batch", None, None),
            P("batch", None, None),
            P("dir", None, None, "unit"),
            P("dir", None, None, "unit"),
            P("dir", None, "unit"),
            P("dir", "unit", None),
            P("dir", "batch", None),
            P("dir", "batch", "unit"),
        ),
        check_vma=False,
    )
```

```python
import functools

import jax
import jax.numpy as jnp
from jax import lax
from jax.experimental import pallas as pl
from jax.experimental.pallas import tpu as pltpu
from jax.sharding import PartitionSpec as P

WIN = 8
BLK = 256
CUT = 128
RING = 4
LATE = 2
RECV_RING = 32
MESH = pl.DeviceIdType.MESH
BF = jnp.bfloat16
F32 = jnp.float32
NT = (((1,), (1,)), ((), ()))
VMEM_LIMIT = 60 * 1024 * 1024
THIRD = 1.0 / 3.0


def sigmoid(v):
    return 0.5 * jnp.tanh(0.5 * v) + 0.5


def mm(a, b):
    return jnp.dot(a, b, preferred_element_type=F32)


def mm_nt(a, b):
    return lax.dot_general(a, b, NT, preferred_element_type=F32)


def identity():
    rows = lax.broadcasted_iota(jnp.int32, (BLK, BLK), 0)
    cols = lax.broadcasted_iota(jnp.int32, (BLK, BLK), 1)
    return jnp.where(rows == cols, 1.0, 0.0).astype(BF)


def gate_order():
    rows = lax.broadcasted_iota(jnp.int32, (BLK, BLK), 0)
    cols = lax.broadcasted_iota(jnp.int32, (BLK, BLK), 1)
    want = (rows & (BLK // 4 - 1)) * 4 + (rows >> 6)
    return jnp.where(want == cols, 1.0, 0.0).astype(BF)


def recurrence_kernel(
    x_hbm,
    y_hbm,
    win_ref,
    last_ref,
    h0_ref,
    c0_ref,
    bias_ref,
    wx_hbm,
    wh_hbm,
    wp_hbm,
    lay_ref,
    hfin_ref,
    cfin_ref,
    dx_ref,
    dzg,
    late,
    xhg,
    mg,
    drg,
    w,
    wht,
    wp,
    wpt,
    raw,
    z,
    c,
    th,
    x_flat,
    y_flat,
    xh,
    y_now,
    m,
    dr,
    dz,
    dc,
    dh,
    lens,
    snd,
    rcv,
    raw_sem,
    load_sem,
    ex_send,
    ex_recv,
    y_recv,
    whole_send,
    whole_keep,
    ring_send,
    ring_keep,
    late_keep,
):
    steps, streams, width = lay_ref.shape
    units = wp.shape[0]
    tiles = units // BLK
    gate4 = 4 * BLK
    half_cols = 2 * units
    half_units = units // 2
    flip = lax.axis_index("dir")
    batch = lax.axis_index("batch")
    unit = lax.axis_index("unit")
    mine = lax.rem(batch, 2)
    other = 1 - mine
    y_dev = {"batch": batch + 1 - 2 * mine}
    x_dev = {"unit": 1 - unit}
    hid = slice(width, 2 * width)

    def place(t):
        return t + flip * (steps - 1 - 2 * t)

    slots = raw.shape[0]
    span = raw.shape[2]
    halves = units // span
    blocks = halves * width * 4 // BLK

    def fetch(n, w_hbm, slot):
        b = lax.div(n, halves)
        col = lax.rem(n, halves)
        return pltpu.make_async_copy(
            w_hbm.reshape(width * 4, units).at[
                pl.ds(pl.multiple_of(b * BLK, BLK), BLK), pl.ds(pl.multiple_of(col * span, span), span)
            ],
            raw.at[slot],
            raw_sem.at[slot],
        )

    def fetch_any(n):
        slot = lax.rem(n, slots)

        @pl.when(n < blocks)
        def _():
            fetch(n, wx_hbm, slot).start()

        @pl.when(jnp.logical_and(n >= blocks, n < 2 * blocks))
        def _():
            fetch(n - blocks, wh_hbm, slot).start()

    for n in range(slots - 1):
        fetch(n, wx_hbm, n).start()
    x_copy = pltpu.make_async_copy(x_hbm.reshape(streams * steps, width), x_flat, load_sem.at[0])
    y_copy = pltpu.make_async_copy(y_hbm.reshape(streams * steps, width), y_flat, load_sem.at[1])
    proj_copy = pltpu.make_async_copy(wp_hbm, wp, load_sem.at[2])
    x_copy.start()
    proj_copy.start()
    y_copy.start()
    barrier = pltpu.get_barrier_semaphore()
    pl.semaphore_signal(barrier, 1, device_id=x_dev, device_id_type=MESH)
    pl.semaphore_signal(barrier, 1, device_id=y_dev, device_id_type=MESH)

    order = gate_order()

    def spread(n, carry):
        slot = lax.rem(n, slots)
        fetch_any(n + slots - 1)
        fetch(0, wx_hbm, slot).wait()
        which = lax.div(n, blocks)
        left = n - which * blocks
        row = pl.multiple_of(lax.div(left, halves) * 64, 64)
        col = lax.rem(left, halves) * (4 * span)
        for j in range(span // BLK):
            got = mm(order, raw[slot, :, j * BLK : (j + 1) * BLK]).astype(BF)
            for g in range(4):
                w[
                    which,
                    pl.ds(row, 64),
                    pl.ds(pl.multiple_of(col + j * gate4 + g * BLK, BLK), BLK),
                ] = got[g * 64 : (g + 1) * 64]
        return carry

    lax.fori_loop(0, 2 * blocks, spread, 0)
    wx, wh = w.at[0], w.at[1]

    row_len = ((win_ref[...] - 1) * WIN + last_ref[...]).astype(F32)
    rows = lax.broadcasted_iota(jnp.int32, (streams, streams), 0)
    cols = lax.broadcasted_iota(jnp.int32, (streams, streams), 1)
    spot = jnp.where(rows == cols, jnp.broadcast_to(row_len, (streams, streams)), 0.0)
    lens[...] = jnp.broadcast_to(jnp.sum(spot, axis=1, keepdims=True), lens.shape)

    def live_of(t, count):
        live = jnp.where(lens[...] > place(t).astype(F32), 1.0, 0.0)
        return jnp.concatenate([live] * (count // 128), 1)

    def pick(flat, t):
        s = lax.broadcasted_iota(jnp.int32, (streams, streams * steps), 0)
        r = lax.broadcasted_iota(jnp.int32, (streams, streams * steps), 1)
        want = jnp.where(r == s * steps + place(t), 1.0, 0.0).astype(BF)
        return mm(want, flat[...]).astype(BF)

    def exchange(k):
        slot = lax.rem(k, 2)
        return pltpu.make_async_remote_copy(
            snd.at[slot],
            rcv.at[slot],
            ex_send.at[slot],
            ex_recv.at[slot],
            device_id=x_dev,
            device_id_type=MESH,
        )

    def remote(away, target, send, recv):
        return pltpu.make_async_remote_copy(
            away, target, send, recv, device_id=y_dev, device_id_type=MESH
        )

    def whole(kind, src, target):
        return (
            remote(src, target, whole_send.at[kind], y_recv.at[kind]),
            pltpu.make_async_copy(src, target, whole_keep.at[kind]),
        )

    def xh_pair(t):
        return whole(0, xh.at[t], xhg.at[mine, place(t)])

    def dr_pair(t):
        return whole(1, dr.at[t], drg.at[mine, place(t)])

    def m_pair(t):
        slot = lax.rem(t, RING)
        away = m.at[slot, :, pl.ds(pl.multiple_of(other * half_units, half_units), half_units)]
        keep = m.at[slot, :, pl.ds(pl.multiple_of(mine * half_units, half_units), half_units)]
        target = mg.at[mine, place(t)]
        return (
            remote(away, target, ring_send.at[0, slot], y_recv.at[2]),
            pltpu.make_async_copy(keep, target, ring_keep.at[0, slot]),
        )

    early = half_cols - LATE * BLK

    def dz_pair(t):
        slot = lax.rem(t, RING)
        first = pl.multiple_of(other * half_cols, half_cols)
        away = dz.at[slot, :, pl.ds(first, early)]
        rest = dz.at[slot, :, pl.ds(pl.multiple_of(first + early, BLK), LATE * BLK)]
        keep = dz.at[slot, :, pl.ds(pl.multiple_of(mine * half_cols, half_cols), half_cols)]
        return (
            remote(
                away,
                dzg.at[mine, place(t), :, pl.ds(0, early)],
                ring_send.at[1, slot],
                y_recv.at[3],
            ),
            pltpu.make_async_copy(keep, dzg.at[mine, place(t)], ring_keep.at[1, slot]),
            pltpu.make_async_copy(rest, late.at[place(t)], late_keep.at[slot]),
        )

    def begin(copies):
        for one in copies:
            one.start()

    def sent(copies):
        copies[0].wait_send()
        for one in copies[1:]:
            one.wait()

    def input_part(t):
        now = xh[t, :, :width]
        for j in range(tiles):
            part = mm(now, wx[:, j * gate4 : (j + 1) * gate4])
            for g in range(4):
                z[t, :, j * gate4 + g * BLK : j * gate4 + (g + 1) * BLK] = (
                    part[:, g * BLK : (g + 1) * BLK] + bias_ref[g : g + 1, j * BLK : (j + 1) * BLK]
                )

    eye = identity()
    x_copy.wait()
    xh[0, :, :width] = pick(x_flat, 0)
    xh[0, :, hid] = h0_ref[...].astype(BF)
    c[0] = c0_ref[...]
    input_part(0)
    proj_copy.wait()
    y_copy.wait()
    turn_cols = 4 * units // steps
    turn_units = units // steps
    pl.semaphore_wait(barrier, 2)

    def forward(t, carry):
        slot = lax.rem(t, RING)

        @pl.when(t >= RING)
        def _():
            sent(m_pair(t - RING))

        live = live_of(t, BLK) > 0.5
        hidden = xh[t, :, hid]
        for j in range(tiles):
            cols = slice(j * BLK, (j + 1) * BLK)
            base = j * gate4
            pre = z[t, :, base : base + gate4] + mm(hidden, wh[:, base : base + gate4])
            in_gate = sigmoid(pre[:, :BLK])
            forget = sigmoid(pre[:, BLK : 2 * BLK])
            cand = jnp.tanh(pre[:, 2 * BLK : 3 * BLK])
            out_gate = sigmoid(pre[:, 3 * BLK :])
            prev = c[t, :, cols]
            new = 3.0 * jnp.tanh((forget * prev + in_gate * cand) * THIRD)
            m[slot, :, cols] = (out_gate * jnp.tanh(new)).astype(BF)
            z[t, :, base : base + BLK] = in_gate
            z[t, :, base + BLK : base + 2 * BLK] = forget
            z[t, :, base + 2 * BLK : base + 3 * BLK] = cand
            z[t, :, base + 3 * BLK : base + gate4] = out_gate
            c[t + 1, :, cols] = jnp.where(live, new, prev)
        two = lax.rem(t, 2)
        snd[two] = mm(m[slot], wp[...]).astype(BF)
        copy = exchange(t)
        copy.start()
        begin(xh_pair(t))
        begin(m_pair(t))

        @pl.when(t + 1 < steps)
        def _():
            xh[t + 1, :, :width] = pick(x_flat, t + 1)
            input_part(t + 1)

        at = pl.multiple_of(t * turn_cols, turn_cols)
        for kb in range(width // BLK):
            for cb in range(turn_cols // BLK):
                wht[pl.ds(at + cb * BLK, BLK), kb * BLK : (kb + 1) * BLK] = mm_nt(
                    eye, wh[kb * BLK : (kb + 1) * BLK, pl.ds(at + cb * BLK, BLK)]
                ).astype(BF)
        at = pl.multiple_of(t * turn_units, turn_units)
        for kb in range(width // BLK):
            wpt[kb * BLK : (kb + 1) * BLK, pl.ds(at, turn_units)] = mm_nt(
                eye, wp[pl.ds(at, turn_units), kb * BLK : (kb + 1) * BLK]
            ).astype(BF)
        copy.wait()
        total = snd[two].astype(F32) + rcv[two].astype(F32)
        squash = jnp.tanh(total * THIRD)
        th[t] = squash
        new_hidden = (3.0 * squash).astype(BF).astype(F32)
        live_h = live_of(t, width)
        lay_ref[place(t)] = (xh[t, :, :width].astype(F32) + live_h * new_hidden).astype(BF)
        after = jnp.where(live_h > 0.5, new_hidden, hidden.astype(F32))

        @pl.when(t + 1 < steps)
        def _():
            xh[t + 1, :, hid] = after.astype(BF)

        @pl.when(t + 1 == steps)
        def _():
            hfin_ref[...] = after

        return carry

    lax.fori_loop(0, steps, forward, 0)
    cfin_ref[...] = c[steps]
    dc[...] = jnp.zeros_like(dc)
    dh[...] = jnp.zeros_like(dh)
    y_now[0] = pick(y_flat, steps - 1)

    def backward(k, carry):
        t = steps - 1 - k
        slot = lax.rem(t, RING)
        two = lax.rem(k, 2)

        @pl.when(k >= RING)
        def _():
            sent(dz_pair(t + RING))

        grad_hidden = dh[...]
        live_h = live_of(t, width)
        squash = th[t]
        y_low = y_now[two].astype(F32)
        low = (live_h * (y_low + grad_hidden) * (1.0 - squash * squash)).astype(BF)
        dr[t] = low
        live = live_of(t, BLK)
        part = jnp.zeros((streams, width), F32)
        for j in range(tiles):
            cols = slice(j * BLK, (j + 1) * BLK)
            base = j * gate4
            grad_m = mm(low, wpt[:, cols]).astype(BF).astype(F32)
            in_gate = z[t, :, base : base + BLK]
            forget = z[t, :, base + BLK : base + 2 * BLK]
            cand = z[t, :, base + 2 * BLK : base + 3 * BLK]
            out_gate = z[t, :, base + 3 * BLK : base + gate4]
            prev = c[t, :, cols]
            new = c[t + 1, :, cols]
            grad_c = dc[:, cols]
            tanh_new = jnp.tanh(new)
            grad_n = live * grad_c + grad_m * out_gate * (1.0 - tanh_new * tanh_new)
            third = new * THIRD
            grad_u = grad_n * (1.0 - third * third)
            dz[slot, :, base : base + BLK] = (grad_u * cand * in_gate * (1.0 - in_gate)).astype(BF)
            dz[slot, :, base + BLK : base + 2 * BLK] = (
                grad_u * prev * forget * (1.0 - forget)
            ).astype(BF)
            dz[slot, :, base + 2 * BLK : base + 3 * BLK] = (
                grad_u * in_gate * (1.0 - cand * cand)
            ).astype(BF)
            dz[slot, :, base + 3 * BLK : base + gate4] = (
                grad_m * tanh_new * out_gate * (1.0 - out_gate)
            ).astype(BF)
            dc[:, cols] = (1.0 - live) * grad_c + grad_u * forget
            part = part + mm(dz[slot, :, base : base + gate4], wht[base : base + gate4, :])
        snd[two] = part.astype(BF)
        copy = exchange(k)
        copy.start()
        begin(dz_pair(t))
        begin(dr_pair(t))

        @pl.when(k + 1 < steps)
        def _():
            y_now[1 - two] = pick(y_flat, t - 1)

        grad_x = y_low * jnp.where(unit == 0, 1.0, 0.0)
        for j in range(tiles):
            base = j * gate4
            grad_x = grad_x + mm_nt(dz[slot, :, base : base + gate4], wx[:, base : base + gate4])
        dx_ref[place(t)] = grad_x.astype(BF)
        copy.wait()
        dh[...] = (1.0 - live_h) * grad_hidden + (snd[two].astype(F32) + rcv[two].astype(F32))
        return carry

    lax.fori_loop(0, steps, backward, 0)

    def last(i, carry):
        sent(m_pair(steps - RING + i))
        sent(dz_pair(i))
        return carry

    lax.fori_loop(0, RING, last, 0)

    xh_all = whole(0, xh, xhg.at[mine])
    dr_all = whole(1, dr, drg.at[mine])
    sent(xh_all)
    sent(dr_all)
    xh_all[0].wait_recv()
    dr_all[0].wait_recv()
    remote(mg.at[mine], mg.at[mine], ring_send.at[0, 0], y_recv.at[2]).wait_recv()
    part = dzg.at[mine, :, :, pl.ds(0, early)]
    remote(part, part, ring_send.at[1, 0], y_recv.at[3]).wait_recv()


def recurrence(inputs, out_grad, win, last, hidden0, cell0, bias, w_in, w_hid, proj):
    streams, steps, width = inputs.shape
    units = proj.shape[0]
    vmem = pl.BlockSpec(memory_space=pltpu.VMEM)
    hbm = pl.BlockSpec(memory_space=pl.ANY)
    shape = jax.ShapeDtypeStruct
    return pl.pallas_call(
        recurrence_kernel,
        out_shape=(
            shape((steps, streams, width), BF),
            shape((streams, width), F32),
            shape((streams, units), F32),
            shape((steps, streams, width), BF),
            shape((2, steps, streams, 2 * units), BF),
            shape((steps, streams, LATE * BLK), BF),
            shape((2, steps, streams, 2 * width), BF),
            shape((2, steps, streams, units // 2), BF),
            shape((2, steps, streams, width), BF),
        ),
        in_specs=[hbm] * 2 + [vmem] * 5 + [hbm] * 3,
        out_specs=(vmem, vmem, vmem, vmem, hbm, hbm, hbm, hbm, hbm),
        scratch_shapes=[
            pltpu.VMEM((2, width, 4 * units), BF),
            pltpu.VMEM((4 * units, width), BF),
            pltpu.VMEM((units, width), BF),
            pltpu.VMEM((width, units), BF),
            pltpu.VMEM((4, BLK, units // 2), BF),
            pltpu.VMEM((steps, streams, 4 * units), F32),
            pltpu.VMEM((steps + 1, streams, units), F32),
            pltpu.VMEM((steps, streams, width), F32),
            pltpu.VMEM((streams * steps, width), BF),
            pltpu.VMEM((streams * steps, width), BF),
            pltpu.VMEM((steps, streams, 2 * width), BF),
            pltpu.VMEM((2, streams, width), BF),
            pltpu.VMEM((RING, streams, units), BF),
            pltpu.VMEM((steps, streams, width), BF),
            pltpu.VMEM((RING, streams, 4 * units), BF),
            pltpu.VMEM((streams, units), F32),
            pltpu.VMEM((streams, width), F32),
            pltpu.VMEM((streams, 128), F32),
            pltpu.VMEM((2, streams, width), BF),
            pltpu.VMEM((2, streams, width), BF),
            pltpu.SemaphoreType.DMA((4,)),
            pltpu.SemaphoreType.DMA((3,)),
            pltpu.SemaphoreType.DMA((2,)),
            pltpu.SemaphoreType.DMA((2,)),
            pltpu.SemaphoreType.DMA((4,)),
            pltpu.SemaphoreType.DMA((2,)),
            pltpu.SemaphoreType.DMA((2,)),
            pltpu.SemaphoreType.DMA((2, RING)),
            pltpu.SemaphoreType.DMA((2, RING)),
            pltpu.SemaphoreType.DMA((RING,)),
        ],
        compiler_params=pltpu.CompilerParams(
            collective_id=0, has_side_effects=True, vmem_limit_bytes=VMEM_LIMIT
        ),
        name="recurrence",
    )(inputs, out_grad, win, last, hidden0, cell0, bias, w_in, w_hid, proj)


def gradient_kernel(
    lanes,
    dz_hbm,
    late_hbm,
    xh_hbm,
    m_hbm,
    dr_hbm,
    dx_ref,
    res,
    bres,
    ig_ref,
    dz,
    xh,
    xht,
    m,
    mt,
    dr,
    acc,
    bsum,
    own,
    from_left,
    from_right,
    bown,
    bleft,
    bright,
    rx,
    red,
    load_sem,
    dz_sem,
    late_sem,
    l_recv,
    r_recv,
    out_sem,
    b_sem,
    g_send,
    g_recv,
):
    rows, cols = dz.shape
    depth = xh.shape[1]
    row_blocks = depth // CUT
    col_blocks = cols // BLK
    n_cat = row_blocks * col_blocks
    proj_cols = dr.shape[1] // BLK
    n_all = n_cat + (m.shape[1] // CUT) * proj_cols
    flip = lax.axis_index("dir")
    batch = lax.axis_index("batch")
    unit = lax.axis_index("unit")
    mine = lax.rem(batch, 2)
    lane = lax.div(batch, 2)
    mid = lanes // 2
    y_dev = {"batch": batch + 1 - 2 * mine}
    l_dev = {"batch": batch - 2}
    r_dev = {"batch": batch + 2}
    has_left = lane > 0
    has_right = lane < lanes - 1
    before = lane < mid
    after = lane > mid
    middle = lane == mid

    def group(o):
        return {
            "dir": flip + (o % 2) * (1 - 2 * flip),
            "unit": unit + (o // 2) * (1 - 2 * unit),
        }

    barrier = pltpu.get_barrier_semaphore()
    pl.semaphore_signal(barrier, 1, device_id=y_dev, device_id_type=MESH)
    for o in (1, 2, 3):
        pl.semaphore_signal(barrier, 1, device_id=group(o), device_id_type=MESH)

    @pl.when(has_left)
    def _():
        pl.semaphore_signal(barrier, 1, device_id=l_dev, device_id_type=MESH)

    @pl.when(has_right)
    def _():
        pl.semaphore_signal(barrier, 1, device_id=r_dev, device_id_type=MESH)

    xh_load = pltpu.make_async_copy(xh_hbm, xh, load_sem.at[0])
    m_load = pltpu.make_async_copy(m_hbm, m, load_sem.at[1])
    dr_load = pltpu.make_async_copy(dr_hbm, dr, load_sem.at[2])

    half_rows = rows // 2
    my_rows = pl.ds(pl.multiple_of(mine * half_rows, half_rows), half_rows)
    first_late = col_blocks - LATE
    late_cols = pl.ds(first_late * BLK, LATE * BLK)

    def dz_load(b):
        at = pl.ds(pl.multiple_of(b * BLK, BLK), BLK)
        return pltpu.make_async_copy(dz_hbm.at[:, at], dz.at[:, at], dz_sem.at[b])

    late_own = pltpu.make_async_copy(
        dz_hbm.at[my_rows, late_cols], dz.at[my_rows, late_cols], late_sem.at[0]
    )
    late_far = pltpu.make_async_remote_copy(
        late_hbm,
        dz.at[my_rows, late_cols],
        late_sem.at[1],
        late_sem.at[2],
        device_id=y_dev,
        device_id_type=MESH,
    )

    xh_load.start()

    def load_all(b, carry):
        dz_load(b).start()
        return carry

    lax.fori_loop(0, first_late, load_all, 0)
    late_own.start()
    m_load.start()
    dr_load.start()

    eye = identity()

    def turn(src, dst, a):
        at = pl.ds(pl.multiple_of(a * BLK, BLK), BLK)
        for b in range(rows // BLK):
            dst[at, b * BLK : (b + 1) * BLK] = mm_nt(
                eye, src[b * BLK : (b + 1) * BLK, at]
            ).astype(BF)

    quarter = dx_ref.shape[0] // 4
    me = flip + 2 * unit

    def member(o):
        p = group(o)
        return p["dir"] + 2 * p["unit"]

    def share(o):
        return pltpu.make_async_remote_copy(
            dx_ref.at[pl.ds(member(o) * quarter, quarter)],
            rx.at[o - 1],
            g_send.at[0, o - 1],
            g_recv.at[0, o - 1],
            device_id=group(o),
            device_id_type=MESH,
        )

    def hand_out(o):
        return pltpu.make_async_remote_copy(
            red,
            ig_ref.at[pl.ds(me * quarter, quarter)],
            g_send.at[1, o - 1],
            g_recv.at[1, o - 1],
            device_id=group(o),
            device_id_type=MESH,
        )

    bsum[...] = jnp.zeros_like(bsum)
    xh_load.wait()
    turn(xh, xht, 0)
    peers = 4 + jnp.where(has_left, 1, 0) + jnp.where(has_right, 1, 0)
    pl.semaphore_wait(barrier, peers)
    late_far.start()

    def remote(src, dst, send, recv, device):
        return pltpu.make_async_remote_copy(
            src, dst, send, recv, device_id=device, device_id_type=MESH
        )

    class Chunk:
        def __init__(self, refs, sems):
            self.own, self.left, self.right, self.res = refs
            self.l_recv, self.r_recv, self.l_send, self.r_send = sems[:4]
            self.y_send, self.y_recv, self.kept = sems[4:]

        def to_left(self, src):
            return remote(src, self.right, self.l_send, self.r_recv, l_dev)

        def to_right(self, src):
            return remote(src, self.left, self.r_send, self.l_recv, r_dev)

        def left_in(self):
            return remote(self.own, self.left, self.r_send, self.l_recv, l_dev)

        def right_in(self):
            return remote(self.own, self.right, self.l_send, self.r_recv, r_dev)

        def to_y(self, src):
            return remote(src, self.res, self.y_send, self.y_recv, y_dev)

        def keep(self, src):
            return pltpu.make_async_copy(src, self.res, self.kept)

        def reduce(self, value):
            @pl.when(before)
            def _():
                @pl.when(has_left)
                def _():
                    self.left_in().wait_recv()
                    self.own[...] = (value() + self.left[...].astype(F32)).astype(BF)

                @pl.when(jnp.logical_not(has_left))
                def _():
                    self.own[...] = value().astype(BF)

                self.to_right(self.own).start()

            @pl.when(after)
            def _():
                @pl.when(has_right)
                def _():
                    self.right_in().wait_recv()
                    self.own[...] = (value() + self.right[...].astype(F32)).astype(BF)

                @pl.when(jnp.logical_not(has_right))
                def _():
                    self.own[...] = value().astype(BF)

                self.to_left(self.own).start()

            @pl.when(middle)
            def _():
                total = value()
                if mid > 0:
                    self.left_in().wait_recv()
                    total = total + self.left[...].astype(F32)
                if mid < lanes - 1:
                    self.right_in().wait_recv()
                    total = total + self.right[...].astype(F32)
                self.own[...] = total.astype(BF)
                if mid > 0:
                    self.to_left(self.own).start()
                if mid < lanes - 1:
                    self.to_right(self.own).start()
                self.to_y(self.own).start()
                self.keep(self.own).start()

        def publish(self):
            @pl.when(before)
            def _():
                self.right_in().wait_recv()

                @pl.when(has_left)
                def _():
                    self.to_left(self.right).start()

                self.to_y(self.right).start()
                self.keep(self.right).start()

            @pl.when(after)
            def _():
                self.left_in().wait_recv()

                @pl.when(has_right)
                def _():
                    self.to_right(self.left).start()

                self.to_y(self.left).start()
                self.keep(self.left).start()

        def finish(self):
            self.to_y(self.own).wait()

            @pl.when(has_left)
            def _():
                self.to_left(self.own).wait_send()

            @pl.when(has_right)
            def _():
                self.to_right(self.own).wait_send()

            self.keep(self.own).wait()

    leaving = [out_sem.at[i] for i in range(5)]

    def chunk(k):
        slot = lax.rem(k, RECV_RING)
        refs = (own.at[k], from_left.at[k], from_right.at[k], res.at[mine, k])
        return Chunk(refs, [l_recv.at[slot], r_recv.at[slot], *leaving])

    every = Chunk((own, from_left, from_right, res.at[mine]), [l_recv.at[0], r_recv.at[0], *leaving])
    bias = Chunk((bown, bleft, bright, bres.at[mine]), [b_sem.at[i] for i in range(7)])
    ones = jnp.ones((16, rows), BF)
    which = lax.broadcasted_iota(jnp.int32, (16, BLK), 0)
    far = jnp.where(before, mid - lane, lane - mid)
    inner = jnp.logical_and(has_left, has_right)
    lag = 5 * far + jnp.where(inner, 0, 12)
    longest = 5 * max(mid, lanes - 1 - mid) + 12
    turns = depth // BLK

    def body(k, carry):
        @pl.when(jnp.logical_and(k > 0, k < turns))
        def _():
            turn(xh, xht, k)

        @pl.when(k == row_blocks)
        def _():
            m_load.wait()
            dr_load.wait()
            for o in (1, 2, 3):
                share(o).start()

        @pl.when(jnp.logical_and(k >= row_blocks, k < row_blocks + m.shape[1] // BLK))
        def _():
            turn(m, mt, k - row_blocks)

        @pl.when(k < n_all)
        def _():
            @pl.when(k < n_cat)
            def _():
                b = lax.div(k, row_blocks)
                r = pl.multiple_of(lax.rem(k, row_blocks) * CUT, CUT)
                at = pl.ds(pl.multiple_of(b * BLK, BLK), BLK)

                @pl.when(jnp.logical_and(r == 0, b < first_late))
                def _():
                    dz_load(b).wait()

                @pl.when(jnp.logical_and(r == 0, b == first_late))
                def _():
                    late_own.wait()
                    late_far.wait_recv()

                @pl.when(r == 0)
                def _():
                    bsum[...] += jnp.where(which == b, mm(ones, dz[:, at]), 0.0)

                acc[...] = mm(xht[pl.ds(r, CUT), :], dz[:, at])

            @pl.when(k >= n_cat)
            def _():
                n = k - n_cat
                r = pl.multiple_of(lax.div(n, proj_cols) * CUT, CUT)
                b = pl.multiple_of(lax.rem(n, proj_cols) * BLK, BLK)
                acc[...] = mm(mt[pl.ds(r, CUT), :], dr[:, pl.ds(b, BLK)])

            chunk(k).reduce(lambda: acc[...])

            @pl.when(k == n_cat)
            def _():
                bias.reduce(lambda: bsum[...])

        @pl.when(k == 4 * row_blocks)
        def _():
            sums = dx_ref[pl.ds(me * quarter, quarter)].astype(F32)
            for o in (1, 2, 3):
                share(o).wait_recv()
                sums = sums + rx[o - 1].astype(F32)
            red[...] = sums.astype(BF)
            ig_ref[pl.ds(me * quarter, quarter)] = red[...]
            for o in (1, 2, 3):
                hand_out(o).start()

        n = k - lag

        @pl.when(jnp.logical_and(n >= 0, n < n_all))
        def _():
            chunk(n).publish()

            @pl.when(n == n_cat)
            def _():
                bias.publish()

        return carry

    lax.fori_loop(0, n_all + longest, body, 0)
    every.finish()
    late_far.wait_send()
    bias.finish()
    for o in (1, 2, 3):
        share(o).wait_send()
        hand_out(o).wait()


def gradients(lanes, dzg, late, xhg, mg, drg, dx):
    rows, cols = dzg.shape
    depth = xhg.shape[1]
    n_all = (depth // CUT) * (cols // BLK) + (mg.shape[1] // CUT) * (drg.shape[1] // BLK)
    steps, streams, width = dx.shape
    vmem = pl.BlockSpec(memory_space=pltpu.VMEM)
    hbm = pl.BlockSpec(memory_space=pl.ANY)
    shape = jax.ShapeDtypeStruct
    return pl.pallas_call(
        functools.partial(gradient_kernel, lanes),
        out_shape=(
            shape((2, n_all, CUT, BLK), BF),
            shape((2, 16, BLK), BF),
            shape((steps, streams, width), BF),
        ),
        in_specs=[hbm] * 5 + [vmem],
        out_specs=(hbm, hbm, vmem),
        scratch_shapes=[
            pltpu.VMEM((rows, cols), BF),
            pltpu.VMEM((rows, depth), BF),
            pltpu.VMEM((depth, rows), BF),
            pltpu.VMEM(mg.shape, BF),
            pltpu.VMEM((mg.shape[1], rows), BF),
            pltpu.VMEM(drg.shape, BF),
            pltpu.VMEM((CUT, BLK), F32),
            pltpu.VMEM((16, BLK), F32),
            pltpu.VMEM((n_all, CUT, BLK), BF),
            pltpu.VMEM((n_all, CUT, BLK), BF),
            pltpu.VMEM((n_all, CUT, BLK), BF),
            pltpu.VMEM((16, BLK), BF),
            pltpu.VMEM((16, BLK), BF),
            pltpu.VMEM((16, BLK), BF),
            pltpu.VMEM((3, steps // 4, streams, width), BF),
            pltpu.VMEM((steps // 4, streams, width), BF),
            pltpu.SemaphoreType.DMA((3,)),
            pltpu.SemaphoreType.DMA((cols // BLK,)),
            pltpu.SemaphoreType.DMA((3,)),
            pltpu.SemaphoreType.DMA((RECV_RING,)),
            pltpu.SemaphoreType.DMA((RECV_RING,)),
            pltpu.SemaphoreType.DMA((5,)),
            pltpu.SemaphoreType.DMA((7,)),
            pltpu.SemaphoreType.DMA((2, 3)),
            pltpu.SemaphoreType.DMA((2, 3)),
        ],
        compiler_params=pltpu.CompilerParams(
            collective_id=1, has_side_effects=True, vmem_limit_bytes=VMEM_LIMIT
        ),
        name="gradients",
    )(dzg, late, xhg, mg, drg, dx)


def widen_kernel(
    n_cat,
    res,
    bres,
    lay_in,
    ig_in,
    hfin_in,
    cfin_in,
    lay_out,
    ig_out,
    wx_out,
    wh_out,
    b_out,
    wp_out,
    hfin_out,
    cfin_out,
    low,
    wide,
    lay_buf,
    ig_buf,
    p_low,
    in_sem,
    out_sem,
    p_sem,
    s_sem,
    ig_sem,
):
    width, _, units = wx_out.shape
    steps, streams, _ = lay_in.shape
    slots = low.shape[0]
    row_blocks = low.shape[1]
    half = row_blocks // 2
    col_blocks = n_cat // row_blocks
    count = 2 * col_blocks
    n_proj = p_low.shape[1]
    proj_cols = width // BLK

    def fetch(k):
        slot = lax.rem(k, slots)
        return pltpu.make_async_copy(
            res.at[lax.div(k, col_blocks), pl.ds(lax.rem(k, col_blocks) * row_blocks, row_blocks)],
            low.at[slot],
            in_sem.at[slot],
        )

    def store(k):
        slot = lax.rem(k, slots)
        owner = lax.div(k, col_blocks)
        b = lax.rem(k, col_blocks)
        gate = lax.rem(b, 4)
        u = pl.multiple_of(owner * (units // 2) + lax.div(b, 4) * BLK, BLK)
        return [
            pltpu.make_async_copy(
                wide.at[slot, i],
                out.at[:, gate, pl.ds(u, BLK)],
                out_sem.at[slot, i],
            )
            for i, out in enumerate((wx_out, wh_out))
        ]

    for k in range(slots - 1):
        fetch(k).start()
    proj = [
        pltpu.make_async_copy(res.at[o, pl.ds(n_cat, n_proj)], p_low.at[o], p_sem.at[o])
        for o in range(2)
    ]
    states = [
        pltpu.make_async_copy(hfin_in, hfin_out, s_sem.at[0]),
        pltpu.make_async_copy(cfin_in, cfin_out, s_sem.at[1]),
    ]
    for one in proj + states:
        one.start()

    def body(k, carry):
        slot = lax.rem(k, slots)

        @pl.when(k >= slots)
        def _():
            for one in store(k - slots):
                one.wait()

        fetch(k).wait()
        for r in range(row_blocks):
            wide[slot, r // half, (r % half) * CUT : (r % half + 1) * CUT, :] = low[slot, r].astype(F32)
        for one in store(k):
            one.start()

        @pl.when(k + slots - 1 < count)
        def _():
            fetch(k + slots - 1).start()

        return carry

    lax.fori_loop(0, slots, body, 0)

    t = lax.broadcasted_iota(jnp.int32, (steps, streams * steps), 0)
    r = lax.broadcasted_iota(jnp.int32, (steps, streams * steps), 1)
    flat = lay_in[...].reshape(streams * steps, width)
    bunch = BLK // steps
    for b in range(streams // bunch):
        want = jnp.concatenate(
            [jnp.where(r == t * streams + b * bunch + s, 1.0, 0.0) for s in range(bunch)], 0
        ).astype(BF)
        lay_buf[b * BLK : (b + 1) * BLK, :] = mm(want, flat).astype(BF)
    lay_copy = pltpu.make_async_copy(lay_buf, lay_out.reshape(streams * steps, width), s_sem.at[2])
    lay_copy.start()
    ig_copies = []
    for step in range(steps):
        ig_buf[step] = ig_in[step].astype(F32)
        ig_copies.append(
            pltpu.make_async_copy(ig_buf.at[step], ig_out.at[:, step, :], ig_sem.at[step])
        )
        ig_copies[-1].start()
    for owner in range(2):
        proj[owner].wait()
        for n in range(n_proj):
            row = owner * (units // 2) + (n // proj_cols) * CUT
            col = (n % proj_cols) * BLK
            wp_out[row : row + CUT, col : col + BLK] = p_low[owner, n].astype(F32)
        for b in range(col_blocks):
            u = owner * (units // 2) + (b // 4) * BLK
            b_out[b % 4 : b % 4 + 1, u : u + BLK] = bres[owner, b : b + 1, :].astype(F32)

    lax.fori_loop(slots, count, body, 0)
    for k in range(count - slots, count):
        for one in store(k):
            one.wait()
    for one in [*states, lay_copy, *ig_copies]:
        one.wait()


def widen(res, bres, lay, ig, hfin, cfin):
    steps, streams, width = lay.shape
    units = cfin.shape[1]
    row_blocks = 2 * width // CUT
    n_cat = row_blocks * (2 * units // BLK)
    n_proj = res.shape[1] - n_cat
    slots = 4
    vmem = pl.BlockSpec(memory_space=pltpu.VMEM)
    hbm = pl.BlockSpec(memory_space=pl.ANY)
    shape = jax.ShapeDtypeStruct
    return pl.pallas_call(
        functools.partial(widen_kernel, n_cat),
        out_shape=(
            shape((streams, steps, width), BF),
            shape((streams, steps, width), F32),
            shape((width, 4, units), F32),
            shape((width, 4, units), F32),
            shape((4, units), F32),
            shape((units, width), F32),
            shape((streams, width), F32),
            shape((streams, units), F32),
        ),
        in_specs=[hbm, vmem, vmem, vmem, hbm, hbm],
        out_specs=(hbm, hbm, hbm, hbm, vmem, vmem, hbm, hbm),
        scratch_shapes=[
            pltpu.VMEM((slots, row_blocks, CUT, BLK), BF),
            pltpu.VMEM((slots, 2, width, BLK), F32),
            pltpu.VMEM((streams * steps, width), BF),
            pltpu.VMEM((steps, streams, width), F32),
            pltpu.VMEM((2, n_proj, CUT, BLK), BF),
            pltpu.SemaphoreType.DMA((slots,)),
            pltpu.SemaphoreType.DMA((slots, 2)),
            pltpu.SemaphoreType.DMA((2,)),
            pltpu.SemaphoreType.DMA((3,)),
            pltpu.SemaphoreType.DMA((steps,)),
        ],
        compiler_params=pltpu.CompilerParams(vmem_limit_bytes=VMEM_LIMIT),
        name="widen",
    )(res, bres, lay, ig, hfin, cfin)


def on_device(
    inputs,
    win_count,
    last_live,
    hidden_init,
    cell_init,
    w_input,
    w_hidden,
    gate_bias,
    w_proj,
    out_grad,
):
    streams, steps, width = inputs.shape
    units = w_proj.shape[1]
    lanes = lax.axis_size("batch") // 2
    lay, hfin, cfin, dx, dzg, late, xhg, mg, drg = recurrence(
        inputs,
        out_grad[0],
        win_count.reshape(1, streams),
        last_live.reshape(1, streams),
        hidden_init[0],
        cell_init[0],
        gate_bias[0],
        w_input[0],
        w_hidden[0],
        w_proj[0],
    )
    rows = 2 * steps * streams
    res, bres, ig = gradients(
        lanes,
        dzg.reshape(rows, 2 * units),
        late.reshape(steps * streams, LATE * BLK),
        xhg.reshape(rows, 2 * width),
        mg.reshape(rows, units // 2),
        drg.reshape(rows, width),
        dx,
    )
    out = widen(res, bres, lay, ig, hfin, cfin)
    layer_out, input_grad, wx_grad, wh_grad, b_grad, wp_grad, hidden_final, cell_final = out
    return (
        layer_out[None],
        input_grad,
        wx_grad[None],
        wh_grad[None],
        b_grad[None],
        wp_grad[None],
        hidden_final[None],
        cell_final[None],
    )


def solution(mesh):
    placed = (
        P("batch", None, None),
        P("batch"),
        P("batch"),
        P("dir", "batch", None),
        P("dir", "batch", "unit"),
        P("dir", None, None, "unit"),
        P("dir", None, None, "unit"),
        P("dir", None, "unit"),
        P("dir", "unit", None),
        P("dir", "batch", None, None),
    )
    return jax.shard_map(
        on_device,
        mesh=mesh,
        in_specs=placed,
        out_specs=(
            P("dir", "batch", None, None),
            P("batch", None, None),
            P("dir", None, None, "unit"),
            P("dir", None, None, "unit"),
            P("dir", None, "unit"),
            P("dir", "unit", None),
            P("dir", "batch", None),
            P("dir", "batch", "unit"),
        ),
        check_vma=False,
    )
```

```python
import functools

import jax
import jax.numpy as jnp
from jax import lax
from jax.experimental import pallas as pl
from jax.experimental.pallas import tpu as pltpu
from jax.sharding import PartitionSpec as P

WIN = 8
BLK = 256
CUT = 128
RING = 4
LATE = 3
RECV_RING = 32
MESH = pl.DeviceIdType.MESH
BF = jnp.bfloat16
F32 = jnp.float32
NT = (((1,), (1,)), ((), ()))
VMEM_LIMIT = 60 * 1024 * 1024
THIRD = 1.0 / 3.0


def sigmoid(v):
    return 0.5 * jnp.tanh(0.5 * v) + 0.5


def mm(a, b):
    return jnp.dot(a, b, preferred_element_type=F32)


def mm_pad(a, b):
    fill = jnp.zeros((128 - a.shape[0], a.shape[1]), a.dtype)
    return mm(jnp.concatenate([a, fill], 0), b)[: a.shape[0]]


def mm_nt(a, b):
    return lax.dot_general(a, b, NT, preferred_element_type=F32)


def identity():
    rows = lax.broadcasted_iota(jnp.int32, (BLK, BLK), 0)
    cols = lax.broadcasted_iota(jnp.int32, (BLK, BLK), 1)
    return jnp.where(rows == cols, 1.0, 0.0).astype(BF)


def gate_order():
    rows = lax.broadcasted_iota(jnp.int32, (BLK, BLK), 0)
    cols = lax.broadcasted_iota(jnp.int32, (BLK, BLK), 1)
    want = (rows & (BLK // 4 - 1)) * 4 + (rows >> 6)
    return jnp.where(want == cols, 1.0, 0.0).astype(BF)


def recurrence_kernel(
    x_hbm,
    y_hbm,
    win_ref,
    last_ref,
    h0_ref,
    c0_ref,
    bias_ref,
    wx_hbm,
    wh_hbm,
    wp_hbm,
    lay_ref,
    hfin_ref,
    cfin_ref,
    dx_ref,
    dzg,
    late,
    xhg,
    mg,
    drg,
    w,
    wht,
    wp,
    wpt,
    raw,
    z,
    c,
    th,
    x_flat,
    y_flat,
    xh,
    y_now,
    m,
    dr,
    dz,
    dc,
    dh,
    lens,
    snd,
    rcv,
    raw_sem,
    load_sem,
    ex_send,
    ex_recv,
    y_recv,
    whole_send,
    whole_keep,
    ring_send,
    ring_keep,
    late_keep,
):
    steps, streams, width = lay_ref.shape
    units = wp.shape[0]
    tiles = units // BLK
    gate4 = 4 * BLK
    half_cols = 2 * units
    half_units = units // 2
    flip = lax.axis_index("dir")
    batch = lax.axis_index("batch")
    unit = lax.axis_index("unit")
    mine = lax.rem(batch, 2)
    other = 1 - mine
    y_dev = {"batch": batch + 1 - 2 * mine}
    x_dev = {"unit": 1 - unit}
    hid = slice(width, 2 * width)

    def place(t):
        return t + flip * (steps - 1 - 2 * t)

    slots = raw.shape[0]
    span = raw.shape[2]
    halves = units // span
    blocks = halves * width * 4 // BLK

    def fetch(n, w_hbm, slot):
        b = lax.div(n, halves)
        col = lax.rem(n, halves)
        return pltpu.make_async_copy(
            w_hbm.reshape(width * 4, units).at[
                pl.ds(pl.multiple_of(b * BLK, BLK), BLK), pl.ds(pl.multiple_of(col * span, span), span)
            ],
            raw.at[slot],
            raw_sem.at[slot],
        )

    def fetch_any(n):
        slot = lax.rem(n, slots)

        @pl.when(n < blocks)
        def _():
            fetch(n, wx_hbm, slot).start()

        @pl.when(jnp.logical_and(n >= blocks, n < 2 * blocks))
        def _():
            fetch(n - blocks, wh_hbm, slot).start()

    for n in range(slots - 1):
        fetch(n, wx_hbm, n).start()
    x_copy = pltpu.make_async_copy(x_hbm.reshape(streams * steps, width), x_flat, load_sem.at[0])
    y_copy = pltpu.make_async_copy(y_hbm.reshape(streams * steps, width), y_flat, load_sem.at[1])
    proj_copy = pltpu.make_async_copy(wp_hbm, wp, load_sem.at[2])
    x_copy.start()
    proj_copy.start()
    y_copy.start()
    barrier = pltpu.get_barrier_semaphore()
    pl.semaphore_signal(barrier, 1, device_id=x_dev, device_id_type=MESH)
    pl.semaphore_signal(barrier, 1, device_id=y_dev, device_id_type=MESH)

    order = gate_order()

    def spread(n, carry):
        slot = lax.rem(n, slots)
        fetch_any(n + slots - 1)
        fetch(0, wx_hbm, slot).wait()
        which = lax.div(n, blocks)
        left = n - which * blocks
        row = pl.multiple_of(lax.div(left, halves) * 64, 64)
        col = lax.rem(left, halves) * (4 * span)
        for j in range(span // BLK):
            got = mm(order, raw[slot, :, j * BLK : (j + 1) * BLK]).astype(BF)
            for g in range(4):
                w[
                    which,
                    pl.ds(row, 64),
                    pl.ds(pl.multiple_of(col + j * gate4 + g * BLK, BLK), BLK),
                ] = got[g * 64 : (g + 1) * 64]
        return carry

    lax.fori_loop(0, 2 * blocks, spread, 0)
    wx, wh = w.at[0], w.at[1]

    row_len = ((win_ref[...] - 1) * WIN + last_ref[...]).astype(F32)
    rows = lax.broadcasted_iota(jnp.int32, (streams, streams), 0)
    cols = lax.broadcasted_iota(jnp.int32, (streams, streams), 1)
    spot = jnp.where(rows == cols, jnp.broadcast_to(row_len, (streams, streams)), 0.0)
    lens[...] = jnp.broadcast_to(jnp.sum(spot, axis=1, keepdims=True), lens.shape)

    def live_of(t, count):
        live = jnp.where(lens[...] > place(t).astype(F32), 1.0, 0.0)
        return jnp.concatenate([live] * (count // 128), 1)

    def pick(flat, t):
        s = lax.broadcasted_iota(jnp.int32, (streams, streams * steps), 0)
        r = lax.broadcasted_iota(jnp.int32, (streams, streams * steps), 1)
        want = jnp.where(r == s * steps + place(t), 1.0, 0.0).astype(BF)
        return mm(want, flat[...]).astype(BF)

    def exchange(k):
        slot = lax.rem(k, 2)
        return pltpu.make_async_remote_copy(
            snd.at[slot],
            rcv.at[slot],
            ex_send.at[slot],
            ex_recv.at[slot],
            device_id=x_dev,
            device_id_type=MESH,
        )

    def remote(away, target, send, recv):
        return pltpu.make_async_remote_copy(
            away, target, send, recv, device_id=y_dev, device_id_type=MESH
        )

    def whole(kind, src, target):
        return (
            remote(src, target, whole_send.at[kind], y_recv.at[kind]),
            pltpu.make_async_copy(src, target, whole_keep.at[kind]),
        )

    def xh_pair(t):
        return whole(0, xh.at[t], xhg.at[mine, place(t)])

    def dr_pair(t):
        return whole(1, dr.at[t], drg.at[mine, place(t)])

    def m_pair(t):
        slot = lax.rem(t, RING)
        away = m.at[slot, :, pl.ds(pl.multiple_of(other * half_units, half_units), half_units)]
        keep = m.at[slot, :, pl.ds(pl.multiple_of(mine * half_units, half_units), half_units)]
        target = mg.at[mine, place(t)]
        return (
            remote(away, target, ring_send.at[0, slot], y_recv.at[2]),
            pltpu.make_async_copy(keep, target, ring_keep.at[0, slot]),
        )

    early = half_cols - LATE * BLK

    def dz_pair(t):
        slot = lax.rem(t, RING)
        first = pl.multiple_of(other * half_cols, half_cols)
        away = dz.at[slot, :, pl.ds(first, early)]
        rest = dz.at[slot, :, pl.ds(pl.multiple_of(first + early, BLK), LATE * BLK)]
        keep = dz.at[slot, :, pl.ds(pl.multiple_of(mine * half_cols, half_cols), half_cols)]
        return (
            remote(
                away,
                dzg.at[mine, place(t), :, pl.ds(0, early)],
                ring_send.at[1, slot],
                y_recv.at[3],
            ),
            pltpu.make_async_copy(keep, dzg.at[mine, place(t)], ring_keep.at[1, slot]),
            pltpu.make_async_copy(rest, late.at[place(t)], late_keep.at[slot]),
        )

    def begin(copies):
        for one in copies:
            one.start()

    def sent(copies):
        copies[0].wait_send()
        for one in copies[1:]:
            one.wait()

    def input_part(t):
        now = xh[t, :, :width]
        for j in range(tiles):
            part = mm(now, wx[:, j * gate4 : (j + 1) * gate4])
            for g in range(4):
                z[t, :, j * gate4 + g * BLK : j * gate4 + (g + 1) * BLK] = (
                    part[:, g * BLK : (g + 1) * BLK] + bias_ref[g : g + 1, j * BLK : (j + 1) * BLK]
                )

    eye = identity()
    x_copy.wait()
    xh[0, :, :width] = pick(x_flat, 0)
    xh[0, :, hid] = h0_ref[...].astype(BF)
    c[0] = c0_ref[...]
    input_part(0)
    proj_copy.wait()
    y_copy.wait()
    turn_cols = 4 * units // steps
    turn_units = units // steps
    pl.semaphore_wait(barrier, 2)

    def forward(t, carry):
        slot = lax.rem(t, RING)

        @pl.when(t >= RING)
        def _():
            sent(m_pair(t - RING))

        live = live_of(t, BLK) > 0.5
        hidden = xh[t, :, hid]
        for j in range(tiles):
            cols = slice(j * BLK, (j + 1) * BLK)
            base = j * gate4
            pre = z[t, :, base : base + gate4] + mm_pad(hidden, wh[:, base : base + gate4])
            in_gate = sigmoid(pre[:, :BLK])
            forget = sigmoid(pre[:, BLK : 2 * BLK])
            cand = jnp.tanh(pre[:, 2 * BLK : 3 * BLK])
            out_gate = sigmoid(pre[:, 3 * BLK :])
            prev = c[t, :, cols]
            new = 3.0 * jnp.tanh((forget * prev + in_gate * cand) * THIRD)
            m[slot, :, cols] = (out_gate * jnp.tanh(new)).astype(BF)
            z[t, :, base : base + BLK] = in_gate
            z[t, :, base + BLK : base + 2 * BLK] = forget
            z[t, :, base + 2 * BLK : base + 3 * BLK] = cand
            z[t, :, base + 3 * BLK : base + gate4] = out_gate
            c[t + 1, :, cols] = jnp.where(live, new, prev)
        two = lax.rem(t, 2)
        snd[two] = mm_pad(m[slot], wp[...]).astype(BF)
        copy = exchange(t)
        copy.start()
        begin(xh_pair(t))
        begin(m_pair(t))

        @pl.when(t + 1 < steps)
        def _():
            xh[t + 1, :, :width] = pick(x_flat, t + 1)
            input_part(t + 1)

        at = pl.multiple_of(t * turn_cols, turn_cols)
        for kb in range(width // BLK):
            for cb in range(turn_cols // BLK):
                wht[pl.ds(at + cb * BLK, BLK), kb * BLK : (kb + 1) * BLK] = mm_nt(
                    eye, wh[kb * BLK : (kb + 1) * BLK, pl.ds(at + cb * BLK, BLK)]
                ).astype(BF)
        at = pl.multiple_of(t * turn_units, turn_units)
        for kb in range(width // BLK):
            wpt[kb * BLK : (kb + 1) * BLK, pl.ds(at, turn_units)] = mm_nt(
                eye, wp[pl.ds(at, turn_units), kb * BLK : (kb + 1) * BLK]
            ).astype(BF)
        copy.wait()
        total = snd[two].astype(F32) + rcv[two].astype(F32)
        squash = jnp.tanh(total * THIRD)
        th[t] = squash
        new_hidden = (3.0 * squash).astype(BF).astype(F32)
        live_h = live_of(t, width)
        lay_ref[place(t)] = (xh[t, :, :width].astype(F32) + live_h * new_hidden).astype(BF)
        after = jnp.where(live_h > 0.5, new_hidden, hidden.astype(F32))

        @pl.when(t + 1 < steps)
        def _():
            xh[t + 1, :, hid] = after.astype(BF)

        @pl.when(t + 1 == steps)
        def _():
            hfin_ref[...] = after

        return carry

    lax.fori_loop(0, steps, forward, 0)
    cfin_ref[...] = c[steps]
    dc[...] = jnp.zeros_like(dc)
    dh[...] = jnp.zeros_like(dh)
    y_now[0] = pick(y_flat, steps - 1)

    def backward(k, carry):
        t = steps - 1 - k
        slot = lax.rem(t, RING)
        two = lax.rem(k, 2)

        @pl.when(k >= RING)
        def _():
            sent(dz_pair(t + RING))

        grad_hidden = dh[...]
        live_h = live_of(t, width)
        squash = th[t]
        y_low = y_now[two].astype(F32)
        low = (live_h * (y_low + grad_hidden) * (1.0 - squash * squash)).astype(BF)
        dr[t] = low
        live = live_of(t, BLK)
        grads_m = mm_pad(low, wpt[...]).astype(BF).astype(F32)
        for j in range(tiles):
            cols = slice(j * BLK, (j + 1) * BLK)
            base = j * gate4
            grad_m = grads_m[:, cols]
            in_gate = z[t, :, base : base + BLK]
            forget = z[t, :, base + BLK : base + 2 * BLK]
            cand = z[t, :, base + 2 * BLK : base + 3 * BLK]
            out_gate = z[t, :, base + 3 * BLK : base + gate4]
            prev = c[t, :, cols]
            new = c[t + 1, :, cols]
            grad_c = dc[:, cols]
            tanh_new = jnp.tanh(new)
            grad_n = live * grad_c + grad_m * out_gate * (1.0 - tanh_new * tanh_new)
            third = new * THIRD
            grad_u = grad_n * (1.0 - third * third)
            dz[slot, :, base : base + BLK] = (grad_u * cand * in_gate * (1.0 - in_gate)).astype(BF)
            dz[slot, :, base + BLK : base + 2 * BLK] = (
                grad_u * prev * forget * (1.0 - forget)
            ).astype(BF)
            dz[slot, :, base + 2 * BLK : base + 3 * BLK] = (
                grad_u * in_gate * (1.0 - cand * cand)
            ).astype(BF)
            dz[slot, :, base + 3 * BLK : base + gate4] = (
                grad_m * tanh_new * out_gate * (1.0 - out_gate)
            ).astype(BF)
            dc[:, cols] = (1.0 - live) * grad_c + grad_u * forget
        part = mm_pad(dz[slot], wht[...])
        snd[two] = part.astype(BF)
        copy = exchange(k)
        copy.start()
        begin(dz_pair(t))
        begin(dr_pair(t))

        @pl.when(k + 1 < steps)
        def _():
            y_now[1 - two] = pick(y_flat, t - 1)

        grad_x = y_low * jnp.where(unit == 0, 1.0, 0.0)
        for j in range(tiles):
            base = j * gate4
            grad_x = grad_x + mm_nt(dz[slot, :, base : base + gate4], wx[:, base : base + gate4])
        dx_ref[place(t)] = grad_x.astype(BF)
        copy.wait()
        dh[...] = (1.0 - live_h) * grad_hidden + (snd[two].astype(F32) + rcv[two].astype(F32))
        return carry

    lax.fori_loop(0, steps, backward, 0)

    def last(i, carry):
        sent(m_pair(steps - RING + i))
        sent(dz_pair(i))
        return carry

    lax.fori_loop(0, RING, last, 0)

    xh_all = whole(0, xh, xhg.at[mine])
    dr_all = whole(1, dr, drg.at[mine])
    sent(xh_all)
    sent(dr_all)
    xh_all[0].wait_recv()
    dr_all[0].wait_recv()
    remote(mg.at[mine], mg.at[mine], ring_send.at[0, 0], y_recv.at[2]).wait_recv()
    part = dzg.at[mine, :, :, pl.ds(0, early)]
    remote(part, part, ring_send.at[1, 0], y_recv.at[3]).wait_recv()


def recurrence(inputs, out_grad, win, last, hidden0, cell0, bias, w_in, w_hid, proj):
    streams, steps, width = inputs.shape
    units = proj.shape[0]
    vmem = pl.BlockSpec(memory_space=pltpu.VMEM)
    hbm = pl.BlockSpec(memory_space=pl.ANY)
    shape = jax.ShapeDtypeStruct
    return pl.pallas_call(
        recurrence_kernel,
        out_shape=(
            shape((steps, streams, width), BF),
            shape((streams, width), F32),
            shape((streams, units), F32),
            shape((steps, streams, width), BF),
            shape((2, steps, streams, 2 * units), BF),
            shape((steps, streams, LATE * BLK), BF),
            shape((2, steps, streams, 2 * width), BF),
            shape((2, steps, streams, units // 2), BF),
            shape((2, steps, streams, width), BF),
        ),
        in_specs=[hbm] * 2 + [vmem] * 5 + [hbm] * 3,
        out_specs=(vmem, vmem, vmem, vmem, hbm, hbm, hbm, hbm, hbm),
        scratch_shapes=[
            pltpu.VMEM((2, width, 4 * units), BF),
            pltpu.VMEM((4 * units, width), BF),
            pltpu.VMEM((units, width), BF),
            pltpu.VMEM((width, units), BF),
            pltpu.VMEM((4, BLK, units // 2), BF),
            pltpu.VMEM((steps, streams, 4 * units), F32),
            pltpu.VMEM((steps + 1, streams, units), F32),
            pltpu.VMEM((steps, streams, width), F32),
            pltpu.VMEM((streams * steps, width), BF),
            pltpu.VMEM((streams * steps, width), BF),
            pltpu.VMEM((steps, streams, 2 * width), BF),
            pltpu.VMEM((2, streams, width), BF),
            pltpu.VMEM((RING, streams, units), BF),
            pltpu.VMEM((steps, streams, width), BF),
            pltpu.VMEM((RING, streams, 4 * units), BF),
            pltpu.VMEM((streams, units), F32),
            pltpu.VMEM((streams, width), F32),
            pltpu.VMEM((streams, 128), F32),
            pltpu.VMEM((2, streams, width), BF),
            pltpu.VMEM((2, streams, width), BF),
            pltpu.SemaphoreType.DMA((4,)),
            pltpu.SemaphoreType.DMA((3,)),
            pltpu.SemaphoreType.DMA((2,)),
            pltpu.SemaphoreType.DMA((2,)),
            pltpu.SemaphoreType.DMA((4,)),
            pltpu.SemaphoreType.DMA((2,)),
            pltpu.SemaphoreType.DMA((2,)),
            pltpu.SemaphoreType.DMA((2, RING)),
            pltpu.SemaphoreType.DMA((2, RING)),
            pltpu.SemaphoreType.DMA((RING,)),
        ],
        compiler_params=pltpu.CompilerParams(
            collective_id=0, has_side_effects=True, vmem_limit_bytes=VMEM_LIMIT
        ),
        name="recurrence",
    )(inputs, out_grad, win, last, hidden0, cell0, bias, w_in, w_hid, proj)


def gradient_kernel(
    lanes,
    dz_hbm,
    late_hbm,
    xh_hbm,
    m_hbm,
    dr_hbm,
    dx_ref,
    res,
    bres,
    ig_ref,
    dz,
    xh,
    xht,
    m,
    mt,
    dr,
    acc,
    bsum,
    own,
    from_left,
    from_right,
    bown,
    bleft,
    bright,
    rx,
    red,
    load_sem,
    dz_sem,
    late_sem,
    l_recv,
    r_recv,
    out_sem,
    b_sem,
    g_send,
    g_recv,
):
    rows, cols = dz.shape
    depth = xh.shape[1]
    row_blocks = depth // CUT
    col_blocks = cols // BLK
    n_cat = row_blocks * col_blocks
    proj_cols = dr.shape[1] // BLK
    n_all = n_cat + (m.shape[1] // CUT) * proj_cols
    flip = lax.axis_index("dir")
    batch = lax.axis_index("batch")
    unit = lax.axis_index("unit")
    mine = lax.rem(batch, 2)
    lane = lax.div(batch, 2)
    mid = lanes // 2
    y_dev = {"batch": batch + 1 - 2 * mine}
    l_dev = {"batch": batch - 2}
    r_dev = {"batch": batch + 2}
    has_left = lane > 0
    has_right = lane < lanes - 1
    before = lane < mid
    after = lane > mid
    middle = lane == mid

    def group(o):
        return {
            "dir": flip + (o % 2) * (1 - 2 * flip),
            "unit": unit + (o // 2) * (1 - 2 * unit),
        }

    barrier = pltpu.get_barrier_semaphore()
    pl.semaphore_signal(barrier, 1, device_id=y_dev, device_id_type=MESH)
    for o in (1, 2, 3):
        pl.semaphore_signal(barrier, 1, device_id=group(o), device_id_type=MESH)

    @pl.when(has_left)
    def _():
        pl.semaphore_signal(barrier, 1, device_id=l_dev, device_id_type=MESH)

    @pl.when(has_right)
    def _():
        pl.semaphore_signal(barrier, 1, device_id=r_dev, device_id_type=MESH)

    xh_load = pltpu.make_async_copy(xh_hbm, xh, load_sem.at[0])
    m_load = pltpu.make_async_copy(m_hbm, m, load_sem.at[1])
    dr_load = pltpu.make_async_copy(dr_hbm, dr, load_sem.at[2])

    half_rows = rows // 2
    my_rows = pl.ds(pl.multiple_of(mine * half_rows, half_rows), half_rows)
    first_late = col_blocks - LATE
    late_cols = pl.ds(first_late * BLK, LATE * BLK)

    def dz_load(b):
        at = pl.ds(pl.multiple_of(b * BLK, BLK), BLK)
        return pltpu.make_async_copy(dz_hbm.at[:, at], dz.at[:, at], dz_sem.at[b])

    late_own = pltpu.make_async_copy(
        dz_hbm.at[my_rows, late_cols], dz.at[my_rows, late_cols], late_sem.at[0]
    )
    late_far = pltpu.make_async_remote_copy(
        late_hbm,
        dz.at[my_rows, late_cols],
        late_sem.at[1],
        late_sem.at[2],
        device_id=y_dev,
        device_id_type=MESH,
    )

    xh_load.start()

    def load_all(b, carry):
        dz_load(b).start()
        return carry

    lax.fori_loop(0, first_late, load_all, 0)
    late_own.start()
    m_load.start()
    dr_load.start()

    eye = identity()

    def turn(src, dst, a):
        at = pl.ds(pl.multiple_of(a * BLK, BLK), BLK)
        for b in range(rows // BLK):
            dst[at, b * BLK : (b + 1) * BLK] = mm_nt(
                eye, src[b * BLK : (b + 1) * BLK, at]
            ).astype(BF)

    quarter = dx_ref.shape[0] // 4
    me = flip + 2 * unit

    def member(o):
        p = group(o)
        return p["dir"] + 2 * p["unit"]

    def share(o):
        return pltpu.make_async_remote_copy(
            dx_ref.at[pl.ds(member(o) * quarter, quarter)],
            rx.at[o - 1],
            g_send.at[0, o - 1],
            g_recv.at[0, o - 1],
            device_id=group(o),
            device_id_type=MESH,
        )

    def hand_out(o):
        return pltpu.make_async_remote_copy(
            red,
            ig_ref.at[pl.ds(me * quarter, quarter)],
            g_send.at[1, o - 1],
            g_recv.at[1, o - 1],
            device_id=group(o),
            device_id_type=MESH,
        )

    bsum[...] = jnp.zeros_like(bsum)
    xh_load.wait()
    turn(xh, xht, 0)
    peers = 4 + jnp.where(has_left, 1, 0) + jnp.where(has_right, 1, 0)
    pl.semaphore_wait(barrier, peers)
    late_far.start()

    def remote(src, dst, send, recv, device):
        return pltpu.make_async_remote_copy(
            src, dst, send, recv, device_id=device, device_id_type=MESH
        )

    class Chunk:
        def __init__(self, refs, sems):
            self.own, self.left, self.right, self.res = refs
            self.l_recv, self.r_recv, self.l_send, self.r_send = sems[:4]
            self.y_send, self.y_recv, self.kept = sems[4:]

        def to_left(self, src):
            return remote(src, self.right, self.l_send, self.r_recv, l_dev)

        def to_right(self, src):
            return remote(src, self.left, self.r_send, self.l_recv, r_dev)

        def left_in(self):
            return remote(self.own, self.left, self.r_send, self.l_recv, l_dev)

        def right_in(self):
            return remote(self.own, self.right, self.l_send, self.r_recv, r_dev)

        def to_y(self, src):
            return remote(src, self.res, self.y_send, self.y_recv, y_dev)

        def keep(self, src):
            return pltpu.make_async_copy(src, self.res, self.kept)

        def reduce(self, value):
            @pl.when(before)
            def _():
                @pl.when(has_left)
                def _():
                    self.left_in().wait_recv()
                    self.own[...] = (value() + self.left[...].astype(F32)).astype(BF)

                @pl.when(jnp.logical_not(has_left))
                def _():
                    self.own[...] = value().astype(BF)

                self.to_right(self.own).start()

            @pl.when(after)
            def _():
                @pl.when(has_right)
                def _():
                    self.right_in().wait_recv()
                    self.own[...] = (value() + self.right[...].astype(F32)).astype(BF)

                @pl.when(jnp.logical_not(has_right))
                def _():
                    self.own[...] = value().astype(BF)

                self.to_left(self.own).start()

            @pl.when(middle)
            def _():
                total = value()
                if mid > 0:
                    self.left_in().wait_recv()
                    total = total + self.left[...].astype(F32)
                if mid < lanes - 1:
                    self.right_in().wait_recv()
                    total = total + self.right[...].astype(F32)
                self.own[...] = total.astype(BF)
                if mid > 0:
                    self.to_left(self.own).start()
                if mid < lanes - 1:
                    self.to_right(self.own).start()
                self.to_y(self.own).start()
                self.keep(self.own).start()

        def publish(self):
            @pl.when(before)
            def _():
                self.right_in().wait_recv()

                @pl.when(has_left)
                def _():
                    self.to_left(self.right).start()

                self.to_y(self.right).start()
                self.keep(self.right).start()

            @pl.when(after)
            def _():
                self.left_in().wait_recv()

                @pl.when(has_right)
                def _():
                    self.to_right(self.left).start()

                self.to_y(self.left).start()
                self.keep(self.left).start()

        def finish(self):
            self.to_y(self.own).wait()

            @pl.when(has_left)
            def _():
                self.to_left(self.own).wait_send()

            @pl.when(has_right)
            def _():
                self.to_right(self.own).wait_send()

            self.keep(self.own).wait()

    leaving = [out_sem.at[i] for i in range(5)]

    def chunk(k):
        slot = lax.rem(k, RECV_RING)
        refs = (own.at[k], from_left.at[k], from_right.at[k], res.at[mine, k])
        return Chunk(refs, [l_recv.at[slot], r_recv.at[slot], *leaving])

    every = Chunk((own, from_left, from_right, res.at[mine]), [l_recv.at[0], r_recv.at[0], *leaving])
    bias = Chunk((bown, bleft, bright, bres.at[mine]), [b_sem.at[i] for i in range(7)])
    ones = jnp.ones((16, rows), BF)
    which = lax.broadcasted_iota(jnp.int32, (16, BLK), 0)
    far = jnp.where(before, mid - lane, lane - mid)
    inner = jnp.logical_and(has_left, has_right)
    lag = 5 * far + jnp.where(inner, 0, 12)
    longest = 5 * max(mid, lanes - 1 - mid) + 12
    turns = depth // BLK

    def body(k, carry):
        @pl.when(jnp.logical_and(k > 0, k < turns))
        def _():
            turn(xh, xht, k)

        @pl.when(k == row_blocks)
        def _():
            m_load.wait()
            dr_load.wait()
            for o in (1, 2, 3):
                share(o).start()

        @pl.when(jnp.logical_and(k >= row_blocks, k < row_blocks + m.shape[1] // BLK))
        def _():
            turn(m, mt, k - row_blocks)

        @pl.when(k < n_all)
        def _():
            @pl.when(k < n_cat)
            def _():
                b = lax.div(k, row_blocks)
                r = pl.multiple_of(lax.rem(k, row_blocks) * CUT, CUT)
                at = pl.ds(pl.multiple_of(b * BLK, BLK), BLK)

                @pl.when(jnp.logical_and(r == 0, b < first_late))
                def _():
                    dz_load(b).wait()

                @pl.when(jnp.logical_and(r == 0, b == first_late))
                def _():
                    late_own.wait()
                    late_far.wait_recv()

                @pl.when(r == 0)
                def _():
                    bsum[...] += jnp.where(which == b, mm(ones, dz[:, at]), 0.0)

                acc[...] = mm(xht[pl.ds(r, CUT), :], dz[:, at])

            @pl.when(k >= n_cat)
            def _():
                n = k - n_cat
                r = pl.multiple_of(lax.div(n, proj_cols) * CUT, CUT)
                b = pl.multiple_of(lax.rem(n, proj_cols) * BLK, BLK)
                acc[...] = mm(mt[pl.ds(r, CUT), :], dr[:, pl.ds(b, BLK)])

            chunk(k).reduce(lambda: acc[...])

            @pl.when(k == n_cat)
            def _():
                bias.reduce(lambda: bsum[...])

        @pl.when(k == 4 * row_blocks)
        def _():
            sums = dx_ref[pl.ds(me * quarter, quarter)].astype(F32)
            for o in (1, 2, 3):
                share(o).wait_recv()
                sums = sums + rx[o - 1].astype(F32)
            red[...] = sums.astype(BF)
            ig_ref[pl.ds(me * quarter, quarter)] = red[...]
            for o in (1, 2, 3):
                hand_out(o).start()

        n = k - lag

        @pl.when(jnp.logical_and(n >= 0, n < n_all))
        def _():
            chunk(n).publish()

            @pl.when(n == n_cat)
            def _():
                bias.publish()

        return carry

    lax.fori_loop(0, n_all + longest, body, 0)
    every.finish()
    late_far.wait_send()
    bias.finish()
    for o in (1, 2, 3):
        share(o).wait_send()
        hand_out(o).wait()


def gradients(lanes, dzg, late, xhg, mg, drg, dx):
    rows, cols = dzg.shape
    depth = xhg.shape[1]
    n_all = (depth // CUT) * (cols // BLK) + (mg.shape[1] // CUT) * (drg.shape[1] // BLK)
    steps, streams, width = dx.shape
    vmem = pl.BlockSpec(memory_space=pltpu.VMEM)
    hbm = pl.BlockSpec(memory_space=pl.ANY)
    shape = jax.ShapeDtypeStruct
    return pl.pallas_call(
        functools.partial(gradient_kernel, lanes),
        out_shape=(
            shape((2, n_all, CUT, BLK), BF),
            shape((2, 16, BLK), BF),
            shape((steps, streams, width), BF),
        ),
        in_specs=[hbm] * 5 + [vmem],
        out_specs=(hbm, hbm, vmem),
        scratch_shapes=[
            pltpu.VMEM((rows, cols), BF),
            pltpu.VMEM((rows, depth), BF),
            pltpu.VMEM((depth, rows), BF),
            pltpu.VMEM(mg.shape, BF),
            pltpu.VMEM((mg.shape[1], rows), BF),
            pltpu.VMEM(drg.shape, BF),
            pltpu.VMEM((CUT, BLK), F32),
            pltpu.VMEM((16, BLK), F32),
            pltpu.VMEM((n_all, CUT, BLK), BF),
            pltpu.VMEM((n_all, CUT, BLK), BF),
            pltpu.VMEM((n_all, CUT, BLK), BF),
            pltpu.VMEM((16, BLK), BF),
            pltpu.VMEM((16, BLK), BF),
            pltpu.VMEM((16, BLK), BF),
            pltpu.VMEM((3, steps // 4, streams, width), BF),
            pltpu.VMEM((steps // 4, streams, width), BF),
            pltpu.SemaphoreType.DMA((3,)),
            pltpu.SemaphoreType.DMA((cols // BLK,)),
            pltpu.SemaphoreType.DMA((3,)),
            pltpu.SemaphoreType.DMA((RECV_RING,)),
            pltpu.SemaphoreType.DMA((RECV_RING,)),
            pltpu.SemaphoreType.DMA((5,)),
            pltpu.SemaphoreType.DMA((7,)),
            pltpu.SemaphoreType.DMA((2, 3)),
            pltpu.SemaphoreType.DMA((2, 3)),
        ],
        compiler_params=pltpu.CompilerParams(
            collective_id=1, has_side_effects=True, vmem_limit_bytes=VMEM_LIMIT
        ),
        name="gradients",
    )(dzg, late, xhg, mg, drg, dx)


def widen_kernel(
    n_cat,
    res,
    bres,
    lay_in,
    ig_in,
    hfin_in,
    cfin_in,
    lay_out,
    ig_out,
    wx_out,
    wh_out,
    b_out,
    wp_out,
    hfin_out,
    cfin_out,
    low,
    wide,
    lay_buf,
    ig_buf,
    p_low,
    in_sem,
    out_sem,
    p_sem,
    s_sem,
    ig_sem,
):
    width, _, units = wx_out.shape
    steps, streams, _ = lay_in.shape
    slots = low.shape[0]
    row_blocks = low.shape[1]
    half = row_blocks // 2
    col_blocks = n_cat // row_blocks
    count = 2 * col_blocks
    n_proj = p_low.shape[1]
    proj_cols = width // BLK

    def fetch(k):
        slot = lax.rem(k, slots)
        return pltpu.make_async_copy(
            res.at[lax.div(k, col_blocks), pl.ds(lax.rem(k, col_blocks) * row_blocks, row_blocks)],
            low.at[slot],
            in_sem.at[slot],
        )

    def store(k):
        slot = lax.rem(k, slots)
        owner = lax.div(k, col_blocks)
        b = lax.rem(k, col_blocks)
        gate = lax.rem(b, 4)
        u = pl.multiple_of(owner * (units // 2) + lax.div(b, 4) * BLK, BLK)
        return [
            pltpu.make_async_copy(
                wide.at[slot, i],
                out.at[:, gate, pl.ds(u, BLK)],
                out_sem.at[slot, i],
            )
            for i, out in enumerate((wx_out, wh_out))
        ]

    for k in range(slots - 1):
        fetch(k).start()
    proj = [
        pltpu.make_async_copy(res.at[o, pl.ds(n_cat, n_proj)], p_low.at[o], p_sem.at[o])
        for o in range(2)
    ]
    states = [
        pltpu.make_async_copy(hfin_in, hfin_out, s_sem.at[0]),
        pltpu.make_async_copy(cfin_in, cfin_out, s_sem.at[1]),
    ]
    for one in proj + states:
        one.start()

    def body(k, carry):
        slot = lax.rem(k, slots)

        @pl.when(k >= slots)
        def _():
            for one in store(k - slots):
                one.wait()

        fetch(k).wait()
        for r in range(row_blocks):
            wide[slot, r // half, (r % half) * CUT : (r % half + 1) * CUT, :] = low[slot, r].astype(F32)
        for one in store(k):
            one.start()

        @pl.when(k + slots - 1 < count)
        def _():
            fetch(k + slots - 1).start()

        return carry

    lax.fori_loop(0, slots, body, 0)

    t = lax.broadcasted_iota(jnp.int32, (steps, streams * steps), 0)
    r = lax.broadcasted_iota(jnp.int32, (steps, streams * steps), 1)
    flat = lay_in[...].reshape(streams * steps, width)
    bunch = BLK // steps
    for b in range(streams // bunch):
        want = jnp.concatenate(
            [jnp.where(r == t * streams + b * bunch + s, 1.0, 0.0) for s in range(bunch)], 0
        ).astype(BF)
        lay_buf[b * BLK : (b + 1) * BLK, :] = mm(want, flat).astype(BF)
    lay_copy = pltpu.make_async_copy(lay_buf, lay_out.reshape(streams * steps, width), s_sem.at[2])
    lay_copy.start()
    ig_copies = []
    for step in range(steps):
        ig_buf[step] = ig_in[step].astype(F32)
        ig_copies.append(
            pltpu.make_async_copy(ig_buf.at[step], ig_out.at[:, step, :], ig_sem.at[step])
        )
        ig_copies[-1].start()
    for owner in range(2):
        proj[owner].wait()
        for n in range(n_proj):
            row = owner * (units // 2) + (n // proj_cols) * CUT
            col = (n % proj_cols) * BLK
            wp_out[row : row + CUT, col : col + BLK] = p_low[owner, n].astype(F32)
        for b in range(col_blocks):
            u = owner * (units // 2) + (b // 4) * BLK
            b_out[b % 4 : b % 4 + 1, u : u + BLK] = bres[owner, b : b + 1, :].astype(F32)

    lax.fori_loop(slots, count, body, 0)
    for k in range(count - slots, count):
        for one in store(k):
            one.wait()
    for one in [*states, lay_copy, *ig_copies]:
        one.wait()


def widen(res, bres, lay, ig, hfin, cfin):
    steps, streams, width = lay.shape
    units = cfin.shape[1]
    row_blocks = 2 * width // CUT
    n_cat = row_blocks * (2 * units // BLK)
    n_proj = res.shape[1] - n_cat
    slots = 4
    vmem = pl.BlockSpec(memory_space=pltpu.VMEM)
    hbm = pl.BlockSpec(memory_space=pl.ANY)
    shape = jax.ShapeDtypeStruct
    return pl.pallas_call(
        functools.partial(widen_kernel, n_cat),
        out_shape=(
            shape((streams, steps, width), BF),
            shape((streams, steps, width), F32),
            shape((width, 4, units), F32),
            shape((width, 4, units), F32),
            shape((4, units), F32),
            shape((units, width), F32),
            shape((streams, width), F32),
            shape((streams, units), F32),
        ),
        in_specs=[hbm, vmem, vmem, vmem, hbm, hbm],
        out_specs=(hbm, hbm, hbm, hbm, vmem, vmem, hbm, hbm),
        scratch_shapes=[
            pltpu.VMEM((slots, row_blocks, CUT, BLK), BF),
            pltpu.VMEM((slots, 2, width, BLK), F32),
            pltpu.VMEM((streams * steps, width), BF),
            pltpu.VMEM((steps, streams, width), F32),
            pltpu.VMEM((2, n_proj, CUT, BLK), BF),
            pltpu.SemaphoreType.DMA((slots,)),
            pltpu.SemaphoreType.DMA((slots, 2)),
            pltpu.SemaphoreType.DMA((2,)),
            pltpu.SemaphoreType.DMA((3,)),
            pltpu.SemaphoreType.DMA((steps,)),
        ],
        compiler_params=pltpu.CompilerParams(vmem_limit_bytes=VMEM_LIMIT),
        name="widen",
    )(res, bres, lay, ig, hfin, cfin)


def on_device(
    inputs,
    win_count,
    last_live,
    hidden_init,
    cell_init,
    w_input,
    w_hidden,
    gate_bias,
    w_proj,
    out_grad,
):
    streams, steps, width = inputs.shape
    units = w_proj.shape[1]
    lanes = lax.axis_size("batch") // 2
    lay, hfin, cfin, dx, dzg, late, xhg, mg, drg = recurrence(
        inputs,
        out_grad[0],
        win_count.reshape(1, streams),
        last_live.reshape(1, streams),
        hidden_init[0],
        cell_init[0],
        gate_bias[0],
        w_input[0],
        w_hidden[0],
        w_proj[0],
    )
    rows = 2 * steps * streams
    res, bres, ig = gradients(
        lanes,
        dzg.reshape(rows, 2 * units),
        late.reshape(steps * streams, LATE * BLK),
        xhg.reshape(rows, 2 * width),
        mg.reshape(rows, units // 2),
        drg.reshape(rows, width),
        dx,
    )
    out = widen(res, bres, lay, ig, hfin, cfin)
    layer_out, input_grad, wx_grad, wh_grad, b_grad, wp_grad, hidden_final, cell_final = out
    return (
        layer_out[None],
        input_grad,
        wx_grad[None],
        wh_grad[None],
        b_grad[None],
        wp_grad[None],
        hidden_final[None],
        cell_final[None],
    )


def solution(mesh):
    placed = (
        P("batch", None, None),
        P("batch"),
        P("batch"),
        P("dir", "batch", None),
        P("dir", "batch", "unit"),
        P("dir", None, None, "unit"),
        P("dir", None, None, "unit"),
        P("dir", None, "unit"),
        P("dir", "unit", None),
        P("dir", "batch", None, None),
    )
    return jax.shard_map(
        on_device,
        mesh=mesh,
        in_specs=placed,
        out_specs=(
            P("dir", "batch", None, None),
            P("batch", None, None),
            P("dir", None, None, "unit"),
            P("dir", None, None, "unit"),
            P("dir", None, "unit"),
            P("dir", "unit", None),
            P("dir", "batch", None),
            P("dir", "batch", "unit"),
        ),
        check_vma=False,
    )
```

```python
import functools

import jax
import jax.numpy as jnp
from jax import lax
from jax.experimental import pallas as pl
from jax.experimental.pallas import tpu as pltpu
from jax.sharding import PartitionSpec as P

WIN = 8
BLK = 256
CUT = 128
RING = 4
LATE = 3
RECV_RING = 32
MESH = pl.DeviceIdType.MESH
BF = jnp.bfloat16
F32 = jnp.float32
NT = (((1,), (1,)), ((), ()))
VMEM_LIMIT = 60 * 1024 * 1024
THIRD = 1.0 / 3.0


def sigmoid(v):
    return 0.5 * jnp.tanh(0.5 * v) + 0.5


def mm(a, b):
    return jnp.dot(a, b, preferred_element_type=F32)


def mm_pad(a, b):
    fill = jnp.zeros((128 - a.shape[0], a.shape[1]), a.dtype)
    return mm(jnp.concatenate([a, fill], 0), b)[: a.shape[0]]


def mm_nt(a, b):
    return lax.dot_general(a, b, NT, preferred_element_type=F32)


def identity():
    rows = lax.broadcasted_iota(jnp.int32, (BLK, BLK), 0)
    cols = lax.broadcasted_iota(jnp.int32, (BLK, BLK), 1)
    return jnp.where(rows == cols, 1.0, 0.0).astype(BF)


def gate_order():
    rows = lax.broadcasted_iota(jnp.int32, (BLK, BLK), 0)
    cols = lax.broadcasted_iota(jnp.int32, (BLK, BLK), 1)
    want = (rows & (BLK // 4 - 1)) * 4 + (rows >> 6)
    return jnp.where(want == cols, 1.0, 0.0).astype(BF)


def recurrence_kernel(
    x_hbm,
    y_hbm,
    win_ref,
    last_ref,
    h0_ref,
    c0_ref,
    bias_ref,
    wx_hbm,
    wh_hbm,
    wp_hbm,
    lay_ref,
    hfin_ref,
    cfin_ref,
    dx_ref,
    dzg,
    late,
    xhg,
    mg,
    drg,
    w,
    wht,
    wp,
    wpt,
    z,
    c,
    th,
    x_flat,
    y_flat,
    xh,
    y_now,
    m,
    dr,
    dz,
    dc,
    dh,
    lens,
    snd,
    rcv,
    raw_sem,
    load_sem,
    ex_send,
    ex_recv,
    y_recv,
    whole_send,
    whole_keep,
    ring_send,
    ring_keep,
    late_keep,
):
    steps, streams, width = lay_ref.shape
    units = wp.shape[0]
    tiles = units // BLK
    gate4 = 4 * BLK
    half_cols = 2 * units
    half_units = units // 2
    flip = lax.axis_index("dir")
    batch = lax.axis_index("batch")
    unit = lax.axis_index("unit")
    mine = lax.rem(batch, 2)
    other = 1 - mine
    y_dev = {"batch": batch + 1 - 2 * mine}
    x_dev = {"unit": 1 - unit}
    hid = slice(width, 2 * width)

    def place(t):
        return t + flip * (steps - 1 - 2 * t)

    slots = wpt.shape[0] // BLK
    blocks = width * 4 // BLK

    def raw(slot):
        return wpt.at[pl.ds(pl.multiple_of(slot * BLK, BLK), BLK)]

    def fetch(b, w_hbm, slot):
        return pltpu.make_async_copy(
            w_hbm.reshape(width * 4, units).at[pl.ds(pl.multiple_of(b * BLK, BLK), BLK)],
            raw(slot),
            raw_sem.at[slot],
        )

    def fetch_any(n):
        slot = lax.rem(n, slots)

        @pl.when(n < blocks)
        def _():
            fetch(n, wx_hbm, slot).start()

        @pl.when(jnp.logical_and(n >= blocks, n < 2 * blocks))
        def _():
            fetch(n - blocks, wh_hbm, slot).start()

    for n in range(slots - 1):
        fetch(n, wx_hbm, n).start()
    x_copy = pltpu.make_async_copy(x_hbm.reshape(streams * steps, width), x_flat, load_sem.at[0])
    y_copy = pltpu.make_async_copy(y_hbm.reshape(streams * steps, width), y_flat, load_sem.at[1])
    proj_copy = pltpu.make_async_copy(wp_hbm, wp, load_sem.at[2])
    x_copy.start()
    proj_copy.start()
    y_copy.start()
    barrier = pltpu.get_barrier_semaphore()
    pl.semaphore_signal(barrier, 1, device_id=x_dev, device_id_type=MESH)
    pl.semaphore_signal(barrier, 1, device_id=y_dev, device_id_type=MESH)

    order = gate_order()

    def spread(n, carry):
        slot = lax.rem(n, slots)
        fetch_any(n + slots - 1)
        fetch(0, wx_hbm, slot).wait()
        which = lax.div(n, blocks)
        left = n - which * blocks
        row = pl.multiple_of(left * 64, 64)
        for j in range(tiles):
            got = mm(order, raw(slot)[:, j * BLK : (j + 1) * BLK]).astype(BF)
            for g in range(4):
                base = j * gate4 + g * BLK
                w[which, pl.ds(row, 64), base : base + BLK] = got[g * 64 : (g + 1) * 64]
        return carry

    lax.fori_loop(0, 2 * blocks, spread, 0)
    wx, wh = w.at[0], w.at[1]

    row_len = ((win_ref[...] - 1) * WIN + last_ref[...]).astype(F32)
    rows = lax.broadcasted_iota(jnp.int32, (streams, streams), 0)
    cols = lax.broadcasted_iota(jnp.int32, (streams, streams), 1)
    spot = jnp.where(rows == cols, jnp.broadcast_to(row_len, (streams, streams)), 0.0)
    lens[...] = jnp.broadcast_to(jnp.sum(spot, axis=1, keepdims=True), lens.shape)

    def live_of(t, count):
        live = jnp.where(lens[...] > place(t).astype(F32), 1.0, 0.0)
        return jnp.concatenate([live] * (count // 128), 1)

    def pick(flat, t):
        s = lax.broadcasted_iota(jnp.int32, (streams, streams * steps), 0)
        r = lax.broadcasted_iota(jnp.int32, (streams, streams * steps), 1)
        want = jnp.where(r == s * steps + place(t), 1.0, 0.0).astype(BF)
        return mm(want, flat[...]).astype(BF)

    def exchange(k):
        slot = lax.rem(k, 2)
        return pltpu.make_async_remote_copy(
            snd.at[slot],
            rcv.at[slot],
            ex_send.at[slot],
            ex_recv.at[slot],
            device_id=x_dev,
            device_id_type=MESH,
        )

    def remote(away, target, send, recv):
        return pltpu.make_async_remote_copy(
            away, target, send, recv, device_id=y_dev, device_id_type=MESH
        )

    def whole(kind, src, target):
        return (
            remote(src, target, whole_send.at[kind], y_recv.at[kind]),
            pltpu.make_async_copy(src, target, whole_keep.at[kind]),
        )

    def xh_pair(t):
        return whole(0, xh.at[t], xhg.at[mine, place(t)])

    def dr_pair(t):
        return whole(1, dr.at[t], drg.at[mine, place(t)])

    def m_pair(t):
        slot = lax.rem(t, RING)
        away = m.at[slot, :, pl.ds(pl.multiple_of(other * half_units, half_units), half_units)]
        keep = m.at[slot, :, pl.ds(pl.multiple_of(mine * half_units, half_units), half_units)]
        target = mg.at[mine, place(t)]
        return (
            remote(away, target, ring_send.at[0, slot], y_recv.at[2]),
            pltpu.make_async_copy(keep, target, ring_keep.at[0, slot]),
        )

    early = half_cols - LATE * BLK

    def dz_pair(t):
        slot = lax.rem(t, RING)
        first = pl.multiple_of(other * half_cols, half_cols)
        away = dz.at[slot, :, pl.ds(first, early)]
        rest = dz.at[slot, :, pl.ds(pl.multiple_of(first + early, BLK), LATE * BLK)]
        keep = dz.at[slot, :, pl.ds(pl.multiple_of(mine * half_cols, half_cols), half_cols)]
        return (
            remote(
                away,
                dzg.at[mine, place(t), :, pl.ds(0, early)],
                ring_send.at[1, slot],
                y_recv.at[3],
            ),
            pltpu.make_async_copy(keep, dzg.at[mine, place(t)], ring_keep.at[1, slot]),
            pltpu.make_async_copy(rest, late.at[place(t)], late_keep.at[slot]),
        )

    def begin(copies):
        for one in copies:
            one.start()

    def sent(copies):
        copies[0].wait_send()
        for one in copies[1:]:
            one.wait()

    def input_part(t):
        now = xh[t, :, :width]
        for j in range(tiles):
            part = mm(now, wx[:, j * gate4 : (j + 1) * gate4])
            for g in range(4):
                z[t, :, j * gate4 + g * BLK : j * gate4 + (g + 1) * BLK] = (
                    part[:, g * BLK : (g + 1) * BLK] + bias_ref[g : g + 1, j * BLK : (j + 1) * BLK]
                )

    eye = identity()
    x_copy.wait()
    xh[0, :, :width] = pick(x_flat, 0)
    xh[0, :, hid] = h0_ref[...].astype(BF)
    c[0] = c0_ref[...]
    input_part(0)
    proj_copy.wait()
    y_copy.wait()
    turn_cols = 4 * units // steps
    turn_units = units // steps
    pl.semaphore_wait(barrier, 2)

    def forward(t, carry):
        slot = lax.rem(t, RING)

        @pl.when(t >= RING)
        def _():
            sent(m_pair(t - RING))

        live = live_of(t, BLK) > 0.5
        hidden = xh[t, :, hid]
        for j in range(tiles):
            cols = slice(j * BLK, (j + 1) * BLK)
            base = j * gate4
            pre = z[t, :, base : base + gate4] + mm_pad(hidden, wh[:, base : base + gate4])
            in_gate = sigmoid(pre[:, :BLK])
            forget = sigmoid(pre[:, BLK : 2 * BLK])
            cand = jnp.tanh(pre[:, 2 * BLK : 3 * BLK])
            out_gate = sigmoid(pre[:, 3 * BLK :])
            prev = c[t, :, cols]
            new = 3.0 * jnp.tanh((forget * prev + in_gate * cand) * THIRD)
            m[slot, :, cols] = (out_gate * jnp.tanh(new)).astype(BF)
            z[t, :, base : base + BLK] = in_gate
            z[t, :, base + BLK : base + 2 * BLK] = forget
            z[t, :, base + 2 * BLK : base + 3 * BLK] = cand
            z[t, :, base + 3 * BLK : base + gate4] = out_gate
            c[t + 1, :, cols] = jnp.where(live, new, prev)
        two = lax.rem(t, 2)
        snd[two] = mm_pad(m[slot], wp[...]).astype(BF)
        copy = exchange(t)
        copy.start()
        begin(xh_pair(t))
        begin(m_pair(t))

        @pl.when(t + 1 < steps)
        def _():
            xh[t + 1, :, :width] = pick(x_flat, t + 1)
            input_part(t + 1)

        at = pl.multiple_of(t * turn_cols, turn_cols)
        for kb in range(width // BLK):
            for cb in range(turn_cols // BLK):
                wht[pl.ds(at + cb * BLK, BLK), kb * BLK : (kb + 1) * BLK] = mm_nt(
                    eye, wh[kb * BLK : (kb + 1) * BLK, pl.ds(at + cb * BLK, BLK)]
                ).astype(BF)
        at = pl.multiple_of(t * turn_units, turn_units)
        for kb in range(width // BLK):
            wpt[kb * BLK : (kb + 1) * BLK, pl.ds(at, turn_units)] = mm_nt(
                eye, wp[pl.ds(at, turn_units), kb * BLK : (kb + 1) * BLK]
            ).astype(BF)
        copy.wait()
        total = snd[two].astype(F32) + rcv[two].astype(F32)
        squash = jnp.tanh(total * THIRD)
        th[t] = squash
        new_hidden = (3.0 * squash).astype(BF).astype(F32)
        live_h = live_of(t, width)
        lay_ref[place(t)] = (xh[t, :, :width].astype(F32) + live_h * new_hidden).astype(BF)
        after = jnp.where(live_h > 0.5, new_hidden, hidden.astype(F32))

        @pl.when(t + 1 < steps)
        def _():
            xh[t + 1, :, hid] = after.astype(BF)

        @pl.when(t + 1 == steps)
        def _():
            hfin_ref[...] = after

        return carry

    lax.fori_loop(0, steps, forward, 0)
    cfin_ref[...] = c[steps]
    dc[...] = jnp.zeros_like(dc)
    dh[...] = jnp.zeros_like(dh)
    y_now[0] = pick(y_flat, steps - 1)

    def backward(k, carry):
        t = steps - 1 - k
        slot = lax.rem(t, RING)
        two = lax.rem(k, 2)

        @pl.when(k >= RING)
        def _():
            sent(dz_pair(t + RING))

        grad_hidden = dh[...]
        live_h = live_of(t, width)
        squash = th[t]
        y_low = y_now[two].astype(F32)
        low = (live_h * (y_low + grad_hidden) * (1.0 - squash * squash)).astype(BF)
        dr[t] = low
        live = live_of(t, BLK)
        grads_m = mm_pad(low, wpt[:width, :]).astype(BF).astype(F32)
        for j in range(tiles):
            cols = slice(j * BLK, (j + 1) * BLK)
            base = j * gate4
            grad_m = grads_m[:, cols]
            in_gate = z[t, :, base : base + BLK]
            forget = z[t, :, base + BLK : base + 2 * BLK]
            cand = z[t, :, base + 2 * BLK : base + 3 * BLK]
            out_gate = z[t, :, base + 3 * BLK : base + gate4]
            prev = c[t, :, cols]
            new = c[t + 1, :, cols]
            grad_c = dc[:, cols]
            tanh_new = jnp.tanh(new)
            grad_n = live * grad_c + grad_m * out_gate * (1.0 - tanh_new * tanh_new)
            third = new * THIRD
            grad_u = grad_n * (1.0 - third * third)
            dz[slot, :, base : base + BLK] = (grad_u * cand * in_gate * (1.0 - in_gate)).astype(BF)
            dz[slot, :, base + BLK : base + 2 * BLK] = (
                grad_u * prev * forget * (1.0 - forget)
            ).astype(BF)
            dz[slot, :, base + 2 * BLK : base + 3 * BLK] = (
                grad_u * in_gate * (1.0 - cand * cand)
            ).astype(BF)
            dz[slot, :, base + 3 * BLK : base + gate4] = (
                grad_m * tanh_new * out_gate * (1.0 - out_gate)
            ).astype(BF)
            dc[:, cols] = (1.0 - live) * grad_c + grad_u * forget
        part = mm_pad(dz[slot], wht[...])
        snd[two] = part.astype(BF)
        copy = exchange(k)
        copy.start()
        begin(dz_pair(t))
        begin(dr_pair(t))

        @pl.when(k + 1 < steps)
        def _():
            y_now[1 - two] = pick(y_flat, t - 1)

        grad_x = y_low * jnp.where(unit == 0, 1.0, 0.0)
        for j in range(tiles):
            base = j * gate4
            grad_x = grad_x + mm_nt(dz[slot, :, base : base + gate4], wx[:, base : base + gate4])
        dx_ref[place(t)] = grad_x.astype(BF)
        copy.wait()
        dh[...] = (1.0 - live_h) * grad_hidden + (snd[two].astype(F32) + rcv[two].astype(F32))
        return carry

    lax.fori_loop(0, steps, backward, 0)

    def last(i, carry):
        sent(m_pair(steps - RING + i))
        sent(dz_pair(i))
        return carry

    lax.fori_loop(0, RING, last, 0)

    xh_all = whole(0, xh, xhg.at[mine])
    dr_all = whole(1, dr, drg.at[mine])
    sent(xh_all)
    sent(dr_all)
    xh_all[0].wait_recv()
    dr_all[0].wait_recv()
    remote(mg.at[mine], mg.at[mine], ring_send.at[0, 0], y_recv.at[2]).wait_recv()
    part = dzg.at[mine, :, :, pl.ds(0, early)]
    remote(part, part, ring_send.at[1, 0], y_recv.at[3]).wait_recv()


def recurrence(inputs, out_grad, win, last, hidden0, cell0, bias, w_in, w_hid, proj):
    streams, steps, width = inputs.shape
    units = proj.shape[0]
    vmem = pl.BlockSpec(memory_space=pltpu.VMEM)
    hbm = pl.BlockSpec(memory_space=pl.ANY)
    shape = jax.ShapeDtypeStruct
    return pl.pallas_call(
        recurrence_kernel,
        out_shape=(
            shape((steps, streams, width), BF),
            shape((streams, width), F32),
            shape((streams, units), F32),
            shape((steps, streams, width), BF),
            shape((2, steps, streams, 2 * units), BF),
            shape((steps, streams, LATE * BLK), BF),
            shape((2, steps, streams, 2 * width), BF),
            shape((2, steps, streams, units // 2), BF),
            shape((2, steps, streams, width), BF),
        ),
        in_specs=[hbm] * 2 + [vmem] * 5 + [hbm] * 3,
        out_specs=(vmem, vmem, vmem, vmem, hbm, hbm, hbm, hbm, hbm),
        scratch_shapes=[
            pltpu.VMEM((2, width, 4 * units), BF),
            pltpu.VMEM((4 * units, width), BF),
            pltpu.VMEM((units, width), BF),
            pltpu.VMEM((max(width, 4 * BLK), units), BF),
            pltpu.VMEM((steps, streams, 4 * units), F32),
            pltpu.VMEM((steps + 1, streams, units), F32),
            pltpu.VMEM((steps, streams, width), F32),
            pltpu.VMEM((streams * steps, width), BF),
            pltpu.VMEM((streams * steps, width), BF),
            pltpu.VMEM((steps, streams, 2 * width), BF),
            pltpu.VMEM((2, streams, width), BF),
            pltpu.VMEM((RING, streams, units), BF),
            pltpu.VMEM((steps, streams, width), BF),
            pltpu.VMEM((RING, streams, 4 * units), BF),
            pltpu.VMEM((streams, units), F32),
            pltpu.VMEM((streams, width), F32),
            pltpu.VMEM((streams, 128), F32),
            pltpu.VMEM((2, streams, width), BF),
            pltpu.VMEM((2, streams, width), BF),
            pltpu.SemaphoreType.DMA((4,)),
            pltpu.SemaphoreType.DMA((3,)),
            pltpu.SemaphoreType.DMA((2,)),
            pltpu.SemaphoreType.DMA((2,)),
            pltpu.SemaphoreType.DMA((4,)),
            pltpu.SemaphoreType.DMA((2,)),
            pltpu.SemaphoreType.DMA((2,)),
            pltpu.SemaphoreType.DMA((2, RING)),
            pltpu.SemaphoreType.DMA((2, RING)),
            pltpu.SemaphoreType.DMA((RING,)),
        ],
        compiler_params=pltpu.CompilerParams(
            collective_id=0, has_side_effects=True, vmem_limit_bytes=VMEM_LIMIT
        ),
        name="recurrence",
    )(inputs, out_grad, win, last, hidden0, cell0, bias, w_in, w_hid, proj)


def gradient_kernel(
    lanes,
    dz_hbm,
    late_hbm,
    xh_hbm,
    m_hbm,
    dr_hbm,
    dx_ref,
    res,
    bres,
    ig_ref,
    dz,
    xh,
    xht,
    m,
    mt,
    dr,
    acc,
    bsum,
    own,
    from_left,
    from_right,
    bown,
    bleft,
    bright,
    rx,
    red,
    load_sem,
    dz_sem,
    late_sem,
    l_recv,
    r_recv,
    out_sem,
    b_sem,
    g_send,
    g_recv,
):
    rows, cols = dz.shape
    depth = xh.shape[1]
    row_blocks = depth // CUT
    col_blocks = cols // BLK
    n_cat = row_blocks * col_blocks
    proj_cols = dr.shape[1] // BLK
    n_all = n_cat + (m.shape[1] // CUT) * proj_cols
    flip = lax.axis_index("dir")
    batch = lax.axis_index("batch")
    unit = lax.axis_index("unit")
    mine = lax.rem(batch, 2)
    lane = lax.div(batch, 2)
    mid = lanes // 2
    y_dev = {"batch": batch + 1 - 2 * mine}
    l_dev = {"batch": batch - 2}
    r_dev = {"batch": batch + 2}
    has_left = lane > 0
    has_right = lane < lanes - 1
    before = lane < mid
    after = lane > mid
    middle = lane == mid

    def group(o):
        return {
            "dir": flip + (o % 2) * (1 - 2 * flip),
            "unit": unit + (o // 2) * (1 - 2 * unit),
        }

    barrier = pltpu.get_barrier_semaphore()
    pl.semaphore_signal(barrier, 1, device_id=y_dev, device_id_type=MESH)
    for o in (1, 2, 3):
        pl.semaphore_signal(barrier, 1, device_id=group(o), device_id_type=MESH)

    @pl.when(has_left)
    def _():
        pl.semaphore_signal(barrier, 1, device_id=l_dev, device_id_type=MESH)

    @pl.when(has_right)
    def _():
        pl.semaphore_signal(barrier, 1, device_id=r_dev, device_id_type=MESH)

    xh_load = pltpu.make_async_copy(xh_hbm, xh, load_sem.at[0])
    m_load = pltpu.make_async_copy(m_hbm, m, load_sem.at[1])
    dr_load = pltpu.make_async_copy(dr_hbm, dr, load_sem.at[2])

    half_rows = rows // 2
    my_rows = pl.ds(pl.multiple_of(mine * half_rows, half_rows), half_rows)
    first_late = col_blocks - LATE
    late_cols = pl.ds(first_late * BLK, LATE * BLK)

    def dz_load(b):
        at = pl.ds(pl.multiple_of(b * BLK, BLK), BLK)
        return pltpu.make_async_copy(dz_hbm.at[:, at], dz.at[:, at], dz_sem.at[b])

    late_own = pltpu.make_async_copy(
        dz_hbm.at[my_rows, late_cols], dz.at[my_rows, late_cols], late_sem.at[0]
    )
    late_far = pltpu.make_async_remote_copy(
        late_hbm,
        dz.at[my_rows, late_cols],
        late_sem.at[1],
        late_sem.at[2],
        device_id=y_dev,
        device_id_type=MESH,
    )

    xh_load.start()

    def load_all(b, carry):
        dz_load(b).start()
        return carry

    lax.fori_loop(0, first_late, load_all, 0)
    late_own.start()
    m_load.start()
    dr_load.start()

    eye = identity()

    def turn(src, dst, a):
        at = pl.ds(pl.multiple_of(a * BLK, BLK), BLK)
        for b in range(rows // BLK):
            dst[at, b * BLK : (b + 1) * BLK] = mm_nt(
                eye, src[b * BLK : (b + 1) * BLK, at]
            ).astype(BF)

    quarter = dx_ref.shape[0] // 4
    me = flip + 2 * unit

    def member(o):
        p = group(o)
        return p["dir"] + 2 * p["unit"]

    def share(o):
        return pltpu.make_async_remote_copy(
            dx_ref.at[pl.ds(member(o) * quarter, quarter)],
            rx.at[o - 1],
            g_send.at[0, o - 1],
            g_recv.at[0, o - 1],
            device_id=group(o),
            device_id_type=MESH,
        )

    def hand_out(o):
        return pltpu.make_async_remote_copy(
            red,
            ig_ref.at[pl.ds(me * quarter, quarter)],
            g_send.at[1, o - 1],
            g_recv.at[1, o - 1],
            device_id=group(o),
            device_id_type=MESH,
        )

    bsum[...] = jnp.zeros_like(bsum)
    xh_load.wait()
    turn(xh, xht, 0)
    peers = 4 + jnp.where(has_left, 1, 0) + jnp.where(has_right, 1, 0)
    pl.semaphore_wait(barrier, peers)
    late_far.start()

    def remote(src, dst, send, recv, device):
        return pltpu.make_async_remote_copy(
            src, dst, send, recv, device_id=device, device_id_type=MESH
        )

    class Chunk:
        def __init__(self, refs, sems):
            self.own, self.left, self.right, self.res = refs
            self.l_recv, self.r_recv, self.l_send, self.r_send = sems[:4]
            self.y_send, self.y_recv, self.kept = sems[4:]

        def to_left(self, src):
            return remote(src, self.right, self.l_send, self.r_recv, l_dev)

        def to_right(self, src):
            return remote(src, self.left, self.r_send, self.l_recv, r_dev)

        def left_in(self):
            return remote(self.own, self.left, self.r_send, self.l_recv, l_dev)

        def right_in(self):
            return remote(self.own, self.right, self.l_send, self.r_recv, r_dev)

        def to_y(self, src):
            return remote(src, self.res, self.y_send, self.y_recv, y_dev)

        def keep(self, src):
            return pltpu.make_async_copy(src, self.res, self.kept)

        def reduce(self, value):
            @pl.when(before)
            def _():
                @pl.when(has_left)
                def _():
                    self.left_in().wait_recv()
                    self.own[...] = (value() + self.left[...].astype(F32)).astype(BF)

                @pl.when(jnp.logical_not(has_left))
                def _():
                    self.own[...] = value().astype(BF)

                self.to_right(self.own).start()

            @pl.when(after)
            def _():
                @pl.when(has_right)
                def _():
                    self.right_in().wait_recv()
                    self.own[...] = (value() + self.right[...].astype(F32)).astype(BF)

                @pl.when(jnp.logical_not(has_right))
                def _():
                    self.own[...] = value().astype(BF)

                self.to_left(self.own).start()

            @pl.when(middle)
            def _():
                total = value()
                if mid > 0:
                    self.left_in().wait_recv()
                    total = total + self.left[...].astype(F32)
                if mid < lanes - 1:
                    self.right_in().wait_recv()
                    total = total + self.right[...].astype(F32)
                self.own[...] = total.astype(BF)
                if mid > 0:
                    self.to_left(self.own).start()
                if mid < lanes - 1:
                    self.to_right(self.own).start()
                self.to_y(self.own).start()
                self.keep(self.own).start()

        def publish(self):
            @pl.when(before)
            def _():
                self.right_in().wait_recv()

                @pl.when(has_left)
                def _():
                    self.to_left(self.right).start()

                self.to_y(self.right).start()
                self.keep(self.right).start()

            @pl.when(after)
            def _():
                self.left_in().wait_recv()

                @pl.when(has_right)
                def _():
                    self.to_right(self.left).start()

                self.to_y(self.left).start()
                self.keep(self.left).start()

        def finish(self):
            self.to_y(self.own).wait()

            @pl.when(has_left)
            def _():
                self.to_left(self.own).wait_send()

            @pl.when(has_right)
            def _():
                self.to_right(self.own).wait_send()

            self.keep(self.own).wait()

    leaving = [out_sem.at[i] for i in range(5)]

    def chunk(k):
        slot = lax.rem(k, RECV_RING)
        refs = (own.at[k], from_left.at[k], from_right.at[k], res.at[mine, k])
        return Chunk(refs, [l_recv.at[slot], r_recv.at[slot], *leaving])

    every = Chunk((own, from_left, from_right, res.at[mine]), [l_recv.at[0], r_recv.at[0], *leaving])
    bias = Chunk((bown, bleft, bright, bres.at[mine]), [b_sem.at[i] for i in range(7)])
    ones = jnp.ones((16, rows), BF)
    which = lax.broadcasted_iota(jnp.int32, (16, BLK), 0)
    far = jnp.where(before, mid - lane, lane - mid)
    inner = jnp.logical_and(has_left, has_right)
    lag = 5 * far + jnp.where(inner, 0, 12)
    longest = 5 * max(mid, lanes - 1 - mid) + 12
    turns = depth // BLK

    def body(k, carry):
        @pl.when(jnp.logical_and(k > 0, k < turns))
        def _():
            turn(xh, xht, k)

        @pl.when(k == row_blocks)
        def _():
            m_load.wait()
            dr_load.wait()
            for o in (1, 2, 3):
                share(o).start()

        @pl.when(jnp.logical_and(k >= row_blocks, k < row_blocks + m.shape[1] // BLK))
        def _():
            turn(m, mt, k - row_blocks)

        @pl.when(k < n_all)
        def _():
            @pl.when(k < n_cat)
            def _():
                b = lax.div(k, row_blocks)
                r = pl.multiple_of(lax.rem(k, row_blocks) * CUT, CUT)
                at = pl.ds(pl.multiple_of(b * BLK, BLK), BLK)

                @pl.when(jnp.logical_and(r == 0, b < first_late))
                def _():
                    dz_load(b).wait()

                @pl.when(jnp.logical_and(r == 0, b == first_late))
                def _():
                    late_own.wait()
                    late_far.wait_recv()

                @pl.when(r == 0)
                def _():
                    bsum[...] += jnp.where(which == b, mm(ones, dz[:, at]), 0.0)

                acc[...] = mm(xht[pl.ds(r, CUT), :], dz[:, at])

            @pl.when(k >= n_cat)
            def _():
                n = k - n_cat
                r = pl.multiple_of(lax.div(n, proj_cols) * CUT, CUT)
                b = pl.multiple_of(lax.rem(n, proj_cols) * BLK, BLK)
                acc[...] = mm(mt[pl.ds(r, CUT), :], dr[:, pl.ds(b, BLK)])

            chunk(k).reduce(lambda: acc[...])

            @pl.when(k == n_cat)
            def _():
                bias.reduce(lambda: bsum[...])

        @pl.when(k == 4 * row_blocks)
        def _():
            sums = dx_ref[pl.ds(me * quarter, quarter)].astype(F32)
            for o in (1, 2, 3):
                share(o).wait_recv()
                sums = sums + rx[o - 1].astype(F32)
            red[...] = sums.astype(BF)
            ig_ref[pl.ds(me * quarter, quarter)] = red[...]
            for o in (1, 2, 3):
                hand_out(o).start()

        n = k - lag

        @pl.when(jnp.logical_and(n >= 0, n < n_all))
        def _():
            chunk(n).publish()

            @pl.when(n == n_cat)
            def _():
                bias.publish()

        return carry

    lax.fori_loop(0, n_all + longest, body, 0)
    every.finish()
    late_far.wait_send()
    bias.finish()
    for o in (1, 2, 3):
        share(o).wait_send()
        hand_out(o).wait()


def gradients(lanes, dzg, late, xhg, mg, drg, dx):
    rows, cols = dzg.shape
    depth = xhg.shape[1]
    n_all = (depth // CUT) * (cols // BLK) + (mg.shape[1] // CUT) * (drg.shape[1] // BLK)
    steps, streams, width = dx.shape
    vmem = pl.BlockSpec(memory_space=pltpu.VMEM)
    hbm = pl.BlockSpec(memory_space=pl.ANY)
    shape = jax.ShapeDtypeStruct
    return pl.pallas_call(
        functools.partial(gradient_kernel, lanes),
        out_shape=(
            shape((2, n_all, CUT, BLK), BF),
            shape((2, 16, BLK), BF),
            shape((steps, streams, width), BF),
        ),
        in_specs=[hbm] * 5 + [vmem],
        out_specs=(hbm, hbm, vmem),
        scratch_shapes=[
            pltpu.VMEM((rows, cols), BF),
            pltpu.VMEM((rows, depth), BF),
            pltpu.VMEM((depth, rows), BF),
            pltpu.VMEM(mg.shape, BF),
            pltpu.VMEM((mg.shape[1], rows), BF),
            pltpu.VMEM(drg.shape, BF),
            pltpu.VMEM((CUT, BLK), F32),
            pltpu.VMEM((16, BLK), F32),
            pltpu.VMEM((n_all, CUT, BLK), BF),
            pltpu.VMEM((n_all, CUT, BLK), BF),
            pltpu.VMEM((n_all, CUT, BLK), BF),
            pltpu.VMEM((16, BLK), BF),
            pltpu.VMEM((16, BLK), BF),
            pltpu.VMEM((16, BLK), BF),
            pltpu.VMEM((3, steps // 4, streams, width), BF),
            pltpu.VMEM((steps // 4, streams, width), BF),
            pltpu.SemaphoreType.DMA((3,)),
            pltpu.SemaphoreType.DMA((cols // BLK,)),
            pltpu.SemaphoreType.DMA((3,)),
            pltpu.SemaphoreType.DMA((RECV_RING,)),
            pltpu.SemaphoreType.DMA((RECV_RING,)),
            pltpu.SemaphoreType.DMA((5,)),
            pltpu.SemaphoreType.DMA((7,)),
            pltpu.SemaphoreType.DMA((2, 3)),
            pltpu.SemaphoreType.DMA((2, 3)),
        ],
        compiler_params=pltpu.CompilerParams(
            collective_id=1, has_side_effects=True, vmem_limit_bytes=VMEM_LIMIT
        ),
        name="gradients",
    )(dzg, late, xhg, mg, drg, dx)


def widen_kernel(
    n_cat,
    res,
    bres,
    lay_in,
    ig_in,
    hfin_in,
    cfin_in,
    lay_out,
    ig_out,
    wx_out,
    wh_out,
    b_out,
    wp_out,
    hfin_out,
    cfin_out,
    low,
    wide,
    lay_low,
    lay_buf,
    ig_low,
    ig_buf,
    p_low,
    p_wide,
    b_wide,
    h_buf,
    c_buf,
    in_sem,
    out_sem,
    p_sem,
    s_in,
    s_out,
    ig_sem,
    wp_sem,
):
    width, _, units = wx_out.shape
    steps, streams, _ = lay_low.shape
    slots = low.shape[0]
    row_blocks = low.shape[1]
    half = row_blocks // 2
    col_blocks = n_cat // row_blocks
    count = 2 * col_blocks
    n_proj = p_low.shape[1]
    proj_cols = width // BLK

    def fetch(k):
        slot = lax.rem(k, slots)
        return pltpu.make_async_copy(
            res.at[lax.div(k, col_blocks), pl.ds(lax.rem(k, col_blocks) * row_blocks, row_blocks)],
            low.at[slot],
            in_sem.at[slot],
        )

    def store(k):
        slot = lax.rem(k, slots)
        owner = lax.div(k, col_blocks)
        b = lax.rem(k, col_blocks)
        gate = lax.rem(b, 4)
        u = pl.multiple_of(owner * (units // 2) + lax.div(b, 4) * BLK, BLK)
        return [
            pltpu.make_async_copy(
                wide.at[slot, i],
                out.at[:, gate, pl.ds(u, BLK)],
                out_sem.at[slot, i],
            )
            for i, out in enumerate((wx_out, wh_out))
        ]

    for k in range(slots - 1):
        fetch(k).start()
    proj = [
        pltpu.make_async_copy(res.at[o, pl.ds(n_cat, n_proj)], p_low.at[o], p_sem.at[o])
        for o in range(2)
    ]
    taken = [
        pltpu.make_async_copy(src, dst, s_in.at[i])
        for i, (src, dst) in enumerate(
            ((lay_in, lay_low), (ig_in, ig_low), (hfin_in, h_buf), (cfin_in, c_buf))
        )
    ]
    given = [
        pltpu.make_async_copy(src, dst, s_out.at[i])
        for i, (src, dst) in enumerate(
            (
                (lay_buf, lay_out.reshape(streams * steps, width)),
                (h_buf, hfin_out),
                (c_buf, cfin_out),
                (b_wide, b_out),
            )
        )
    ]
    for one in taken + proj:
        one.start()

    def body(k, carry):
        slot = lax.rem(k, slots)

        @pl.when(k >= slots)
        def _():
            for one in store(k - slots):
                one.wait()

        fetch(k).wait()
        for r in range(row_blocks):
            wide[slot, r // half, (r % half) * CUT : (r % half + 1) * CUT, :] = low[slot, r].astype(F32)
        for one in store(k):
            one.start()

        @pl.when(k + slots - 1 < count)
        def _():
            fetch(k + slots - 1).start()

        return carry

    def layer_rows():
        taken[0].wait()
        t = lax.broadcasted_iota(jnp.int32, (steps, streams * steps), 0)
        r = lax.broadcasted_iota(jnp.int32, (steps, streams * steps), 1)
        flat = lay_low[...].reshape(streams * steps, width)
        bunch = BLK // steps
        for b in range(streams // bunch):
            want = jnp.concatenate(
                [jnp.where(r == t * streams + b * bunch + s, 1.0, 0.0) for s in range(bunch)], 0
            ).astype(BF)
            lay_buf[b * BLK : (b + 1) * BLK, :] = mm(want, flat).astype(BF)
        given[0].start()

    def states():
        for i in (2, 3):
            taken[i].wait()
            given[i - 1].start()

    def input_rows():
        taken[1].wait()
        for step in range(steps):
            ig_buf[step] = ig_low[step].astype(F32)
            ig_copy(step).start()

    def ig_copy(step):
        return pltpu.make_async_copy(ig_buf.at[step], ig_out.at[:, step, :], ig_sem.at[step])

    def bias_rows():
        for owner in range(2):
            for b in range(col_blocks):
                u = owner * (units // 2) + (b // 4) * BLK
                b_wide[b % 4 : b % 4 + 1, u : u + BLK] = bres[owner, b : b + 1, :].astype(F32)
        given[3].start()

    proj_rows = n_proj // proj_cols * CUT

    def proj_copy(owner):
        return pltpu.make_async_copy(
            p_wide.at[owner], wp_out.at[pl.ds(owner * proj_rows, proj_rows)], wp_sem.at[owner]
        )

    def proj_part(owner):
        proj[owner].wait()
        for n in range(n_proj):
            row = (n // proj_cols) * CUT
            col = (n % proj_cols) * BLK
            p_wide[owner, row : row + CUT, col : col + BLK] = p_low[owner, n].astype(F32)
        proj_copy(owner).start()

    extras = [
        layer_rows,
        states,
        input_rows,
        bias_rows,
        functools.partial(proj_part, 0),
        functools.partial(proj_part, 1),
    ]
    at = slots
    lax.fori_loop(0, at, body, 0)
    for extra in extras:
        extra()
        lax.fori_loop(at, at + 3, body, 0)
        at += 3
    lax.fori_loop(at, count, body, 0)
    for k in range(count - slots, count):
        for one in store(k):
            one.wait()
    for one in [*given, *(ig_copy(step) for step in range(steps)), proj_copy(0), proj_copy(1)]:
        one.wait()


def widen(res, bres, lay, ig, hfin, cfin):
    steps, streams, width = lay.shape
    units = cfin.shape[1]
    row_blocks = 2 * width // CUT
    n_cat = row_blocks * (2 * units // BLK)
    n_proj = res.shape[1] - n_cat
    slots = 6
    vmem = pl.BlockSpec(memory_space=pltpu.VMEM)
    hbm = pl.BlockSpec(memory_space=pl.ANY)
    shape = jax.ShapeDtypeStruct
    return pl.pallas_call(
        functools.partial(widen_kernel, n_cat),
        out_shape=(
            shape((streams, steps, width), BF),
            shape((streams, steps, width), F32),
            shape((width, 4, units), F32),
            shape((width, 4, units), F32),
            shape((4, units), F32),
            shape((units, width), F32),
            shape((streams, width), F32),
            shape((streams, units), F32),
        ),
        in_specs=[hbm, vmem, hbm, hbm, hbm, hbm],
        out_specs=(hbm,) * 8,
        scratch_shapes=[
            pltpu.VMEM((slots, row_blocks, CUT, BLK), BF),
            pltpu.VMEM((slots, 2, width, BLK), F32),
            pltpu.VMEM((steps, streams, width), BF),
            pltpu.VMEM((streams * steps, width), BF),
            pltpu.VMEM((steps, streams, width), BF),
            pltpu.VMEM((steps, streams, width), F32),
            pltpu.VMEM((2, n_proj, CUT, BLK), BF),
            pltpu.VMEM((2, units // 2, width), F32),
            pltpu.VMEM((4, units), F32),
            pltpu.VMEM((streams, width), F32),
            pltpu.VMEM((streams, units), F32),
            pltpu.SemaphoreType.DMA((slots,)),
            pltpu.SemaphoreType.DMA((slots, 2)),
            pltpu.SemaphoreType.DMA((2,)),
            pltpu.SemaphoreType.DMA((4,)),
            pltpu.SemaphoreType.DMA((4,)),
            pltpu.SemaphoreType.DMA((steps,)),
            pltpu.SemaphoreType.DMA((2,)),
        ],
        compiler_params=pltpu.CompilerParams(vmem_limit_bytes=VMEM_LIMIT),
        name="widen",
    )(res, bres, lay, ig, hfin, cfin)


def on_device(
    inputs,
    win_count,
    last_live,
    hidden_init,
    cell_init,
    w_input,
    w_hidden,
    gate_bias,
    w_proj,
    out_grad,
):
    streams, steps, width = inputs.shape
    units = w_proj.shape[1]
    lanes = lax.axis_size("batch") // 2
    lay, hfin, cfin, dx, dzg, late, xhg, mg, drg = recurrence(
        inputs,
        out_grad[0],
        win_count.reshape(1, streams),
        last_live.reshape(1, streams),
        hidden_init[0],
        cell_init[0],
        gate_bias[0],
        w_input[0],
        w_hidden[0],
        w_proj[0],
    )
    rows = 2 * steps * streams
    res, bres, ig = gradients(
        lanes,
        dzg.reshape(rows, 2 * units),
        late.reshape(steps * streams, LATE * BLK),
        xhg.reshape(rows, 2 * width),
        mg.reshape(rows, units // 2),
        drg.reshape(rows, width),
        dx,
    )
    out = widen(res, bres, lay, ig, hfin, cfin)
    layer_out, input_grad, wx_grad, wh_grad, b_grad, wp_grad, hidden_final, cell_final = out
    return (
        layer_out[None],
        input_grad,
        wx_grad[None],
        wh_grad[None],
        b_grad[None],
        wp_grad[None],
        hidden_final[None],
        cell_final[None],
    )


def solution(mesh):
    placed = (
        P("batch", None, None),
        P("batch"),
        P("batch"),
        P("dir", "batch", None),
        P("dir", "batch", "unit"),
        P("dir", None, None, "unit"),
        P("dir", None, None, "unit"),
        P("dir", None, "unit"),
        P("dir", "unit", None),
        P("dir", "batch", None, None),
    )
    return jax.shard_map(
        on_device,
        mesh=mesh,
        in_specs=placed,
        out_specs=(
            P("dir", "batch", None, None),
            P("batch", None, None),
            P("dir", None, None, "unit"),
            P("dir", None, None, "unit"),
            P("dir", None, "unit"),
            P("dir", "unit", None),
            P("dir", "batch", None),
            P("dir", "batch", "unit"),
        ),
        check_vma=False,
    )
```

```python
import functools

import jax
import jax.numpy as jnp
from jax import lax
from jax.experimental import pallas as pl
from jax.experimental.pallas import tpu as pltpu
from jax.sharding import PartitionSpec as P

WIN = 8
BLK = 256
CUT = 128
RING = 4
LATE = 3
RECV_RING = 32
MESH = pl.DeviceIdType.MESH
BF = jnp.bfloat16
F32 = jnp.float32
NT = (((1,), (1,)), ((), ()))
VMEM_LIMIT = 60 * 1024 * 1024
THIRD = 1.0 / 3.0


def sigmoid(v):
    return 0.5 * jnp.tanh(0.5 * v) + 0.5


def mm(a, b):
    return jnp.dot(a, b, preferred_element_type=F32)


def mm_pad(a, b):
    fill = jnp.zeros((128 - a.shape[0], a.shape[1]), a.dtype)
    return mm(jnp.concatenate([a, fill], 0), b)[: a.shape[0]]


def mm_nt(a, b):
    return lax.dot_general(a, b, NT, preferred_element_type=F32)


def identity():
    rows = lax.broadcasted_iota(jnp.int32, (BLK, BLK), 0)
    cols = lax.broadcasted_iota(jnp.int32, (BLK, BLK), 1)
    return jnp.where(rows == cols, 1.0, 0.0).astype(BF)


def gate_order():
    rows = lax.broadcasted_iota(jnp.int32, (BLK, BLK), 0)
    cols = lax.broadcasted_iota(jnp.int32, (BLK, BLK), 1)
    want = (rows & (BLK // 4 - 1)) * 4 + (rows >> 6)
    return jnp.where(want == cols, 1.0, 0.0).astype(BF)


def recurrence_kernel(
    x_hbm,
    y_hbm,
    win_hbm,
    last_hbm,
    h0_hbm,
    c0_hbm,
    bias_hbm,
    wx_hbm,
    wh_hbm,
    wp_hbm,
    lay_hbm,
    hfin_hbm,
    cfin_hbm,
    dx_hbm,
    dzg,
    late,
    xhg,
    mg,
    drg,
    w,
    wht,
    wp,
    wpt,
    z,
    c,
    th,
    x_flat,
    y_flat,
    xh,
    y_now,
    m,
    dr,
    dz,
    dc,
    dh,
    lens,
    snd,
    rcv,
    win_ref,
    last_ref,
    h0_ref,
    bias_ref,
    lay_ref,
    dx_ref,
    raw_sem,
    load_sem,
    state_sem,
    ex_send,
    ex_recv,
    y_recv,
    whole_send,
    whole_keep,
    ring_send,
    ring_keep,
    late_keep,
):
    steps, streams, width = lay_hbm.shape
    units = wp.shape[0]
    tiles = units // BLK
    gate4 = 4 * BLK
    half_cols = 2 * units
    half_units = units // 2
    flip = lax.axis_index("dir")
    batch = lax.axis_index("batch")
    unit = lax.axis_index("unit")
    mine = lax.rem(batch, 2)
    other = 1 - mine
    y_dev = {"batch": batch + 1 - 2 * mine}
    x_dev = {"unit": 1 - unit}
    hid = slice(width, 2 * width)

    def place(t):
        return t + flip * (steps - 1 - 2 * t)

    slots = wpt.shape[0] // BLK
    blocks = width * 4 // BLK

    def raw(slot):
        return wpt.at[pl.ds(pl.multiple_of(slot * BLK, BLK), BLK)]

    def fetch(b, w_hbm, slot):
        return pltpu.make_async_copy(
            w_hbm.reshape(width * 4, units).at[pl.ds(pl.multiple_of(b * BLK, BLK), BLK)],
            raw(slot),
            raw_sem.at[slot],
        )

    def fetch_any(n):
        slot = lax.rem(n, slots)

        @pl.when(n < blocks)
        def _():
            fetch(n, wx_hbm, slot).start()

        @pl.when(jnp.logical_and(n >= blocks, n < 2 * blocks))
        def _():
            fetch(n - blocks, wh_hbm, slot).start()

    for n in range(slots - 1):
        fetch(n, wx_hbm, n).start()
    x_copy = pltpu.make_async_copy(x_hbm.reshape(streams * steps, width), x_flat, load_sem.at[0])
    y_copy = pltpu.make_async_copy(y_hbm.reshape(streams * steps, width), y_flat, load_sem.at[1])
    proj_copy = pltpu.make_async_copy(wp_hbm, wp, load_sem.at[2])
    small = [
        pltpu.make_async_copy(src, dst, load_sem.at[3 + i])
        for i, (src, dst) in enumerate(
            (
                (win_hbm, win_ref),
                (last_hbm, last_ref),
                (h0_hbm, h0_ref),
                (bias_hbm, bias_ref),
                (c0_hbm, c.at[0]),
            )
        )
    ]
    finals = [
        pltpu.make_async_copy(lay_ref, lay_hbm, state_sem.at[0]),
        pltpu.make_async_copy(h0_ref, hfin_hbm, state_sem.at[1]),
        pltpu.make_async_copy(c.at[steps], cfin_hbm, state_sem.at[2]),
    ]

    def dx_copy(t):
        return pltpu.make_async_copy(dx_ref.at[t], dx_hbm.at[t], state_sem.at[3])

    for one in [x_copy, proj_copy, y_copy, *small]:
        one.start()
    barrier = pltpu.get_barrier_semaphore()
    pl.semaphore_signal(barrier, 1, device_id=x_dev, device_id_type=MESH)
    pl.semaphore_signal(barrier, 1, device_id=y_dev, device_id_type=MESH)

    order = gate_order()

    def spread(n, carry):
        slot = lax.rem(n, slots)
        fetch_any(n + slots - 1)
        fetch(0, wx_hbm, slot).wait()
        which = lax.div(n, blocks)
        left = n - which * blocks
        row = pl.multiple_of(left * 64, 64)
        for j in range(tiles):
            got = mm(order, raw(slot)[:, j * BLK : (j + 1) * BLK]).astype(BF)
            for g in range(4):
                base = j * gate4 + g * BLK
                w[which, pl.ds(row, 64), base : base + BLK] = got[g * 64 : (g + 1) * 64]
        return carry

    lax.fori_loop(0, 2 * blocks, spread, 0)
    wx, wh = w.at[0], w.at[1]

    for one in small:
        one.wait()
    row_len = ((win_ref[...] - 1) * WIN + last_ref[...]).astype(F32)
    rows = lax.broadcasted_iota(jnp.int32, (streams, streams), 0)
    cols = lax.broadcasted_iota(jnp.int32, (streams, streams), 1)
    spot = jnp.where(rows == cols, jnp.broadcast_to(row_len, (streams, streams)), 0.0)
    lens[...] = jnp.broadcast_to(jnp.sum(spot, axis=1, keepdims=True), lens.shape)

    def live_of(t, count):
        live = jnp.where(lens[...] > place(t).astype(F32), 1.0, 0.0)
        return jnp.concatenate([live] * (count // 128), 1)

    def pick(flat, t):
        s = lax.broadcasted_iota(jnp.int32, (streams, streams * steps), 0)
        r = lax.broadcasted_iota(jnp.int32, (streams, streams * steps), 1)
        want = jnp.where(r == s * steps + place(t), 1.0, 0.0).astype(BF)
        return mm(want, flat[...]).astype(BF)

    def exchange(k):
        slot = lax.rem(k, 2)
        return pltpu.make_async_remote_copy(
            snd.at[slot],
            rcv.at[slot],
            ex_send.at[slot],
            ex_recv.at[slot],
            device_id=x_dev,
            device_id_type=MESH,
        )

    def remote(away, target, send, recv):
        return pltpu.make_async_remote_copy(
            away, target, send, recv, device_id=y_dev, device_id_type=MESH
        )

    def whole(kind, src, target):
        return (
            remote(src, target, whole_send.at[kind], y_recv.at[kind]),
            pltpu.make_async_copy(src, target, whole_keep.at[kind]),
        )

    def xh_pair(t):
        return whole(0, xh.at[t], xhg.at[mine, place(t)])

    def dr_pair(t):
        return whole(1, dr.at[t], drg.at[mine, place(t)])

    def m_pair(t):
        slot = lax.rem(t, RING)
        away = m.at[slot, :, pl.ds(pl.multiple_of(other * half_units, half_units), half_units)]
        keep = m.at[slot, :, pl.ds(pl.multiple_of(mine * half_units, half_units), half_units)]
        target = mg.at[mine, place(t)]
        return (
            remote(away, target, ring_send.at[0, slot], y_recv.at[2]),
            pltpu.make_async_copy(keep, target, ring_keep.at[0, slot]),
        )

    early = half_cols - LATE * BLK

    def dz_pair(t):
        slot = lax.rem(t, RING)
        first = pl.multiple_of(other * half_cols, half_cols)
        away = dz.at[slot, :, pl.ds(first, early)]
        rest = dz.at[slot, :, pl.ds(pl.multiple_of(first + early, BLK), LATE * BLK)]
        keep = dz.at[slot, :, pl.ds(pl.multiple_of(mine * half_cols, half_cols), half_cols)]
        return (
            remote(
                away,
                dzg.at[mine, place(t), :, pl.ds(0, early)],
                ring_send.at[1, slot],
                y_recv.at[3],
            ),
            pltpu.make_async_copy(keep, dzg.at[mine, place(t)], ring_keep.at[1, slot]),
            pltpu.make_async_copy(rest, late.at[place(t)], late_keep.at[slot]),
        )

    def begin(copies):
        for one in copies:
            one.start()

    def sent(copies):
        copies[0].wait_send()
        for one in copies[1:]:
            one.wait()

    def input_part(t):
        now = xh[t, :, :width]
        for j in range(tiles):
            part = mm(now, wx[:, j * gate4 : (j + 1) * gate4])
            for g in range(4):
                z[t, :, j * gate4 + g * BLK : j * gate4 + (g + 1) * BLK] = (
                    part[:, g * BLK : (g + 1) * BLK] + bias_ref[g : g + 1, j * BLK : (j + 1) * BLK]
                )

    eye = identity()
    x_copy.wait()
    xh[0, :, :width] = pick(x_flat, 0)
    xh[0, :, hid] = h0_ref[...].astype(BF)
    input_part(0)
    proj_copy.wait()
    y_copy.wait()
    turn_cols = 4 * units // steps
    turn_units = units // steps
    pl.semaphore_wait(barrier, 2)

    def forward(t, carry):
        slot = lax.rem(t, RING)

        @pl.when(t >= RING)
        def _():
            sent(m_pair(t - RING))

        live = live_of(t, BLK) > 0.5
        hidden = xh[t, :, hid]
        for j in range(tiles):
            cols = slice(j * BLK, (j + 1) * BLK)
            base = j * gate4
            pre = z[t, :, base : base + gate4] + mm_pad(hidden, wh[:, base : base + gate4])
            in_gate = sigmoid(pre[:, :BLK])
            forget = sigmoid(pre[:, BLK : 2 * BLK])
            cand = jnp.tanh(pre[:, 2 * BLK : 3 * BLK])
            out_gate = sigmoid(pre[:, 3 * BLK :])
            prev = c[t, :, cols]
            new = 3.0 * jnp.tanh((forget * prev + in_gate * cand) * THIRD)
            m[slot, :, cols] = (out_gate * jnp.tanh(new)).astype(BF)
            z[t, :, base : base + BLK] = in_gate
            z[t, :, base + BLK : base + 2 * BLK] = forget
            z[t, :, base + 2 * BLK : base + 3 * BLK] = cand
            z[t, :, base + 3 * BLK : base + gate4] = out_gate
            c[t + 1, :, cols] = jnp.where(live, new, prev)
        two = lax.rem(t, 2)
        snd[two] = mm_pad(m[slot], wp[...]).astype(BF)
        copy = exchange(t)
        copy.start()
        begin(xh_pair(t))
        begin(m_pair(t))

        @pl.when(t + 1 < steps)
        def _():
            xh[t + 1, :, :width] = pick(x_flat, t + 1)
            input_part(t + 1)

        at = pl.multiple_of(t * turn_cols, turn_cols)
        for kb in range(width // BLK):
            for cb in range(turn_cols // BLK):
                wht[pl.ds(at + cb * BLK, BLK), kb * BLK : (kb + 1) * BLK] = mm_nt(
                    eye, wh[kb * BLK : (kb + 1) * BLK, pl.ds(at + cb * BLK, BLK)]
                ).astype(BF)
        at = pl.multiple_of(t * turn_units, turn_units)
        for kb in range(width // BLK):
            wpt[kb * BLK : (kb + 1) * BLK, pl.ds(at, turn_units)] = mm_nt(
                eye, wp[pl.ds(at, turn_units), kb * BLK : (kb + 1) * BLK]
            ).astype(BF)
        copy.wait()
        total = snd[two].astype(F32) + rcv[two].astype(F32)
        squash = jnp.tanh(total * THIRD)
        th[t] = squash
        new_hidden = (3.0 * squash).astype(BF).astype(F32)
        live_h = live_of(t, width)
        lay_ref[place(t)] = (xh[t, :, :width].astype(F32) + live_h * new_hidden).astype(BF)
        after = jnp.where(live_h > 0.5, new_hidden, hidden.astype(F32))

        @pl.when(t + 1 < steps)
        def _():
            xh[t + 1, :, hid] = after.astype(BF)

        @pl.when(t + 1 == steps)
        def _():
            h0_ref[...] = after

        return carry

    lax.fori_loop(0, steps, forward, 0)
    for one in finals:
        one.start()
    dc[...] = jnp.zeros_like(dc)
    dh[...] = jnp.zeros_like(dh)
    y_now[0] = pick(y_flat, steps - 1)

    def backward(k, carry):
        t = steps - 1 - k
        slot = lax.rem(t, RING)
        two = lax.rem(k, 2)

        @pl.when(k >= RING)
        def _():
            sent(dz_pair(t + RING))

        grad_hidden = dh[...]
        live_h = live_of(t, width)
        squash = th[t]
        y_low = y_now[two].astype(F32)
        low = (live_h * (y_low + grad_hidden) * (1.0 - squash * squash)).astype(BF)
        dr[t] = low
        live = live_of(t, BLK)
        grads_m = mm_pad(low, wpt[:width, :]).astype(BF).astype(F32)
        for j in range(tiles):
            cols = slice(j * BLK, (j + 1) * BLK)
            base = j * gate4
            grad_m = grads_m[:, cols]
            in_gate = z[t, :, base : base + BLK]
            forget = z[t, :, base + BLK : base + 2 * BLK]
            cand = z[t, :, base + 2 * BLK : base + 3 * BLK]
            out_gate = z[t, :, base + 3 * BLK : base + gate4]
            prev = c[t, :, cols]
            new = c[t + 1, :, cols]
            grad_c = dc[:, cols]
            tanh_new = jnp.tanh(new)
            grad_n = live * grad_c + grad_m * out_gate * (1.0 - tanh_new * tanh_new)
            third = new * THIRD
            grad_u = grad_n * (1.0 - third * third)
            dz[slot, :, base : base + BLK] = (grad_u * cand * in_gate * (1.0 - in_gate)).astype(BF)
            dz[slot, :, base + BLK : base + 2 * BLK] = (
                grad_u * prev * forget * (1.0 - forget)
            ).astype(BF)
            dz[slot, :, base + 2 * BLK : base + 3 * BLK] = (
                grad_u * in_gate * (1.0 - cand * cand)
            ).astype(BF)
            dz[slot, :, base + 3 * BLK : base + gate4] = (
                grad_m * tanh_new * out_gate * (1.0 - out_gate)
            ).astype(BF)
            dc[:, cols] = (1.0 - live) * grad_c + grad_u * forget
        part = mm_pad(dz[slot], wht[...])
        snd[two] = part.astype(BF)
        copy = exchange(k)
        copy.start()
        begin(dz_pair(t))
        begin(dr_pair(t))

        @pl.when(k + 1 < steps)
        def _():
            y_now[1 - two] = pick(y_flat, t - 1)

        grad_x = y_low * jnp.where(unit == 0, 1.0, 0.0)
        for j in range(tiles):
            base = j * gate4
            grad_x = grad_x + mm_nt(dz[slot, :, base : base + gate4], wx[:, base : base + gate4])
        dx_ref[place(t)] = grad_x.astype(BF)
        dx_copy(place(t)).start()
        copy.wait()
        dh[...] = (1.0 - live_h) * grad_hidden + (snd[two].astype(F32) + rcv[two].astype(F32))
        return carry

    lax.fori_loop(0, steps, backward, 0)

    def last(i, carry):
        sent(m_pair(steps - RING + i))
        sent(dz_pair(i))
        return carry

    lax.fori_loop(0, RING, last, 0)

    for one in finals:
        one.wait()
    pltpu.make_async_copy(dx_ref, dx_hbm, state_sem.at[3]).wait()
    xh_all = whole(0, xh, xhg.at[mine])
    dr_all = whole(1, dr, drg.at[mine])
    sent(xh_all)
    sent(dr_all)
    xh_all[0].wait_recv()
    dr_all[0].wait_recv()
    remote(mg.at[mine], mg.at[mine], ring_send.at[0, 0], y_recv.at[2]).wait_recv()
    part = dzg.at[mine, :, :, pl.ds(0, early)]
    remote(part, part, ring_send.at[1, 0], y_recv.at[3]).wait_recv()


def recurrence(inputs, out_grad, win, last, hidden0, cell0, bias, w_in, w_hid, proj):
    streams, steps, width = inputs.shape
    units = proj.shape[0]
    hbm = pl.BlockSpec(memory_space=pl.ANY)
    shape = jax.ShapeDtypeStruct
    return pl.pallas_call(
        recurrence_kernel,
        out_shape=(
            shape((steps, streams, width), BF),
            shape((streams, width), F32),
            shape((streams, units), F32),
            shape((steps, streams, width), BF),
            shape((2, steps, streams, 2 * units), BF),
            shape((steps, streams, LATE * BLK), BF),
            shape((2, steps, streams, 2 * width), BF),
            shape((2, steps, streams, units // 2), BF),
            shape((2, steps, streams, width), BF),
        ),
        in_specs=[hbm] * 10,
        out_specs=(hbm,) * 9,
        scratch_shapes=[
            pltpu.VMEM((2, width, 4 * units), BF),
            pltpu.VMEM((4 * units, width), BF),
            pltpu.VMEM((units, width), BF),
            pltpu.VMEM((max(width, 4 * BLK), units), BF),
            pltpu.VMEM((steps, streams, 4 * units), F32),
            pltpu.VMEM((steps + 1, streams, units), F32),
            pltpu.VMEM((steps, streams, width), F32),
            pltpu.VMEM((streams * steps, width), BF),
            pltpu.VMEM((streams * steps, width), BF),
            pltpu.VMEM((steps, streams, 2 * width), BF),
            pltpu.VMEM((2, streams, width), BF),
            pltpu.VMEM((RING, streams, units), BF),
            pltpu.VMEM((steps, streams, width), BF),
            pltpu.VMEM((RING, streams, 4 * units), BF),
            pltpu.VMEM((streams, units), F32),
            pltpu.VMEM((streams, width), F32),
            pltpu.VMEM((streams, 128), F32),
            pltpu.VMEM((2, streams, width), BF),
            pltpu.VMEM((2, streams, width), BF),
            pltpu.VMEM((1, streams), jnp.int32),
            pltpu.VMEM((1, streams), jnp.int32),
            pltpu.VMEM((streams, width), F32),
            pltpu.VMEM((4, units), F32),
            pltpu.VMEM((steps, streams, width), BF),
            pltpu.VMEM((steps, streams, width), BF),
            pltpu.SemaphoreType.DMA((4,)),
            pltpu.SemaphoreType.DMA((8,)),
            pltpu.SemaphoreType.DMA((4,)),
            pltpu.SemaphoreType.DMA((2,)),
            pltpu.SemaphoreType.DMA((2,)),
            pltpu.SemaphoreType.DMA((4,)),
            pltpu.SemaphoreType.DMA((2,)),
            pltpu.SemaphoreType.DMA((2,)),
            pltpu.SemaphoreType.DMA((2, RING)),
            pltpu.SemaphoreType.DMA((2, RING)),
            pltpu.SemaphoreType.DMA((RING,)),
        ],
        compiler_params=pltpu.CompilerParams(
            collective_id=0, has_side_effects=True, vmem_limit_bytes=VMEM_LIMIT
        ),
        name="recurrence",
    )(inputs, out_grad, win, last, hidden0, cell0, bias, w_in, w_hid, proj)


def gradient_kernel(
    lanes,
    dz_hbm,
    late_hbm,
    xh_hbm,
    m_hbm,
    dr_hbm,
    dx_hbm,
    res,
    bres,
    ig_hbm,
    dz,
    xh,
    xht,
    m,
    mt,
    dr,
    acc,
    bsum,
    own,
    from_left,
    from_right,
    bown,
    bleft,
    bright,
    rx,
    red,
    load_sem,
    xh_sem,
    dz_sem,
    late_sem,
    l_recv,
    r_recv,
    out_sem,
    b_sem,
    g_send,
    g_recv,
):
    rows, cols = dz.shape
    depth = xh.shape[1]
    row_blocks = depth // CUT
    col_blocks = cols // BLK
    n_cat = row_blocks * col_blocks
    proj_cols = dr.shape[1] // BLK
    n_all = n_cat + (m.shape[1] // CUT) * proj_cols
    flip = lax.axis_index("dir")
    batch = lax.axis_index("batch")
    unit = lax.axis_index("unit")
    mine = lax.rem(batch, 2)
    lane = lax.div(batch, 2)
    mid = lanes // 2
    y_dev = {"batch": batch + 1 - 2 * mine}
    l_dev = {"batch": batch - 2}
    r_dev = {"batch": batch + 2}
    has_left = lane > 0
    has_right = lane < lanes - 1
    before = lane < mid
    after = lane > mid
    middle = lane == mid

    def group(o):
        return {
            "dir": flip + (o % 2) * (1 - 2 * flip),
            "unit": unit + (o // 2) * (1 - 2 * unit),
        }

    barrier = pltpu.get_barrier_semaphore()
    pl.semaphore_signal(barrier, 1, device_id=y_dev, device_id_type=MESH)
    for o in (1, 2, 3):
        pl.semaphore_signal(barrier, 1, device_id=group(o), device_id_type=MESH)

    @pl.when(has_left)
    def _():
        pl.semaphore_signal(barrier, 1, device_id=l_dev, device_id_type=MESH)

    @pl.when(has_right)
    def _():
        pl.semaphore_signal(barrier, 1, device_id=r_dev, device_id_type=MESH)

    def xh_load(a):
        at = pl.ds(pl.multiple_of(a * BLK, BLK), BLK)
        return pltpu.make_async_copy(xh_hbm.at[:, at], xh.at[:, at], xh_sem.at[a])

    m_load = pltpu.make_async_copy(m_hbm, m, load_sem.at[1])
    dr_load = pltpu.make_async_copy(dr_hbm, dr, load_sem.at[2])

    half_rows = rows // 2
    my_rows = pl.ds(pl.multiple_of(mine * half_rows, half_rows), half_rows)
    first_late = col_blocks - LATE
    late_cols = pl.ds(first_late * BLK, LATE * BLK)

    def dz_load(b):
        at = pl.ds(pl.multiple_of(b * BLK, BLK), BLK)
        return pltpu.make_async_copy(dz_hbm.at[:, at], dz.at[:, at], dz_sem.at[b])

    late_own = pltpu.make_async_copy(
        dz_hbm.at[my_rows, late_cols], dz.at[my_rows, late_cols], late_sem.at[0]
    )
    late_far = pltpu.make_async_remote_copy(
        late_hbm,
        dz.at[my_rows, late_cols],
        late_sem.at[1],
        late_sem.at[2],
        device_id=y_dev,
        device_id_type=MESH,
    )

    def load_all(b, carry):
        dz_load(b).start()
        return carry

    turns = depth // BLK
    xh_load(0).start()
    dz_load(0).start()
    for a in range(1, turns):
        xh_load(a).start()
    lax.fori_loop(1, first_late, load_all, 0)
    late_own.start()
    m_load.start()
    dr_load.start()

    eye = identity()

    def turn(src, dst, a):
        at = pl.ds(pl.multiple_of(a * BLK, BLK), BLK)
        for b in range(rows // BLK):
            dst[at, b * BLK : (b + 1) * BLK] = mm_nt(
                eye, src[b * BLK : (b + 1) * BLK, at]
            ).astype(BF)

    quarter = dx_hbm.shape[0] // 4
    me = flip + 2 * unit

    def member(o):
        p = group(o)
        return p["dir"] + 2 * p["unit"]

    dx_own = pltpu.make_async_copy(
        dx_hbm.at[pl.ds(me * quarter, quarter)], red.at[0], load_sem.at[0]
    )
    ig_own = pltpu.make_async_copy(
        red.at[1], ig_hbm.at[pl.ds(me * quarter, quarter)], load_sem.at[0]
    )

    def share(o):
        return pltpu.make_async_remote_copy(
            dx_hbm.at[pl.ds(member(o) * quarter, quarter)],
            rx.at[o - 1],
            g_send.at[0, o - 1],
            g_recv.at[0, o - 1],
            device_id=group(o),
            device_id_type=MESH,
        )

    def hand_out(o):
        return pltpu.make_async_remote_copy(
            red.at[1],
            ig_hbm.at[pl.ds(me * quarter, quarter)],
            g_send.at[1, o - 1],
            g_recv.at[1, o - 1],
            device_id=group(o),
            device_id_type=MESH,
        )

    peers = 4 + jnp.where(has_left, 1, 0) + jnp.where(has_right, 1, 0)
    pl.semaphore_wait(barrier, peers)
    late_far.start()
    bsum[...] = jnp.zeros_like(bsum)
    xh_load(0).wait()
    turn(xh, xht, 0)

    def remote(src, dst, send, recv, device):
        return pltpu.make_async_remote_copy(
            src, dst, send, recv, device_id=device, device_id_type=MESH
        )

    class Chunk:
        def __init__(self, refs, sems):
            self.own, self.left, self.right, self.res = refs
            self.l_recv, self.r_recv, self.l_send, self.r_send = sems[:4]
            self.y_send, self.y_recv, self.kept = sems[4:]

        def to_left(self, src):
            return remote(src, self.right, self.l_send, self.r_recv, l_dev)

        def to_right(self, src):
            return remote(src, self.left, self.r_send, self.l_recv, r_dev)

        def left_in(self):
            return remote(self.own, self.left, self.r_send, self.l_recv, l_dev)

        def right_in(self):
            return remote(self.own, self.right, self.l_send, self.r_recv, r_dev)

        def to_y(self, src):
            return remote(src, self.res, self.y_send, self.y_recv, y_dev)

        def keep(self, src):
            return pltpu.make_async_copy(src, self.res, self.kept)

        def reduce(self, value):
            @pl.when(before)
            def _():
                @pl.when(has_left)
                def _():
                    self.left_in().wait_recv()
                    self.own[...] = (value() + self.left[...].astype(F32)).astype(BF)

                @pl.when(jnp.logical_not(has_left))
                def _():
                    self.own[...] = value().astype(BF)

                self.to_right(self.own).start()

            @pl.when(after)
            def _():
                @pl.when(has_right)
                def _():
                    self.right_in().wait_recv()
                    self.own[...] = (value() + self.right[...].astype(F32)).astype(BF)

                @pl.when(jnp.logical_not(has_right))
                def _():
                    self.own[...] = value().astype(BF)

                self.to_left(self.own).start()

            @pl.when(middle)
            def _():
                total = value()
                if mid > 0:
                    self.left_in().wait_recv()
                    total = total + self.left[...].astype(F32)
                if mid < lanes - 1:
                    self.right_in().wait_recv()
                    total = total + self.right[...].astype(F32)
                self.own[...] = total.astype(BF)
                if mid > 0:
                    self.to_left(self.own).start()
                if mid < lanes - 1:
                    self.to_right(self.own).start()
                self.to_y(self.own).start()
                self.keep(self.own).start()

        def publish(self):
            @pl.when(before)
            def _():
                self.right_in().wait_recv()

                @pl.when(has_left)
                def _():
                    self.to_left(self.right).start()

                self.to_y(self.right).start()
                self.keep(self.right).start()

            @pl.when(after)
            def _():
                self.left_in().wait_recv()

                @pl.when(has_right)
                def _():
                    self.to_right(self.left).start()

                self.to_y(self.left).start()
                self.keep(self.left).start()

        def finish(self):
            self.to_y(self.own).wait()

            @pl.when(has_left)
            def _():
                self.to_left(self.own).wait_send()

            @pl.when(has_right)
            def _():
                self.to_right(self.own).wait_send()

            self.keep(self.own).wait()

    leaving = [out_sem.at[i] for i in range(5)]

    def chunk(k):
        slot = lax.rem(k, RECV_RING)
        refs = (own.at[k], from_left.at[k], from_right.at[k], res.at[mine, k])
        return Chunk(refs, [l_recv.at[slot], r_recv.at[slot], *leaving])

    every = Chunk((own, from_left, from_right, res.at[mine]), [l_recv.at[0], r_recv.at[0], *leaving])
    bias = Chunk((bown, bleft, bright, bres.at[mine]), [b_sem.at[i] for i in range(7)])
    ones = jnp.ones((16, rows), BF)
    which = lax.broadcasted_iota(jnp.int32, (16, BLK), 0)
    far = jnp.where(before, mid - lane, lane - mid)
    inner = jnp.logical_and(has_left, has_right)
    lag = 5 * far + jnp.where(inner, 0, 12)
    longest = 5 * max(mid, lanes - 1 - mid) + 12

    def body(k, carry):
        @pl.when(jnp.logical_and(k > 0, k < turns))
        def _():
            xh_load(k).wait()
            turn(xh, xht, k)

        @pl.when(k == row_blocks)
        def _():
            m_load.wait()
            dr_load.wait()
            dx_own.start()
            for o in (1, 2, 3):
                share(o).start()

        @pl.when(jnp.logical_and(k >= row_blocks, k < row_blocks + m.shape[1] // BLK))
        def _():
            turn(m, mt, k - row_blocks)

        @pl.when(k < n_all)
        def _():
            @pl.when(k < n_cat)
            def _():
                b = lax.div(k, row_blocks)
                r = pl.multiple_of(lax.rem(k, row_blocks) * CUT, CUT)
                at = pl.ds(pl.multiple_of(b * BLK, BLK), BLK)

                @pl.when(jnp.logical_and(r == 0, b < first_late))
                def _():
                    dz_load(b).wait()

                @pl.when(jnp.logical_and(r == 0, b == first_late))
                def _():
                    late_own.wait()
                    late_far.wait_recv()

                @pl.when(r == 0)
                def _():
                    bsum[...] += jnp.where(which == b, mm(ones, dz[:, at]), 0.0)

                acc[...] = mm(xht[pl.ds(r, CUT), :], dz[:, at])

            @pl.when(k >= n_cat)
            def _():
                n = k - n_cat
                r = pl.multiple_of(lax.div(n, proj_cols) * CUT, CUT)
                b = pl.multiple_of(lax.rem(n, proj_cols) * BLK, BLK)
                acc[...] = mm(mt[pl.ds(r, CUT), :], dr[:, pl.ds(b, BLK)])

            chunk(k).reduce(lambda: acc[...])

            @pl.when(k == n_cat)
            def _():
                bias.reduce(lambda: bsum[...])

        @pl.when(k == 4 * row_blocks)
        def _():
            dx_own.wait()
            sums = red[0].astype(F32)
            for o in (1, 2, 3):
                share(o).wait_recv()
                sums = sums + rx[o - 1].astype(F32)
            red[1] = sums.astype(BF)
            ig_own.start()
            for o in (1, 2, 3):
                hand_out(o).start()

        n = k - lag

        @pl.when(jnp.logical_and(n >= 0, n < n_all))
        def _():
            chunk(n).publish()

            @pl.when(n == n_cat)
            def _():
                bias.publish()

        return carry

    lax.fori_loop(0, n_all + longest, body, 0)
    every.finish()
    late_far.wait_send()
    ig_own.wait()
    bias.finish()
    for o in (1, 2, 3):
        share(o).wait_send()
        hand_out(o).wait()


def gradients(lanes, dzg, late, xhg, mg, drg, dx):
    rows, cols = dzg.shape
    depth = xhg.shape[1]
    n_all = (depth // CUT) * (cols // BLK) + (mg.shape[1] // CUT) * (drg.shape[1] // BLK)
    steps, streams, width = dx.shape
    hbm = pl.BlockSpec(memory_space=pl.ANY)
    shape = jax.ShapeDtypeStruct
    return pl.pallas_call(
        functools.partial(gradient_kernel, lanes),
        out_shape=(
            shape((2, n_all, CUT, BLK), BF),
            shape((2, 16, BLK), BF),
            shape((steps, streams, width), BF),
        ),
        in_specs=[hbm] * 6,
        out_specs=(hbm, hbm, hbm),
        scratch_shapes=[
            pltpu.VMEM((rows, cols), BF),
            pltpu.VMEM((rows, depth), BF),
            pltpu.VMEM((depth, rows), BF),
            pltpu.VMEM(mg.shape, BF),
            pltpu.VMEM((mg.shape[1], rows), BF),
            pltpu.VMEM(drg.shape, BF),
            pltpu.VMEM((CUT, BLK), F32),
            pltpu.VMEM((16, BLK), F32),
            pltpu.VMEM((n_all, CUT, BLK), BF),
            pltpu.VMEM((n_all, CUT, BLK), BF),
            pltpu.VMEM((n_all, CUT, BLK), BF),
            pltpu.VMEM((16, BLK), BF),
            pltpu.VMEM((16, BLK), BF),
            pltpu.VMEM((16, BLK), BF),
            pltpu.VMEM((3, steps // 4, streams, width), BF),
            pltpu.VMEM((2, steps // 4, streams, width), BF),
            pltpu.SemaphoreType.DMA((3,)),
            pltpu.SemaphoreType.DMA((depth // BLK,)),
            pltpu.SemaphoreType.DMA((cols // BLK,)),
            pltpu.SemaphoreType.DMA((3,)),
            pltpu.SemaphoreType.DMA((RECV_RING,)),
            pltpu.SemaphoreType.DMA((RECV_RING,)),
            pltpu.SemaphoreType.DMA((5,)),
            pltpu.SemaphoreType.DMA((7,)),
            pltpu.SemaphoreType.DMA((2, 3)),
            pltpu.SemaphoreType.DMA((2, 3)),
        ],
        compiler_params=pltpu.CompilerParams(
            collective_id=1, has_side_effects=True, vmem_limit_bytes=VMEM_LIMIT
        ),
        name="gradients",
    )(dzg, late, xhg, mg, drg, dx)


def widen_kernel(
    n_cat,
    res,
    bres,
    lay_in,
    ig_in,
    hfin_in,
    cfin_in,
    lay_out,
    ig_out,
    wx_out,
    wh_out,
    b_out,
    wp_out,
    hfin_out,
    cfin_out,
    low,
    wide,
    lay_low,
    lay_buf,
    ig_low,
    ig_buf,
    p_low,
    p_wide,
    b_wide,
    h_buf,
    c_buf,
    in_sem,
    out_sem,
    p_sem,
    s_in,
    s_out,
    ig_sem,
    wp_sem,
):
    width, _, units = wx_out.shape
    steps, streams, _ = lay_low.shape
    slots = low.shape[0]
    row_blocks = low.shape[1]
    half = row_blocks // 2
    col_blocks = n_cat // row_blocks
    count = 2 * col_blocks
    n_proj = p_low.shape[1]
    proj_cols = width // BLK

    def fetch(k):
        slot = lax.rem(k, slots)
        return pltpu.make_async_copy(
            res.at[lax.div(k, col_blocks), pl.ds(lax.rem(k, col_blocks) * row_blocks, row_blocks)],
            low.at[slot],
            in_sem.at[slot],
        )

    def store(k):
        slot = lax.rem(k, slots)
        owner = lax.div(k, col_blocks)
        b = lax.rem(k, col_blocks)
        gate = lax.rem(b, 4)
        u = pl.multiple_of(owner * (units // 2) + lax.div(b, 4) * BLK, BLK)
        return [
            pltpu.make_async_copy(
                wide.at[slot, i],
                out.at[:, gate, pl.ds(u, BLK)],
                out_sem.at[slot, i],
            )
            for i, out in enumerate((wx_out, wh_out))
        ]

    for k in range(slots - 1):
        fetch(k).start()
    proj = [
        pltpu.make_async_copy(res.at[o, pl.ds(n_cat, n_proj)], p_low.at[o], p_sem.at[o])
        for o in range(2)
    ]
    taken = [
        pltpu.make_async_copy(src, dst, s_in.at[i])
        for i, (src, dst) in enumerate(
            ((lay_in, lay_low), (ig_in, ig_low), (hfin_in, h_buf), (cfin_in, c_buf))
        )
    ]
    given = [
        pltpu.make_async_copy(src, dst, s_out.at[i])
        for i, (src, dst) in enumerate(
            (
                (lay_buf, lay_out.reshape(streams * steps, width)),
                (h_buf, hfin_out),
                (c_buf, cfin_out),
                (b_wide, b_out),
            )
        )
    ]
    for one in taken + proj:
        one.start()

    def body(k, carry):
        slot = lax.rem(k, slots)

        @pl.when(k >= slots)
        def _():
            for one in store(k - slots):
                one.wait()

        fetch(k).wait()
        for r in range(row_blocks):
            wide[slot, r // half, (r % half) * CUT : (r % half + 1) * CUT, :] = low[slot, r].astype(F32)
        for one in store(k):
            one.start()

        @pl.when(k + slots - 1 < count)
        def _():
            fetch(k + slots - 1).start()

        return carry

    def layer_rows():
        taken[0].wait()
        t = lax.broadcasted_iota(jnp.int32, (steps, streams * steps), 0)
        r = lax.broadcasted_iota(jnp.int32, (steps, streams * steps), 1)
        flat = lay_low[...].reshape(streams * steps, width)
        bunch = BLK // steps
        for b in range(streams // bunch):
            want = jnp.concatenate(
                [jnp.where(r == t * streams + b * bunch + s, 1.0, 0.0) for s in range(bunch)], 0
            ).astype(BF)
            lay_buf[b * BLK : (b + 1) * BLK, :] = mm(want, flat).astype(BF)
        given[0].start()

    def states():
        for i in (2, 3):
            taken[i].wait()
            given[i - 1].start()

    def input_rows():
        taken[1].wait()
        for step in range(steps):
            ig_buf[step] = ig_low[step].astype(F32)
            ig_copy(step).start()

    def ig_copy(step):
        return pltpu.make_async_copy(ig_buf.at[step], ig_out.at[:, step, :], ig_sem.at[step])

    def bias_rows():
        for owner in range(2):
            for b in range(col_blocks):
                u = owner * (units // 2) + (b // 4) * BLK
                b_wide[b % 4 : b % 4 + 1, u : u + BLK] = bres[owner, b : b + 1, :].astype(F32)
        given[3].start()

    proj_rows = n_proj // proj_cols * CUT

    def proj_copy(owner):
        return pltpu.make_async_copy(
            p_wide.at[owner], wp_out.at[pl.ds(owner * proj_rows, proj_rows)], wp_sem.at[owner]
        )

    def proj_part(owner):
        proj[owner].wait()
        for n in range(n_proj):
            row = (n // proj_cols) * CUT
            col = (n % proj_cols) * BLK
            p_wide[owner, row : row + CUT, col : col + BLK] = p_low[owner, n].astype(F32)
        proj_copy(owner).start()

    extras = [
        layer_rows,
        states,
        input_rows,
        bias_rows,
        functools.partial(proj_part, 0),
        functools.partial(proj_part, 1),
    ]
    at = slots
    lax.fori_loop(0, at, body, 0)
    for extra in extras:
        extra()
        lax.fori_loop(at, at + 3, body, 0)
        at += 3
    lax.fori_loop(at, count, body, 0)
    for k in range(count - slots, count):
        for one in store(k):
            one.wait()
    for one in [*given, *(ig_copy(step) for step in range(steps)), proj_copy(0), proj_copy(1)]:
        one.wait()


def widen(res, bres, lay, ig, hfin, cfin):
    steps, streams, width = lay.shape
    units = cfin.shape[1]
    row_blocks = 2 * width // CUT
    n_cat = row_blocks * (2 * units // BLK)
    n_proj = res.shape[1] - n_cat
    slots = 6
    vmem = pl.BlockSpec(memory_space=pltpu.VMEM)
    hbm = pl.BlockSpec(memory_space=pl.ANY)
    shape = jax.ShapeDtypeStruct
    return pl.pallas_call(
        functools.partial(widen_kernel, n_cat),
        out_shape=(
            shape((streams, steps, width), BF),
            shape((streams, steps, width), F32),
            shape((width, 4, units), F32),
            shape((width, 4, units), F32),
            shape((4, units), F32),
            shape((units, width), F32),
            shape((streams, width), F32),
            shape((streams, units), F32),
        ),
        in_specs=[hbm, vmem, hbm, hbm, hbm, hbm],
        out_specs=(hbm,) * 8,
        scratch_shapes=[
            pltpu.VMEM((slots, row_blocks, CUT, BLK), BF),
            pltpu.VMEM((slots, 2, width, BLK), F32),
            pltpu.VMEM((steps, streams, width), BF),
            pltpu.VMEM((streams * steps, width), BF),
            pltpu.VMEM((steps, streams, width), BF),
            pltpu.VMEM((steps, streams, width), F32),
            pltpu.VMEM((2, n_proj, CUT, BLK), BF),
            pltpu.VMEM((2, units // 2, width), F32),
            pltpu.VMEM((4, units), F32),
            pltpu.VMEM((streams, width), F32),
            pltpu.VMEM((streams, units), F32),
            pltpu.SemaphoreType.DMA((slots,)),
            pltpu.SemaphoreType.DMA((slots, 2)),
            pltpu.SemaphoreType.DMA((2,)),
            pltpu.SemaphoreType.DMA((4,)),
            pltpu.SemaphoreType.DMA((4,)),
            pltpu.SemaphoreType.DMA((steps,)),
            pltpu.SemaphoreType.DMA((2,)),
        ],
        compiler_params=pltpu.CompilerParams(vmem_limit_bytes=VMEM_LIMIT),
        name="widen",
    )(res, bres, lay, ig, hfin, cfin)


def on_device(
    inputs,
    win_count,
    last_live,
    hidden_init,
    cell_init,
    w_input,
    w_hidden,
    gate_bias,
    w_proj,
    out_grad,
):
    streams, steps, width = inputs.shape
    units = w_proj.shape[1]
    lanes = lax.axis_size("batch") // 2
    lay, hfin, cfin, dx, dzg, late, xhg, mg, drg = recurrence(
        inputs,
        out_grad[0],
        win_count.reshape(1, streams),
        last_live.reshape(1, streams),
        hidden_init[0],
        cell_init[0],
        gate_bias[0],
        w_input[0],
        w_hidden[0],
        w_proj[0],
    )
    rows = 2 * steps * streams
    res, bres, ig = gradients(
        lanes,
        dzg.reshape(rows, 2 * units),
        late.reshape(steps * streams, LATE * BLK),
        xhg.reshape(rows, 2 * width),
        mg.reshape(rows, units // 2),
        drg.reshape(rows, width),
        dx,
    )
    out = widen(res, bres, lay, ig, hfin, cfin)
    layer_out, input_grad, wx_grad, wh_grad, b_grad, wp_grad, hidden_final, cell_final = out
    return (
        layer_out[None],
        input_grad,
        wx_grad[None],
        wh_grad[None],
        b_grad[None],
        wp_grad[None],
        hidden_final[None],
        cell_final[None],
    )


def solution(mesh):
    placed = (
        P("batch", None, None),
        P("batch"),
        P("batch"),
        P("dir", "batch", None),
        P("dir", "batch", "unit"),
        P("dir", None, None, "unit"),
        P("dir", None, None, "unit"),
        P("dir", None, "unit"),
        P("dir", "unit", None),
        P("dir", "batch", None, None),
    )
    return jax.shard_map(
        on_device,
        mesh=mesh,
        in_specs=placed,
        out_specs=(
            P("dir", "batch", None, None),
            P("batch", None, None),
            P("dir", None, None, "unit"),
            P("dir", None, None, "unit"),
            P("dir", None, "unit"),
            P("dir", "unit", None),
            P("dir", "batch", None),
            P("dir", "batch", "unit"),
        ),
        check_vma=False,
    )
```
